32 devices in a mesh: dp: 16 (over z, y, x), fsdp: 2 (over core).
Axes of the slice: x: 2, y: 2, z: 4, core: 2. Of those that a mesh axis runs over, the one named last changes fastest.
Arguments:
- cells: bfloat16 [4096, 13500], P(('dp', 'fsdp')), may hold values from -6 to 6
- coordinates: float32 [2, 4096], P(None, ('dp', 'fsdp')), may hold values from 0 to 100
- slide_ids: int32 [32, 128], P(('dp', 'fsdp')), may hold values from 0 to 7, never falling along the last dimension, each value on 1 to 32 neighbouring positions
- live_mask: int32 [32, 128], P(('dp', 'fsdp')), may hold values from 0 to 1, as said below
- components: int32 [4096], P(('dp', 'fsdp')), may hold values from 0 to 15
- noise: float32 [4096, 512], P(('dp', 'fsdp')), may hold values from -6 to 6
- ramp_weight: float32 [], replicated, may hold values from 0.3 to 1
- embed_weight: bfloat16 [1024, 13500], P(('dp', 'fsdp')), may hold values from -0.0546875 to 0.0546875
- query_key_value: bfloat16 [1024, 3072], P(('dp', 'fsdp')), may hold values from -0.1875 to 0.1875
- output_weight: bfloat16 [1024, 1024], P(('dp', 'fsdp')), may hold values from -0.5 to 0.5
- up_weight: bfloat16 [1024, 4096], P(('dp', 'fsdp')), may hold values from -0.1875 to 0.1875
- up_bias: bfloat16 [4096], P(('dp', 'fsdp')), may hold values from -3 to 3
- down_weight: bfloat16 [4096, 1024], P(('dp', 'fsdp')), may hold values from -0.09375 to 0.09375
- down_bias: bfloat16 [1024], P(('dp', 'fsdp')), may hold values from -3 to 3
- first_gain: bfloat16 [1024], P(('dp', 'fsdp')), may hold values from 0.25 to 1.75
- first_shift: bfloat16 [1024], P(('dp', 'fsdp')), may hold values from -3 to 3
- second_gain: bfloat16 [1024], P(('dp', 'fsdp')), may hold values from 0.25 to 1.75
- second_shift: bfloat16 [1024], P(('dp', 'fsdp')), may hold values from -3 to 3
- encoder_weight: bfloat16 [1024, 1024], P(('dp', 'fsdp')), may hold values from -0.09375 to 0.09375
- encoder_bias: bfloat16 [1024], P(('dp', 'fsdp')), may hold values from -3 to 3
- prior_mean: bfloat16 [16, 512], P(None, ('dp', 'fsdp')), may hold values from -3 to 3
- prior_logvar: bfloat16 [16, 512], P(None, ('dp', 'fsdp')), may hold values from -1.5 to 1.5
- decoder_weight: bfloat16 [512, 13500], P(('dp', 'fsdp')), may hold values from -0.25 to 0.25
Outputs:
- loss: float32 [], replicated
- cells_grad: bfloat16 [4096, 13500], P(('dp', 'fsdp'))
- embed_weight_grad: float32 [1024, 13500], P(('dp', 'fsdp'))
- query_key_value_grad: float32 [1024, 3072], P(('dp', 'fsdp'))
- output_weight_grad: float32 [1024, 1024], P(('dp', 'fsdp'))
- up_weight_grad: float32 [1024, 4096], P(('dp', 'fsdp'))
- up_bias_grad: float32 [4096], P(('dp', 'fsdp'))
- down_weight_grad: float32 [4096, 1024], P(('dp', 'fsdp'))
- down_bias_grad: float32 [1024], P(('dp', 'fsdp'))
- first_gain_grad: float32 [1024], P(('dp', 'fsdp'))
- first_shift_grad: float32 [1024], P(('dp', 'fsdp'))
- second_gain_grad: float32 [1024], P(('dp', 'fsdp'))
- second_shift_grad: float32 [1024], P(('dp', 'fsdp'))
- encoder_weight_grad: float32 [1024, 1024], P(('dp', 'fsdp'))
- encoder_bias_grad: float32 [1024], P(('dp', 'fsdp'))
- prior_mean_grad: float32 [16, 512], P(None, ('dp', 'fsdp'))
- prior_logvar_grad: float32 [16, 512], P(None, ('dp', 'fsdp'))
- decoder_weight_grad: float32 [512, 13500], P(('dp', 'fsdp'))
The draws below stay inside these ranges and needn't reach their ends.
Inputs may be any that keep to these rules, and one draw needn't show every extreme that they name: `live_mask`: in each row the live cells come first; the last row is all live.
All inputs are finite; a program needn't handle non-finite values.
Results may differ from the reference program's by a relative error of at most 0.025.
Values may be sent and summed in bfloat16 or wider, within the bound.
A program may use at most 384 MiB of HBM per device.

```python
import math
import jax
import jax.numpy as jnp
import numpy as np
from jax import lax

D = 1024
HEADS = 16
HEAD_DIM = 64
FF = 4096
GENES = 13500
LATENT = 512
MIXTURE = 16
TOK_DEV = 128
SLIDES = 8
SLIDE_MOST = 32
BLOCKS = 32
CELLS = 4096


def draw_live_mask(key, part):
    order = jnp.arange(BLOCKS, dtype=jnp.int32)
    least = TOK_DEV // 3
    rising = least + (TOK_DEV - least) * order // max(BLOCKS - 1, 1)
    jitter = jax.random.randint(key, (BLOCKS,), 0, TOK_DEV // 8 + 1)
    filled = jnp.where(order == BLOCKS - 1, TOK_DEV, jnp.maximum(rising - jitter, 1))
    return (jnp.arange(TOK_DEV, dtype=jnp.int32)[None, :] < filled[:, None]).astype(jnp.int32)


def touch_ends(result, own_key, low, high):
    dims = result.shape
    spot = [jax.random.randint(jax.random.fold_in(own_key, axis), (), 0, dims[axis]) for axis in range(len(dims))]
    result = result.at[tuple(spot)].set(low)
    longest = dims.index(max(dims))
    spot[longest] = (spot[longest] + 1) % dims[longest]
    return result.at[tuple(spot)].set(high)


def strengthened(entries, own_key, source, target, shards_of, factor):
    def block_of(dim):
        return (jnp.arange(entries.shape[dim]) // (entries.shape[dim] // shards_of)).reshape((-1,) + (1,) * (entries.ndim - 1 - dim))

    first = jax.random.permutation(own_key, shards_of)[block_of(target)]
    second = (block_of(target) + shards_of // 2) % shards_of
    return jnp.where((block_of(source) == first) | (block_of(source) == second), factor * entries, entries)


def steps_of(key, extent, shards, smallest, high):
    def one(axis_at, parts):
        steps = jax.random.uniform(jax.random.fold_in(jax.random.fold_in(key, 6), axis_at), (parts,), jnp.float32, smallest / len(shards), high / len(shards))
        return jnp.repeat(jnp.exp(steps), extent[axis_at] // parts).reshape((-1,) + (1,) * (len(extent) - axis_at - 1))

    level = one(*shards[0])
    for cut in shards[1:]:
        level = level * one(*cut)
    return level


def length_profile(count, total, reach, slope):
    portions = [(1 << 20) // math.isqrt(rank ** slope) + 1 for rank in range(2, count + 1)]
    spare, counts = total - reach - (count - 1), [1] * (count - 1)
    while spare > 0:
        candidates = [i for i in range(count - 1) if counts[i] < reach]
        mass, left = sum([portions[i] for i in candidates]), spare
        for i in candidates:
            addition = min(reach - counts[i], max(1, left * portions[i] // mass), spare)
            counts[i] = counts[i] + addition
            spare = spare - addition
    return np.array([reach] + counts)


def uneven_parts(own_key, count, total, most, slope):
    if count == 2:
        one = jax.random.randint(own_key, (), max(1, total - most), min(most, total - 1) + 1)
        return jnp.stack([one, total - one])
    lengths = jnp.asarray(length_profile(count, total, most, slope), jnp.int32)
    couples = (count - 1) // 2
    source_of, receiver = lengths[1:1 + 2 * couples:2], lengths[2:2 + 2 * couples:2]
    slack = jnp.minimum(source_of - 1, most - receiver)
    passed = jax.random.randint(jax.random.fold_in(own_key, 1), (couples,), 0, 1 << 20) % (slack + 1)
    lengths = lengths.at[1:1 + 2 * couples:2].set(source_of - passed).at[2:2 + 2 * couples:2].set(receiver + passed)
    return lengths[jax.random.permutation(jax.random.fold_in(own_key, 2), count)]


def bell_draw(rng, shape, scale, most, pieces=(), held_as=jnp.bfloat16):
    factor_of = steps_of(rng, shape, pieces, -0.22, 0.18) if pieces else 1.0
    values = jax.random.normal(rng, shape, jnp.float32) * scale * factor_of
    return jnp.minimum(jnp.maximum(values, -most), most).astype(held_as)


def heavy_noise(stream_key, shape, width, most, cuts, heavy, held_as=jnp.bfloat16):
    values = width * jax.random.normal(stream_key, shape, jnp.float32)
    if cuts:
        values = values * steps_of(stream_key, shape, cuts, -0.22, 0.18)
    return jnp.clip(strengthened(values, jax.random.fold_in(stream_key, 3), *heavy), -most, most).astype(held_as)


def setup_inputs(seed: int = 0) -> dict:
    streams_of = jax.random.split(jax.random.key(seed), 24)
    return {
        "cells": bell_draw(streams_of[0], (CELLS, GENES), 1.0, 6.0, ((0, 32),)),
        "coordinates": jnp.clip(100.0 * jax.random.uniform(streams_of[1], (2, CELLS), jnp.float32) ** steps_of(streams_of[1], (2, CELLS), ((1, 32),), -0.2, 0.2), 0.0, 100.0),
        "slide_ids": jax.vmap(lambda own: jnp.searchsorted(jnp.cumsum(uneven_parts(own, SLIDES, TOK_DEV, SLIDE_MOST, 1)), jnp.arange(TOK_DEV), side="right"))(jax.random.split(streams_of[2], BLOCKS)).reshape((BLOCKS, TOK_DEV)).astype(jnp.int32),
        "live_mask": draw_live_mask(jax.random.fold_in(streams_of[23], 71), 0),
        "components": touch_ends(jax.random.randint(streams_of[4], (CELLS,), 0, MIXTURE), jax.random.fold_in(streams_of[4], 1), 0, MIXTURE - 1).astype(jnp.int32),
        "noise": heavy_noise(streams_of[5], (CELLS, LATENT), 1.0, 6.0, ((0, 32),), (0, 1, 32, 2.75), jnp.float32),
        "ramp_weight": jnp.clip(jax.random.uniform(streams_of[6], (), jnp.float32, 0.3, 1.0), 0.3, 1.0),
        "embed_weight": bell_draw(streams_of[7], (D, GENES), GENES ** -0.5, 0.0546875, ((0, 32),)),
        "query_key_value": bell_draw(streams_of[8], (D, 3 * D), D ** -0.5, 0.1875, ((0, 32),)),
        "output_weight": bell_draw(streams_of[9], (D, D), (D // 8) ** -0.5, 0.5, ((0, 32),)),
        "up_weight": bell_draw(streams_of[10], (D, FF), D ** -0.5, 0.1875, ((0, 32),)),
        "up_bias": bell_draw(streams_of[11], (FF,), 0.5, 3.0, ((0, 32),)),
        "down_weight": bell_draw(streams_of[12], (FF, D), FF ** -0.5, 0.09375, ((0, 32),)),
        "down_bias": bell_draw(streams_of[13], (D,), 0.3, 3.0, ((0, 32),)),
        "first_gain": jnp.clip(1.0 + 0.15 * jax.random.normal(streams_of[14], (D,), jnp.float32), 0.25, 1.75).astype(jnp.bfloat16),
        "first_shift": bell_draw(streams_of[15], (D,), 0.3, 3.0, ((0, 32),)),
        "second_gain": jnp.clip(1.0 + 0.15 * jax.random.normal(streams_of[16], (D,), jnp.float32), 0.25, 1.75).astype(jnp.bfloat16),
        "second_shift": bell_draw(streams_of[17], (D,), 0.3, 3.0, ((0, 32),)),
        "encoder_weight": bell_draw(streams_of[18], (D, 2 * LATENT), (4 * D) ** -0.5, 0.09375, ((0, 32),)),
        "encoder_bias": bell_draw(streams_of[19], (2 * LATENT,), 0.3, 3.0, ((0, 32),)),
        "prior_mean": bell_draw(streams_of[20], (MIXTURE, LATENT), 0.5, 3.0, ((1, 32),)),
        "prior_logvar": jnp.clip(jax.random.uniform(streams_of[21], (MIXTURE, LATENT), jnp.float32, -1.5, 1.5) * steps_of(streams_of[21], (MIXTURE, LATENT), ((1, 32),), -0.4, 0.0), -1.5, 1.5).astype(jnp.bfloat16),
        "decoder_weight": bell_draw(streams_of[22], (LATENT, GENES), LATENT ** -0.5, 0.25, ((0, 32),)),
    }


NEG_SCORE = -1000000000.0
NORM_EPS = 1e-05
FREE_FLOOR = 1.0
FREE_TEMP = 0.25

@jax.custom_vjp
def low(v):
    return lax.optimization_barrier(v.astype(jnp.bfloat16)).astype(jnp.float32)

@jax.custom_vjp
def low_back(v):
    return v

def low_keep(v):
    return (low(v), None)

def low_pass(kept, grad):
    return (grad,)

def back_keep(v):
    return (v, None)

def back_low(kept, grad):
    return (low(grad),)
low.defvjp(low_keep, low_pass)
low_back.defvjp(back_keep, back_low)

def product(left, right):
    return jnp.dot(left, right, precision=lax.Precision.HIGHEST, preferred_element_type=jnp.float32)

def layer_norm(hidden, gain, shift):
    center = hidden - lax.optimization_barrier(jnp.mean(hidden, axis=-1, keepdims=True))
    spread = lax.optimization_barrier(jnp.mean(center * center, axis=-1, keepdims=True))
    return center * lax.rsqrt(spread + NORM_EPS) * gain + shift

def positions(coordinates):
    quarter = D // 4
    frequency = jnp.exp(jnp.arange(quarter, dtype=jnp.float32) * (-math.log(10000.0) / quarter))
    angle_x = coordinates[0][:, None] * frequency[None, :]
    angle_y = coordinates[1][:, None] * frequency[None, :]
    return jnp.concatenate([jnp.sin(angle_x), jnp.cos(angle_x), jnp.sin(angle_y), jnp.cos(angle_y)], axis=1)

def sequence_terms(weights, items):
    embed_weight, query_key_value, output_weight, up_weight, up_bias, down_weight, down_bias, first_gain, first_shift, second_gain, second_shift, encoder_weight, encoder_bias, prior_mean, prior_logvar, decoder_weight = weights
    cells, coordinates, slides, live, onehot, noise = items
    length = cells.shape[0]
    highest = lax.Precision.HIGHEST
    embedded = low_back(product(cells, embed_weight.T))
    start_state = embedded + positions(coordinates)
    normed = low(layer_norm(start_state, first_gain, first_shift))
    joint = low_back(low(product(normed, query_key_value)))
    queries = joint[:, :D].reshape(length, HEADS, HEAD_DIM)
    keys = joint[:, D:2 * D].reshape(length, HEADS, HEAD_DIM)
    values = joint[:, 2 * D:].reshape(length, HEADS, HEAD_DIM)
    scores = low_back(jnp.einsum('qhd,khd->hqk', queries, keys, precision=highest) * HEAD_DIM ** (-0.5))
    places = jnp.arange(length)
    allowed = (slides[:, None] == slides[None, :]) & ((live[None, :] > 0.5) | (places[:, None] == places[None, :]))
    masked = jnp.where(allowed[None], scores, NEG_SCORE)
    probs = low(jax.nn.softmax(masked, axis=-1))
    context = low_back(low(jnp.einsum('hqk,khd->qhd', probs, values, precision=highest))).reshape(length, D)
    middle_state = start_state + low_back(product(context, output_weight))
    second = low(layer_norm(middle_state, second_gain, second_shift))
    pre = low_back(product(second, up_weight) + up_bias)
    active = low(jax.nn.gelu(pre, approximate=True))
    end_state = middle_state + low_back(product(active, down_weight) + down_bias)
    encoded = low_back(product(low(end_state), encoder_weight) + encoder_bias)
    latent_mean = encoded[:, :LATENT]
    latent_logvar = encoded[:, LATENT:]
    latent = low(latent_mean + jnp.exp(0.5 * latent_logvar) * noise)
    recon = low_back(product(latent, decoder_weight))
    miss = recon - cells
    recon_total = jnp.sum(live * (0.5 * lax.optimization_barrier(jnp.sum(miss * miss, axis=1))))
    center = product(onehot, prior_mean)
    scale = product(onehot, prior_logvar)
    gap = latent_mean - center
    diverge = 0.5 * (scale - latent_logvar + (jnp.exp(latent_logvar) + gap * gap) * jnp.exp(-scale) - 1.0)
    return (recon_total, lax.optimization_barrier(jnp.sum(live[:, None] * diverge, axis=0)))

def reference(cells, coordinates, slide_ids, live_mask, components, noise, ramp_weight, embed_weight, query_key_value, output_weight, up_weight, up_bias, down_weight, down_bias, first_gain, first_shift, second_gain, second_shift, encoder_weight, encoder_bias, prior_mean, prior_logvar, decoder_weight):
    weights = (embed_weight, query_key_value, output_weight, up_weight, up_bias, down_weight, down_bias, first_gain, first_shift, second_gain, second_shift, encoder_weight, encoder_bias, prior_mean, prior_logvar, decoder_weight)
    weights = tuple((item.astype(jnp.float32) for item in weights))
    cells_wide = cells.astype(jnp.float32)
    live = live_mask.astype(jnp.float32)
    onehot = (components.reshape(BLOCKS, TOK_DEV)[:, :, None] == jnp.arange(MIXTURE, dtype=jnp.int32)[None, None, :]).astype(jnp.float32)
    coords = coordinates.reshape(2, BLOCKS, TOK_DEV).transpose(1, 0, 2)
    noise_blocks = noise.reshape(BLOCKS, TOK_DEV, LATENT)
    count = jnp.sum(live)
    saved = jax.checkpoint(sequence_terms)

    def forward(cell_values, *params):

        def one_block(items):
            return saved(params, items)
        totals, diverge_sums = lax.map(one_block, (cell_values.reshape(BLOCKS, TOK_DEV, GENES), coords, slide_ids, live, onehot, noise_blocks))
        kl_mean = lax.optimization_barrier(jnp.sum(diverge_sums, axis=0)) / count
        free = FREE_FLOOR + FREE_TEMP * jax.nn.softplus((kl_mean - FREE_FLOOR) / FREE_TEMP)
        inner = jnp.sum(totals) / count + ramp_weight * jnp.sum(free)
        return (CELLS * inner, inner / GENES)
    scaled, backward, loss = jax.vjp(forward, cells_wide, *weights, has_aux=True)
    grads = backward(jnp.ones_like(scaled))
    return (loss, grads[0].astype(jnp.bfloat16), grads[1], grads[2], grads[3], grads[4], grads[5], grads[6], grads[7], grads[8], grads[9], grads[10], grads[11], grads[12], grads[13], grads[14], grads[15], grads[16])
```

```python
import math

import jax
import jax.numpy as jnp
from jax import lax
from jax.sharding import PartitionSpec as P

D = 1024
HEAD_DIM = 64
GENES = 13500
LATENT = 512


NEG_SCORE = -1000000000.0
NORM_EPS = 1e-05
FREE_FLOOR = 1.0
FREE_TEMP = 0.25


def layer_norm(hidden, gain, shift):
    center = hidden - jnp.mean(hidden, axis=-1, keepdims=True)
    spread = jnp.mean(center * center, axis=-1, keepdims=True)
    return center * lax.rsqrt(spread + NORM_EPS) * gain + shift


def positions(coordinates):
    quarter = D // 4
    frequency = jnp.exp(jnp.arange(quarter, dtype=jnp.float32) * (-math.log(10000.0) / quarter))
    angle_x = coordinates[0][:, None] * frequency[None, :]
    angle_y = coordinates[1][:, None] * frequency[None, :]
    return jnp.concatenate(
        [jnp.sin(angle_x), jnp.cos(angle_x), jnp.sin(angle_y), jnp.cos(angle_y)], axis=1
    )


def matmul(left, right):
    return jnp.dot(left, right, preferred_element_type=jnp.float32)


def across(left, right):
    return lax.dot_general(
        left, right, (((1,), (1,)), ((), ())), preferred_element_type=jnp.float32
    )


def contract_rows(left, right):
    return lax.dot_general(
        left, right, (((0,), (0,)), ((), ())), preferred_element_type=jnp.float32
    )


def split_heads(joint):
    row_count = joint.shape[0]
    queries = joint[:, :D].reshape(row_count, -1, HEAD_DIM)
    keys = joint[:, D : 2 * D].reshape(row_count, -1, HEAD_DIM)
    values = joint[:, 2 * D :].reshape(row_count, -1, HEAD_DIM)
    return (queries, keys, values)


def masked_scores(queries, keys, allowed):
    scores = jnp.einsum(
        "qhd,khd->hqk", queries, keys, preferred_element_type=jnp.float32
    ) * HEAD_DIM ** (-0.5)
    return jnp.where(allowed[None], scores, NEG_SCORE)


def attention_forward(joint, allowed):
    queries, keys, values = split_heads(joint)
    masked = masked_scores(queries, keys, allowed)
    peak = jnp.max(masked, axis=-1, keepdims=True)
    raised = jnp.exp(masked - peak)
    denom = jnp.sum(raised, axis=-1, keepdims=True)
    probs = raised / denom
    logsum = peak + jnp.log(denom)
    context = jnp.einsum(
        "hqk,khd->qhd", probs.astype(jnp.bfloat16), values, preferred_element_type=jnp.float32
    )
    return (context.reshape(joint.shape[0], D).astype(jnp.bfloat16), logsum)


def attention_backward(joint, allowed, logsum, context_grad):
    row_count = joint.shape[0]
    queries, keys, values = split_heads(joint)
    probs = jnp.exp(masked_scores(queries, keys, allowed) - logsum)
    probs_low = probs.astype(jnp.bfloat16)
    incoming = context_grad.reshape(row_count, -1, HEAD_DIM)
    value_grad = jnp.einsum("hqk,qhd->khd", probs_low, incoming, preferred_element_type=jnp.float32)
    prob_grad = jnp.einsum("qhd,khd->hqk", incoming, values, preferred_element_type=jnp.float32)
    score_grad = (probs * (prob_grad - jnp.sum(probs * prob_grad, axis=-1, keepdims=True))).astype(
        jnp.bfloat16
    )
    query_grad = jnp.einsum(
        "hqk,khd->qhd", score_grad, keys, preferred_element_type=jnp.float32
    ) * HEAD_DIM ** (-0.5)
    key_grad = jnp.einsum(
        "hqk,qhd->khd", score_grad, queries, preferred_element_type=jnp.float32
    ) * HEAD_DIM ** (-0.5)
    return jnp.concatenate(
        [
            query_grad.reshape(row_count, D),
            key_grad.reshape(row_count, D),
            value_grad.reshape(row_count, D),
        ],
        axis=1,
    ).astype(jnp.bfloat16)

AXES = ("dp", "fsdp")
GROUP = 4
CHUNK = 3456
NARROW = 8


def low(values):
    return values.astype(jnp.bfloat16)


def wide(values):
    return values.astype(jnp.float32)


def device_total():
    return lax.axis_size("dp") * lax.axis_size("fsdp")


def device_index():
    return lax.axis_index("dp") * lax.axis_size("fsdp") + lax.axis_index("fsdp")


def swap(values, mask):
    return lax.ppermute(values, AXES, [(i, i ^ mask) for i in range(device_total())])


def ring_order():
    total = device_total() // GROUP
    return list(range(0, total, 2)) + list(range(total - 1, 0, -2))


def shift(values, step):
    order = ring_order()
    total = len(order)
    pairs = []
    for place in range(total):
        for quarter in range(GROUP):
            pairs.append(
                (order[place] * GROUP + quarter, order[(place + step) % total] * GROUP + quarter)
            )
    return lax.ppermute(values, AXES, pairs)


def ring_place():
    order = ring_order()
    inverse = [order.index(t) for t in range(len(order))]
    return jnp.array(inverse, jnp.int32)[device_index() // GROUP]


def ring_owner(step):
    order = ring_order()
    return jnp.array(order, jnp.int32)[(ring_place() - step) % len(order)]


def same_quarter():
    return [[d for d in range(lax.axis_size("dp")) if d % 2 == odd] for odd in range(2)]


def pick(blocks, index):
    return lax.dynamic_index_in_dim(blocks, index, 0, keepdims=False)


def ring_gather(block):
    total = device_total() // GROUP
    if total > NARROW:
        full = lax.all_gather(block, "dp", axis_index_groups=same_quarter(), axis=0, tiled=False)
        return jnp.stack([pick(full, ring_owner(s)) for s in range(total)])
    half = block.shape[0] // 2
    tops, bottoms = [block[:half]], [block[half:]]
    for _ in range(total - 1):
        tops.append(shift(tops[-1], 1))
        bottoms.append(shift(bottoms[-1], -1))
    return jnp.stack(
        [jnp.concatenate([tops[s], bottoms[(total - s) % total]]) for s in range(total)]
    )


def ring_scatter(blocks):
    total = device_total() // GROUP
    if total > NARROW:
        full = jnp.zeros_like(blocks)
        for s in range(total):
            full = lax.dynamic_update_index_in_dim(full, blocks[s], ring_owner(s), 0)
        return lax.psum_scatter(
            full, "dp", axis_index_groups=same_quarter(), scatter_dimension=0, tiled=False
        )
    half = blocks.shape[1] // 2
    top, bottom = blocks[1, :half], blocks[total - 1, half:]
    for s in range(2, total + 1):
        top = shift(top, 1)
        bottom = shift(bottom, -1)
        top = wide(top) + wide(blocks[s % total, :half])
        bottom = wide(bottom) + wide(blocks[(total - s) % total, half:])
        if s < total:
            top, bottom = low(top), low(bottom)
    return jnp.concatenate([top, bottom])


def group_exchange(blocks, quarter):
    return [pick(blocks, quarter)] + [swap(pick(blocks, quarter ^ m), m) for m in range(1, GROUP)]


def group_gather(values):
    pair = jnp.stack([values, swap(values, 2)])
    other = swap(pair, 1)
    return jnp.stack([pair[0], other[0], pair[1], other[1]])


def group_scatter(parts):
    mine = jnp.stack([parts[0], parts[2]])
    theirs = low(jnp.stack([parts[1], parts[3]]))
    summed = wide(mine) + wide(swap(theirs, 1))
    return summed[0] + wide(swap(low(summed[1]), 2))


def by_quarter(pieces, quarter):
    stacked = jnp.stack(pieces)
    return [pick(stacked, quarter ^ j) for j in range(GROUP)]


def gene_chunks(values):
    padded = jnp.pad(values, ((0, 0), (0, GROUP * CHUNK - GENES)))
    return jnp.stack([padded[:, j * CHUNK : (j + 1) * CHUNK] for j in range(GROUP)])


def sum_all(values):
    mask = 1
    while mask < device_total():
        values = values + swap(values, mask)
        mask *= 2
    return values


def scatter_all(values):
    me = device_index()
    mask = 1
    values = values[None]
    while mask < device_total():
        bit = (me // mask) % 2
        rows = values.shape[1]
        split = values.reshape(values.shape[0], rows // 2, 2, values.shape[2])
        keep = lax.dynamic_index_in_dim(split, bit, 2, keepdims=False)
        give = lax.dynamic_index_in_dim(split, 1 - bit, 2, keepdims=False)
        values = keep + swap(give, mask)
        mask *= 2
    return values[0, 0]


def place_rows(pieces, columns, quarter):
    total, rows, _ = pieces[0].shape
    low_col, high_col = columns
    full = jnp.zeros((total, GROUP, rows, high_col - low_col), jnp.bfloat16)
    for m in range(GROUP):
        for s in range(total):
            full = lax.dynamic_update_slice(
                full,
                pieces[m][s, :, low_col:high_col][None, None],
                (ring_owner(s), quarter ^ m, 0, 0),
            )
    return full.reshape(total * GROUP * rows, high_col - low_col)


def block_order(count):
    total = device_total() // GROUP
    owners = jnp.stack([ring_owner(s) for s in range(total)])
    source = jnp.repeat(owners, count) * count + jnp.tile(jnp.arange(count), total)
    return low(jnp.arange(total * count)[:, None] == source[None, :])


def halves_scatter(values, rows, ring_first):
    total = device_total() // GROUP
    me = device_index()
    core, side = me % 2, (me // 2) % 2
    split = values.reshape(total, 2, 2, rows, values.shape[1])
    keep = lax.dynamic_index_in_dim(split, core, 2, keepdims=False)
    give = lax.dynamic_index_in_dim(split, 1 - core, 2, keepdims=False)
    chip = low(wide(keep) + wide(swap(low(give), 1)))
    if ring_first:
        ringed = jnp.stack([pick(chip, ring_owner(s)) for s in range(total)])
        pair = low(ring_scatter(ringed.reshape(total, 2 * rows, -1)).reshape(2, rows, -1))
        return wide(pick(pair, side)) + wide(swap(pick(pair, 1 - side), 2))
    keep = lax.dynamic_index_in_dim(chip, side, 1, keepdims=False)
    give = lax.dynamic_index_in_dim(chip, 1 - side, 1, keepdims=False)
    both = low(wide(keep) + wide(swap(give, 2)))
    return wide(ring_scatter(jnp.stack([pick(both, ring_owner(s)) for s in range(total)])))


def shards(
    cells,
    coordinates,
    slide_ids,
    live_mask,
    components,
    noise,
    ramp_weight,
    embed_weight,
    query_key_value,
    output_weight,
    up_weight,
    up_bias,
    down_weight,
    down_bias,
    first_gain,
    first_shift,
    second_gain,
    second_shift,
    encoder_weight,
    encoder_bias,
    prior_mean,
    prior_logvar,
    decoder_weight,
):
    row_count = cells.shape[0]
    devices = device_total()
    total = devices // GROUP
    me = device_index()
    quarter = me % GROUP
    rows = embed_weight.shape[0]
    thin = decoder_weight.shape[0]
    cell_total = row_count * devices
    live = live_mask[0].astype(jnp.float32)
    slides = slide_ids[0]
    places = jnp.arange(row_count)
    allowed = (slides[:, None] == slides[None, :]) & (
        (live[None, :] > 0.5) | (places[:, None] == places[None, :])
    )
    onehot = (
        components[:, None] == jnp.arange(prior_mean.shape[0], dtype=jnp.int32)[None, :]
    ).astype(jnp.float32)

    cells_group = jnp.stack(group_exchange(gene_chunks(cells), quarter)).reshape(
        GROUP * row_count, CHUNK
    )
    live_group = group_gather(live_mask).reshape(-1).astype(jnp.float32)
    both = gene_chunks(jnp.concatenate([embed_weight, decoder_weight]))
    both = jnp.stack(by_quarter(group_exchange(both, quarter), quarter))
    embed_cols = ring_gather(both[:, :rows].reshape(GROUP * rows, CHUNK)).reshape(-1, CHUNK)
    small = jnp.concatenate(
        [
            up_bias.reshape(rows, 4),
            down_bias.reshape(rows, 1),
            first_gain.reshape(rows, 1),
            first_shift.reshape(rows, 1),
            second_gain.reshape(rows, 1),
            second_shift.reshape(rows, 1),
            encoder_bias.reshape(rows, 1),
            prior_mean.reshape(rows, 8),
            prior_logvar.reshape(rows, 8),
            jnp.full((rows, 1), jnp.sum(live), jnp.bfloat16),
        ],
        axis=1,
    )
    small_columns = small.shape[1]
    small = jnp.pad(small, ((0, 0), (0, 128 - small_columns)))
    first_unit = jnp.concatenate([query_key_value, output_weight, encoder_weight, small], axis=1)
    second_unit = jnp.concatenate(
        [
            up_weight,
            down_weight.reshape(4, rows, D).transpose(1, 0, 2).reshape(rows, 4 * D),
        ],
        axis=1,
    )
    width = first_unit.shape[1]
    pair = jnp.concatenate([first_unit, swap(first_unit, 2)])
    ringed = ring_gather(pair).reshape(total, 2, rows, width)
    other = swap(ringed, 1)
    first_pieces = [ringed[:, 0], other[:, 0], ringed[:, 1], other[:, 1]]
    ringed = ring_gather(second_unit)
    pair = jnp.stack([ringed, swap(ringed, 2)])
    other = swap(pair, 1)
    second_pieces = [pair[0], other[0], pair[1], other[1]]
    decoder_cols = ring_gather(both[:, rows:].reshape(GROUP * thin, CHUNK)).reshape(-1, CHUNK)

    joint_full = place_rows(first_pieces, (0, 3 * D), quarter)
    output_full = place_rows(first_pieces, (3 * D, 4 * D), quarter)
    encoder_full = place_rows(first_pieces, (4 * D, 5 * D), quarter)
    small_full = place_rows(first_pieces, (5 * D, 5 * D + 128), quarter)
    up_full = place_rows(second_pieces, (0, 4 * D), quarter)
    down_full = place_rows(second_pieces, (4 * D, 8 * D), quarter)
    down_full = (
        down_full.reshape(devices, rows, 4, D).transpose(0, 2, 1, 3).reshape(4 * devices * rows, D)
    )
    small_full = wide(small_full)
    up_bias_full = small_full[:, 0:4].reshape(-1)
    down_bias_full = small_full[:, 4]
    gain_first = small_full[:, 5]
    shift_first = small_full[:, 6]
    gain_second = small_full[:, 7]
    shift_second = small_full[:, 8]
    encoder_bias_full = small_full[:, 9]
    kinds = prior_mean.shape[0]

    def prior_full(columns):
        return columns.reshape(devices, kinds, -1).transpose(1, 0, 2).reshape(kinds, LATENT)

    prior_mean_full = prior_full(small_full[:, 10:18])
    prior_logvar_full = prior_full(small_full[:, 18:26])
    count = jnp.sum(small_full.reshape(devices, rows, 128)[:, 0, 26])

    feature_order = block_order(GROUP * rows)
    latent_order = block_order(GROUP * thin)
    embedded = low(across(cells_group, embed_cols))
    embedded = low(across(embedded, feature_order)).reshape(GROUP, row_count, D)
    embedded = group_scatter(embedded)
    start_state = embedded + positions(coordinates)
    normed_first = layer_norm(start_state, gain_first, shift_first).astype(jnp.bfloat16)
    joint = matmul(normed_first, joint_full).astype(jnp.bfloat16)
    context, logsum = attention_forward(joint, allowed)
    middle_state = start_state + matmul(context, output_full)
    normed_second = layer_norm(middle_state, gain_second, shift_second).astype(jnp.bfloat16)
    pre = matmul(normed_second, up_full) + up_bias_full
    active = jax.nn.gelu(pre, approximate=True).astype(jnp.bfloat16)
    end_state = middle_state + (matmul(active, down_full) + down_bias_full)
    end_low = end_state.astype(jnp.bfloat16)
    encoded = matmul(end_low, encoder_full) + encoder_bias_full
    latent_mean = encoded[:, :LATENT]
    latent_logvar = encoded[:, LATENT:]
    latent = (latent_mean + jnp.exp(0.5 * latent_logvar) * noise).astype(jnp.bfloat16)
    latent_group = group_gather(latent).reshape(GROUP * row_count, LATENT)
    latent_group = low(matmul(latent_group, latent_order))

    center = jnp.dot(onehot, prior_mean_full, precision=lax.Precision.HIGHEST)
    scale = jnp.dot(onehot, prior_logvar_full, precision=lax.Precision.HIGHEST)
    gap = latent_mean - center
    inverse = jnp.exp(-scale)
    grown = jnp.exp(latent_logvar)
    diverge = 0.5 * (scale - latent_logvar + (grown + gap * gap) * inverse - 1.0)
    kl_mean = sum_all(jnp.sum(live[:, None] * diverge, axis=0, keepdims=True))[0] / count

    recon = matmul(latent_group, decoder_cols)
    miss = recon - wide(cells_group)
    recon_local = jnp.sum(live_group * (0.5 * jnp.sum(miss * miss, axis=1)))
    shifted = (kl_mean - FREE_FLOOR) / FREE_TEMP
    free = FREE_FLOOR + FREE_TEMP * jax.nn.softplus(shifted)
    ratio = cell_total / count
    recon_grad = low(ratio * live_group[:, None] * miss)
    decoder_term = low(contract_rows(latent_group, recon_grad))
    decoder_block = low(ring_scatter(decoder_term.reshape(total, GROUP * thin, CHUNK)))
    latent_grad = low(across(recon_grad, decoder_cols))
    latent_grad = low(across(latent_grad, latent_order)).reshape(GROUP, row_count, LATENT)
    latent_grad = wide(low(group_scatter(latent_grad)))

    kl_scale = ratio * ramp_weight * jax.nn.sigmoid(shifted)[None, :] * live[:, None]
    pulled = kl_scale * gap * inverse
    mean_grad = latent_grad + pulled
    logvar_grad = latent_grad * 0.5 * jnp.exp(0.5 * latent_logvar) * noise + kl_scale * 0.5 * (
        grown * inverse - 1.0
    )
    encoded_grad = jnp.concatenate([mean_grad, logvar_grad], axis=1).astype(jnp.bfloat16)
    prior_mean_grad = jnp.dot(onehot.T, -pulled, precision=lax.Precision.HIGHEST)
    prior_logvar_grad = jnp.dot(
        onehot.T,
        kl_scale * 0.5 * (1.0 - (grown + gap * gap) * inverse),
        precision=lax.Precision.HIGHEST,
    )
    end_grad = across(encoded_grad, encoder_full)
    branch_grad = end_grad.astype(jnp.bfloat16)
    encoder_term = low(contract_rows(end_low, encoded_grad))
    encoder_bias_grad = jnp.sum(encoded_grad.astype(jnp.float32), axis=0)
    down_term = low(contract_rows(active, branch_grad))
    down_bias_grad = jnp.sum(branch_grad.astype(jnp.float32), axis=0)
    down_pack = jnp.concatenate(
        [
            encoder_term.reshape(devices, rows, D),
            down_term.reshape(devices, 4 * rows, D),
        ],
        axis=1,
    ).reshape(-1, D)
    down_pack = halves_scatter(down_pack, 5 * rows, False)
    encoder_weight_grad = down_pack[:rows]
    down_weight_grad = down_pack[rows:]
    active_grad = across(branch_grad, down_full)
    gelu_value, gelu_back = jax.vjp(lambda value: jax.nn.gelu(value, approximate=True), pre)
    pre_grad = gelu_back(active_grad)[0].astype(jnp.bfloat16)
    up_weight_grad = halves_scatter(low(contract_rows(normed_second, pre_grad)), rows, False)
    up_bias_grad = jnp.sum(pre_grad.astype(jnp.float32), axis=0)
    second_out_grad = across(pre_grad, up_full)
    norm_value, second_back = jax.vjp(layer_norm, middle_state, gain_second, shift_second)
    state_part, second_gain_grad, second_shift_grad = second_back(second_out_grad)
    middle_grad = end_grad + state_part
    attend_grad = middle_grad.astype(jnp.bfloat16)
    output_term = low(contract_rows(context, attend_grad))
    context_grad = across(attend_grad, output_full).astype(jnp.bfloat16)
    joint_grad = attention_backward(joint, allowed, logsum, context_grad)
    joint_term = low(contract_rows(normed_first, joint_grad))
    joint_pack = halves_scatter(jnp.concatenate([joint_term, output_term], axis=1), rows, True)
    joint_weight_grad = joint_pack[:, : 3 * D]
    output_weight_grad = joint_pack[:, 3 * D :]
    first_out_grad = across(joint_grad, joint_full)
    first_value, first_back = jax.vjp(layer_norm, start_state, gain_first, shift_first)
    start_part, first_gain_grad, first_shift_grad = first_back(first_out_grad)
    start_grad = middle_grad + start_part
    start_low = start_grad.astype(jnp.bfloat16)
    start_group = group_gather(start_low).reshape(GROUP * row_count, D)
    start_group = low(matmul(start_group, feature_order))
    embed_term = low(contract_rows(start_group, cells_group))
    embed_block = low(ring_scatter(embed_term.reshape(total, GROUP * rows, CHUNK)))
    cells_half = low(matmul(start_group, embed_cols) - wide(recon_grad))

    def to_owners(blocks):
        pieces = [blocks[0]] + [swap(blocks[m], m) for m in range(1, GROUP)]
        return jnp.concatenate(by_quarter(pieces, quarter), axis=1)[:, :GENES]

    cells_grad = to_owners(cells_half.reshape(GROUP, row_count, CHUNK))
    embed_block = embed_block.reshape(GROUP, rows, CHUNK)
    decoder_block = decoder_block.reshape(GROUP, thin, CHUNK)
    blocks = jnp.concatenate([embed_block, decoder_block], axis=1)
    blocks = [pick(blocks, quarter ^ m) for m in range(GROUP)]
    weight_grads = wide(to_owners(jnp.stack(blocks)))
    embed_grad, decoder_grad = weight_grads[:rows], weight_grads[rows:]

    def prior_rows(values):
        return values.reshape(kinds, devices, -1).transpose(1, 0, 2).reshape(devices, -1)

    vectors = [
        up_bias_grad,
        down_bias_grad,
        first_gain_grad,
        first_shift_grad,
        second_gain_grad,
        second_shift_grad,
        encoder_bias_grad,
    ]
    packed = jnp.concatenate(
        [vector.reshape(devices, -1) for vector in vectors]
        + [prior_rows(prior_mean_grad), prior_rows(prior_logvar_grad)],
        axis=1,
    )
    packed = scatter_all(packed)
    ends = [0]
    for vector in vectors:
        ends.append(ends[-1] + vector.shape[0] // devices)
    vector_grads = [packed[ends[i] : ends[i + 1]] for i in range(len(vectors))]
    prior_size = kinds * LATENT // devices
    prior_mean_out = packed[ends[-1] : ends[-1] + prior_size].reshape(kinds, -1)
    prior_logvar_out = packed[ends[-1] + prior_size :].reshape(kinds, -1)
    recon_total = sum_all(jnp.full((1, 128), recon_local, jnp.float32))[0, 0]
    loss = (recon_total / count + ramp_weight * jnp.sum(free)) / GENES
    return (
        loss,
        cells_grad,
        embed_grad,
        joint_weight_grad,
        output_weight_grad,
        up_weight_grad,
        vector_grads[0],
        down_weight_grad,
        vector_grads[1],
        vector_grads[2],
        vector_grads[3],
        vector_grads[4],
        vector_grads[5],
        encoder_weight_grad,
        vector_grads[6],
        prior_mean_out,
        prior_logvar_out,
        decoder_grad,
    )


def solution(mesh):
    in_specs = (
        P(("dp", "fsdp"), None),
        P(None, ("dp", "fsdp")),
        P(("dp", "fsdp"), None),
        P(("dp", "fsdp"), None),
        P(("dp", "fsdp")),
        P(("dp", "fsdp"), None),
        P(),
        P(("dp", "fsdp"), None),
        P(("dp", "fsdp"), None),
        P(("dp", "fsdp"), None),
        P(("dp", "fsdp"), None),
        P(("dp", "fsdp")),
        P(("dp", "fsdp"), None),
        P(("dp", "fsdp")),
        P(("dp", "fsdp")),
        P(("dp", "fsdp")),
        P(("dp", "fsdp")),
        P(("dp", "fsdp")),
        P(("dp", "fsdp"), None),
        P(("dp", "fsdp")),
        P(None, ("dp", "fsdp")),
        P(None, ("dp", "fsdp")),
        P(("dp", "fsdp"), None),
    )
    out_specs = (
        P(),
        P(("dp", "fsdp"), None),
        P(("dp", "fsdp"), None),
        P(("dp", "fsdp"), None),
        P(("dp", "fsdp"), None),
        P(("dp", "fsdp"), None),
        P(("dp", "fsdp")),
        P(("dp", "fsdp"), None),
        P(("dp", "fsdp")),
        P(("dp", "fsdp")),
        P(("dp", "fsdp")),
        P(("dp", "fsdp")),
        P(("dp", "fsdp")),
        P(("dp", "fsdp"), None),
        P(("dp", "fsdp")),
        P(None, ("dp", "fsdp")),
        P(None, ("dp", "fsdp")),
        P(("dp", "fsdp"), None),
    )
    return jax.shard_map(shards, mesh=mesh, in_specs=in_specs, out_specs=out_specs, check_vma=False)
```

```python
import functools
import math

import jax
import jax.numpy as jnp
from jax import lax
from jax.experimental import pallas as pl
from jax.experimental.pallas import tpu as pltpu
from jax.sharding import PartitionSpec as P

D = 1024
HEAD_DIM = 64
GENES = 13500
LATENT = 512


NEG_SCORE = -1000000000.0
NORM_EPS = 1e-05
FREE_FLOOR = 1.0
FREE_TEMP = 0.25


def layer_norm(hidden, gain, shift):
    center = hidden - jnp.mean(hidden, axis=-1, keepdims=True)
    spread = jnp.mean(center * center, axis=-1, keepdims=True)
    return center * lax.rsqrt(spread + NORM_EPS) * gain + shift


def positions(coordinates):
    quarter = D // 4
    frequency = jnp.exp(jnp.arange(quarter, dtype=jnp.float32) * (-math.log(10000.0) / quarter))
    angle_x = coordinates[0][:, None] * frequency[None, :]
    angle_y = coordinates[1][:, None] * frequency[None, :]
    return jnp.concatenate(
        [jnp.sin(angle_x), jnp.cos(angle_x), jnp.sin(angle_y), jnp.cos(angle_y)], axis=1
    )


def matmul(left, right):
    return jnp.dot(left, right, preferred_element_type=jnp.float32)


def across(left, right):
    return lax.dot_general(
        left, right, (((1,), (1,)), ((), ())), preferred_element_type=jnp.float32
    )


def contract_rows(left, right):
    return lax.dot_general(
        left, right, (((0,), (0,)), ((), ())), preferred_element_type=jnp.float32
    )


def split_heads(joint):
    row_count = joint.shape[0]
    queries = joint[:, :D].reshape(row_count, -1, HEAD_DIM)
    keys = joint[:, D : 2 * D].reshape(row_count, -1, HEAD_DIM)
    values = joint[:, 2 * D :].reshape(row_count, -1, HEAD_DIM)
    return (queries, keys, values)


def masked_scores(queries, keys, allowed):
    scores = jnp.einsum(
        "qhd,khd->hqk", queries, keys, preferred_element_type=jnp.float32
    ) * HEAD_DIM ** (-0.5)
    return jnp.where(allowed[None], scores, NEG_SCORE)


def attention_forward(joint, allowed):
    queries, keys, values = split_heads(joint)
    masked = masked_scores(queries, keys, allowed)
    peak = jnp.max(masked, axis=-1, keepdims=True)
    raised = jnp.exp(masked - peak)
    denom = jnp.sum(raised, axis=-1, keepdims=True)
    probs = raised / denom
    logsum = peak + jnp.log(denom)
    context = jnp.einsum(
        "hqk,khd->qhd", probs.astype(jnp.bfloat16), values, preferred_element_type=jnp.float32
    )
    return (context.reshape(joint.shape[0], D).astype(jnp.bfloat16), logsum)


def attention_backward(joint, allowed, logsum, context_grad):
    row_count = joint.shape[0]
    queries, keys, values = split_heads(joint)
    probs = jnp.exp(masked_scores(queries, keys, allowed) - logsum)
    probs_low = probs.astype(jnp.bfloat16)
    incoming = context_grad.reshape(row_count, -1, HEAD_DIM)
    value_grad = jnp.einsum("hqk,qhd->khd", probs_low, incoming, preferred_element_type=jnp.float32)
    prob_grad = jnp.einsum("qhd,khd->hqk", incoming, values, preferred_element_type=jnp.float32)
    score_grad = (probs * (prob_grad - jnp.sum(probs * prob_grad, axis=-1, keepdims=True))).astype(
        jnp.bfloat16
    )
    query_grad = jnp.einsum(
        "hqk,khd->qhd", score_grad, keys, preferred_element_type=jnp.float32
    ) * HEAD_DIM ** (-0.5)
    key_grad = jnp.einsum(
        "hqk,qhd->khd", score_grad, queries, preferred_element_type=jnp.float32
    ) * HEAD_DIM ** (-0.5)
    return jnp.concatenate(
        [
            query_grad.reshape(row_count, D),
            key_grad.reshape(row_count, D),
            value_grad.reshape(row_count, D),
        ],
        axis=1,
    ).astype(jnp.bfloat16)

AXES = ("dp", "fsdp")
GROUP = 4
CHUNK = 3456
NARROW = 8


def low(values):
    return values.astype(jnp.bfloat16)


def wide(values):
    return values.astype(jnp.float32)


def device_total():
    return lax.axis_size("dp") * lax.axis_size("fsdp")


def device_index():
    return lax.axis_index("dp") * lax.axis_size("fsdp") + lax.axis_index("fsdp")


def swap(values, mask):
    return lax.ppermute(values, AXES, [(i, i ^ mask) for i in range(device_total())])


def ring_order():
    total = device_total() // GROUP
    return list(range(0, total, 2)) + list(range(total - 1, 0, -2))


def shift(values, step):
    order = ring_order()
    total = len(order)
    pairs = []
    for place in range(total):
        for quarter in range(GROUP):
            pairs.append(
                (order[place] * GROUP + quarter, order[(place + step) % total] * GROUP + quarter)
            )
    return lax.ppermute(values, AXES, pairs)


def ring_place():
    order = ring_order()
    inverse = [order.index(t) for t in range(len(order))]
    return jnp.array(inverse, jnp.int32)[device_index() // GROUP]


def ring_owner(step):
    order = ring_order()
    return jnp.array(order, jnp.int32)[(ring_place() - step) % len(order)]


def same_quarter():
    return [[d for d in range(lax.axis_size("dp")) if d % 2 == odd] for odd in range(2)]


def pick(blocks, index):
    return lax.dynamic_index_in_dim(blocks, index, 0, keepdims=False)


def ring_scatter(blocks):
    total = device_total() // GROUP
    if total > NARROW:
        full = jnp.zeros_like(blocks)
        for s in range(total):
            full = lax.dynamic_update_index_in_dim(full, blocks[s], ring_owner(s), 0)
        return lax.psum_scatter(
            full, "dp", axis_index_groups=same_quarter(), scatter_dimension=0, tiled=False
        )
    half = blocks.shape[1] // 2
    top, bottom = blocks[1, :half], blocks[total - 1, half:]
    for s in range(2, total + 1):
        top = shift(top, 1)
        bottom = shift(bottom, -1)
        top = wide(top) + wide(blocks[s % total, :half])
        bottom = wide(bottom) + wide(blocks[(total - s) % total, half:])
        if s < total:
            top, bottom = low(top), low(bottom)
    return jnp.concatenate([top, bottom])


def group_exchange(blocks, quarter):
    return [pick(blocks, quarter)] + [swap(pick(blocks, quarter ^ m), m) for m in range(1, GROUP)]


def group_gather(values):
    pair = jnp.stack([values, swap(values, 2)])
    other = swap(pair, 1)
    return jnp.stack([pair[0], other[0], pair[1], other[1]])


def group_scatter(parts):
    mine = jnp.stack([parts[0], parts[2]])
    theirs = low(jnp.stack([parts[1], parts[3]]))
    summed = wide(mine) + wide(swap(theirs, 1))
    return summed[0] + wide(swap(low(summed[1]), 2))


def by_quarter(pieces, quarter):
    stacked = jnp.stack(pieces)
    return [pick(stacked, quarter ^ j) for j in range(GROUP)]


def gene_chunks(values):
    padded = jnp.pad(values, ((0, 0), (0, GROUP * CHUNK - GENES)))
    return jnp.stack([padded[:, j * CHUNK : (j + 1) * CHUNK] for j in range(GROUP)])


def sum_all(values):
    mask = 1
    while mask < device_total():
        values = values + swap(values, mask)
        mask *= 2
    return values


def scatter_all(values):
    me = device_index()
    mask = 1
    values = values[None]
    while mask < device_total():
        bit = (me // mask) % 2
        rows = values.shape[1]
        split = values.reshape(values.shape[0], rows // 2, 2, values.shape[2])
        keep = lax.dynamic_index_in_dim(split, bit, 2, keepdims=False)
        give = lax.dynamic_index_in_dim(split, 1 - bit, 2, keepdims=False)
        values = keep + swap(give, mask)
        mask *= 2
    return values[0, 0]


def by_ring(blocks):
    return jnp.stack([pick(blocks, ring_owner(s)) for s in range(blocks.shape[0])])


def halves_scatter(values, rows, ring_first):
    total = device_total() // GROUP
    me = device_index()
    core, side = me % 2, (me // 2) % 2
    split = values.reshape(total, 2, 2, rows, values.shape[1])
    keep = lax.dynamic_index_in_dim(split, core, 2, keepdims=False)
    give = lax.dynamic_index_in_dim(split, 1 - core, 2, keepdims=False)
    chip = low(wide(keep) + wide(swap(low(give), 1)))
    if ring_first:
        ringed = jnp.stack([pick(chip, ring_owner(s)) for s in range(total)])
        pair = low(ring_scatter(ringed.reshape(total, 2 * rows, -1)).reshape(2, rows, -1))
        return wide(pick(pair, side)) + wide(swap(pick(pair, 1 - side), 2))
    keep = lax.dynamic_index_in_dim(chip, side, 1, keepdims=False)
    give = lax.dynamic_index_in_dim(chip, 1 - side, 1, keepdims=False)
    both = low(wide(keep) + wide(swap(give, 2)))
    return wide(ring_scatter(jnp.stack([pick(both, ring_owner(s)) for s in range(total)])))


MESH = pl.DeviceIdType.MESH


class Where:
    def __init__(self, total):
        dp = lax.axis_index("dp")
        self.total = total
        self.core = lax.axis_index("fsdp")
        self.x = dp % 2
        self.t = dp // 2
        self.quarter = 2 * self.x + self.core
        y, z = self.t % 2, self.t // 2
        self.k = z + y * (total - 1 - 2 * z)
        self.right = (2 * self.owner(-1) + self.x, self.core)
        self.left = (2 * self.owner(1) + self.x, self.core)
        self.peers = [
            None,
            (dp, 1 - self.core),
            (2 * self.t + 1 - self.x, self.core),
            (2 * self.t + 1 - self.x, 1 - self.core),
        ]
        self.quarters = [
            self.quarter,
            2 * self.x + 1 - self.core,
            2 * (1 - self.x) + self.core,
            2 * (1 - self.x) + 1 - self.core,
        ]

    def owner(self, step):
        place = (self.k - step + self.total) % self.total
        y = place // (self.total // 2)
        return 2 * (place + y * (self.total - 1 - 2 * place)) + y

    def meet(self):
        barrier = pltpu.get_barrier_semaphore()
        others = self.peers[1:] + [self.right, self.left]
        for other in others:
            pl.semaphore_signal(barrier, inc=1, device_id=other, device_id_type=MESH)
        pl.semaphore_wait(barrier, len(others))


class Copies:
    def __init__(self, send_sems, recv_sems, local_sems):
        self.send_sems, self.recv_sems, self.local_sems = send_sems, recv_sems, local_sems
        self.remote_count = self.local_count = 0
        self.sent = []

    def send(self, source, target, device):
        at = self.remote_count
        self.remote_count += 1
        copy = pltpu.make_async_remote_copy(
            source,
            target,
            self.send_sems.at[at],
            self.recv_sems.at[at],
            device_id=device,
            device_id_type=MESH,
        )
        copy.start()
        self.sent.append(copy)
        return copy

    def local(self, source, target):
        at = self.local_count
        self.local_count += 1
        copy = pltpu.make_async_copy(source, target, self.local_sems.at[at])
        copy.start()
        return copy

    def finish(self):
        for copy in self.sent:
            copy.wait_send()


def gather_kernel(total, *refs):
    (cells, embed, decoder, joint, small, output, encoder, up, down) = refs[:9]
    (cells_all, embed_all, decoder_all, joint_all, small_all) = refs[9:14]
    (output_all, encoder_all, up_all, down_all) = refs[14:18]
    here = Where(total)
    copies = Copies(*refs[18:])
    here.meet()
    t, x, core = here.t, here.x, here.core
    last = total - 1

    late = [(up, up_all, 1), (output, output_all, 1), (down, down_all, -1), (encoder, encoder_all, -1)]
    towards = {1: here.right, -1: here.left}
    flying = {}
    for n, (own, full, way) in enumerate(late):
        flying["late", n] = copies.send(own, full.at[t, x, core], towards[way])
    shares = []
    for m in (2, 3, 1):
        to, chunk = here.peers[m], here.quarters[m]
        shares.append(copies.send(embed.at[chunk], embed_all.at[t, here.quarter], to))
        shares.append(copies.send(decoder.at[chunk], decoder_all.at[t, here.quarter], to))
    pairs = [
        copies.send(own, full.at[t, x, core], here.peers[2])
        for own, full in ((joint, joint_all), (small, small_all))
    ]
    cell_moves = [
        copies.send(cells.at[here.quarters[m]], cells_all.at[m], here.peers[m]) for m in (2, 3, 1)
    ]
    own_table = [
        copies.local(embed.at[here.quarter], embed_all.at[t, here.quarter]),
        copies.local(decoder.at[here.quarter], decoder_all.at[t, here.quarter]),
    ]
    own_early = [
        copies.local(own, full.at[t, x, core])
        for own, full in ((joint, joint_all), (small, small_all))
    ]
    own_late = [copies.local(own, full.at[t, x, core]) for own, full, _ in late]
    own_cells = copies.local(cells.at[here.quarter], cells_all.at[0])

    def late_step(s):
        for n, (_, full, way) in enumerate(late):
            flying["late", n].wait_recv()
            if s < last:
                block = full.at[here.owner(way * s), x, core]
                flying["late", n] = copies.send(block, block, towards[way])

    def early_block(full, way, s):
        return full.at[here.owner(way * s), 0 if way == 1 else 1, core]

    def table_block(full, way, s):
        return full.at[here.owner(way * s), pl.ds(0 if way == 1 else 2, 2)]

    early = [(full, way, early_block) for full in (joint_all, small_all) for way in (1, -1)]
    tables = [(full, way, table_block) for full in (embed_all, decoder_all) for way in (1, -1)]

    def step(name, items, s):
        if s == 0:
            for copy in {"early": own_early, "table": own_table}[name]:
                copy.wait()
            for copy in {"early": pairs, "table": shares}[name]:
                copy.wait_recv()
        for n, (full, way, block_of) in enumerate(items):
            if s > 0:
                flying[name, n].wait_recv()
            if s < last:
                block = block_of(full, way, s)
                flying[name, n] = copies.send(block, block, towards[way])

    across_x, across_core = [], []
    for slot in range(1, last + 7):
        if slot <= last:
            late_step(slot)
        if slot == last:
            for copy in own_late:
                copy.wait()
            for _, full, _ in late:
                block = full.at[:, x, core]
                across_x.append(copies.send(block, block, here.peers[2]))
        if 0 <= slot - 2 <= last:
            step("early", early, slot - 2)
        if slot - 2 == last:
            for full in (joint_all, small_all):
                block = full.at[:, :, core]
                across_core.append(copies.send(block, block, here.peers[1]))
        if 0 <= slot - 3 <= last:
            step("table", tables, slot - 3)
    for copy, (_, full, _) in zip(across_x, late):
        copy.wait_recv()
        block = full.at[:, :, core]
        across_core.append(copies.send(block, block, here.peers[1]))
    for copy in cell_moves + across_core:
        copy.wait_recv()
    own_cells.wait()
    copies.finish()


def gather_weights(cells, embed, decoder, joint, small, output, encoder, up, down):
    total = device_total() // GROUP
    own = [joint, small, output, encoder, up, down]
    tables = [embed, decoder]
    operands = [cells] + tables + own
    shapes = (
        [cells.shape]
        + [(total,) + v.shape for v in tables]
        + [(total, 2, 2) + v.shape for v in own]
    )
    remote = 15 + 12 * (total - 1) + 10
    return pl.pallas_call(
        functools.partial(gather_kernel, total),
        out_shape=[jax.ShapeDtypeStruct(s, jnp.bfloat16) for s in shapes],
        in_specs=[pl.BlockSpec(memory_space=pl.ANY)] * len(operands),
        out_specs=[pl.BlockSpec(memory_space=pl.ANY)] * len(operands),
        scratch_shapes=[
            pltpu.SemaphoreType.DMA((remote,)),
            pltpu.SemaphoreType.DMA((remote,)),
            pltpu.SemaphoreType.DMA((9,)),
        ],
        compiler_params=pltpu.CompilerParams(
            collective_id=1, has_side_effects=True, vmem_limit_bytes=8 * 2**20
        ),
        name="gather_weights",
    )(*operands)


def gather_plain(cells, embed, decoder, *own):
    quarter = device_index() % GROUP
    total = device_total() // GROUP
    groups = same_quarter()

    def table(values):
        block = jnp.stack(by_quarter(group_exchange(values, quarter), quarter))
        return lax.all_gather(block, "dp", axis_index_groups=groups, axis=0, tiled=False)

    cells_all = jnp.stack(group_exchange(cells, quarter))
    return [cells_all, table(embed), table(decoder)] + [
        lax.all_gather(v, AXES, axis=0, tiled=False) for v in own
    ]


def shards(
    cells,
    coordinates,
    slide_ids,
    live_mask,
    components,
    noise,
    ramp_weight,
    embed_weight,
    query_key_value,
    output_weight,
    up_weight,
    up_bias,
    down_weight,
    down_bias,
    first_gain,
    first_shift,
    second_gain,
    second_shift,
    encoder_weight,
    encoder_bias,
    prior_mean,
    prior_logvar,
    decoder_weight,
):
    row_count = cells.shape[0]
    devices = device_total()
    total = devices // GROUP
    me = device_index()
    quarter = me % GROUP
    rows = embed_weight.shape[0]
    thin = decoder_weight.shape[0]
    cell_total = row_count * devices
    live = live_mask[0].astype(jnp.float32)
    slides = slide_ids[0]
    places = jnp.arange(row_count)
    allowed = (slides[:, None] == slides[None, :]) & (
        (live[None, :] > 0.5) | (places[:, None] == places[None, :])
    )
    onehot = (
        components[:, None] == jnp.arange(prior_mean.shape[0], dtype=jnp.int32)[None, :]
    ).astype(jnp.float32)

    live_group = group_gather(live_mask).reshape(-1).astype(jnp.float32)
    small = jnp.concatenate(
        [
            up_bias.reshape(rows, 4),
            down_bias.reshape(rows, 1),
            first_gain.reshape(rows, 1),
            first_shift.reshape(rows, 1),
            second_gain.reshape(rows, 1),
            second_shift.reshape(rows, 1),
            encoder_bias.reshape(rows, 1),
            prior_mean.reshape(rows, 8),
            prior_logvar.reshape(rows, 8),
            jnp.full((rows, 1), jnp.sum(live), jnp.bfloat16),
        ],
        axis=1,
    )
    small_columns = small.shape[1]
    small = jnp.pad(small, ((0, 0), (0, 128 - small_columns)))
    gather = gather_weights if total <= NARROW else gather_plain
    cells_group, embed_cols, decoder_cols, *middle = gather(
        gene_chunks(cells),
        gene_chunks(embed_weight),
        gene_chunks(decoder_weight),
        query_key_value,
        small,
        output_weight,
        encoder_weight,
        up_weight,
        down_weight,
    )
    cells_group = cells_group.reshape(GROUP * row_count, CHUNK)
    embed_cols = embed_cols.reshape(-1, CHUNK)
    decoder_cols = decoder_cols.reshape(-1, CHUNK)
    middle = [full.reshape(-1, full.shape[-1]) for full in middle]
    joint_full, small_full, output_full, encoder_full, up_full, down_full = middle
    small_full = wide(small_full)
    up_bias_full = small_full[:, 0:4].reshape(-1)
    down_bias_full = small_full[:, 4]
    gain_first = small_full[:, 5]
    shift_first = small_full[:, 6]
    gain_second = small_full[:, 7]
    shift_second = small_full[:, 8]
    encoder_bias_full = small_full[:, 9]
    kinds = prior_mean.shape[0]

    def prior_full(columns):
        return columns.reshape(devices, kinds, -1).transpose(1, 0, 2).reshape(kinds, LATENT)

    prior_mean_full = prior_full(small_full[:, 10:18])
    prior_logvar_full = prior_full(small_full[:, 18:26])
    count = jnp.sum(small_full.reshape(devices, rows, 128)[:, 0, 26])

    embedded = low(across(cells_group, embed_cols))
    embedded = embedded.reshape(GROUP, row_count, D)
    embedded = group_scatter(embedded)
    start_state = embedded + positions(coordinates)
    normed_first = layer_norm(start_state, gain_first, shift_first).astype(jnp.bfloat16)
    joint = matmul(normed_first, joint_full).astype(jnp.bfloat16)
    context, logsum = attention_forward(joint, allowed)
    middle_state = start_state + matmul(context, output_full)
    normed_second = layer_norm(middle_state, gain_second, shift_second).astype(jnp.bfloat16)
    pre = matmul(normed_second, up_full) + up_bias_full
    active = jax.nn.gelu(pre, approximate=True).astype(jnp.bfloat16)
    end_state = middle_state + (matmul(active, down_full) + down_bias_full)
    end_low = end_state.astype(jnp.bfloat16)
    encoded = matmul(end_low, encoder_full) + encoder_bias_full
    latent_mean = encoded[:, :LATENT]
    latent_logvar = encoded[:, LATENT:]
    latent = (latent_mean + jnp.exp(0.5 * latent_logvar) * noise).astype(jnp.bfloat16)
    latent_group = group_gather(latent).reshape(GROUP * row_count, LATENT)

    center = jnp.dot(onehot, prior_mean_full, precision=lax.Precision.HIGHEST)
    scale = jnp.dot(onehot, prior_logvar_full, precision=lax.Precision.HIGHEST)
    gap = latent_mean - center
    inverse = jnp.exp(-scale)
    grown = jnp.exp(latent_logvar)
    diverge = 0.5 * (scale - latent_logvar + (grown + gap * gap) * inverse - 1.0)
    kl_mean = sum_all(jnp.sum(live[:, None] * diverge, axis=0, keepdims=True))[0] / count

    recon = matmul(latent_group, decoder_cols)
    miss = recon - wide(cells_group)
    recon_local = jnp.sum(live_group * (0.5 * jnp.sum(miss * miss, axis=1)))
    shifted = (kl_mean - FREE_FLOOR) / FREE_TEMP
    free = FREE_FLOOR + FREE_TEMP * jax.nn.softplus(shifted)
    ratio = cell_total / count
    recon_grad = low(ratio * live_group[:, None] * miss)
    decoder_term = low(contract_rows(latent_group, recon_grad))
    decoder_block = low(ring_scatter(by_ring(decoder_term.reshape(total, GROUP * thin, CHUNK))))
    latent_grad = low(across(recon_grad, decoder_cols))
    latent_grad = latent_grad.reshape(GROUP, row_count, LATENT)
    latent_grad = wide(low(group_scatter(latent_grad)))

    kl_scale = ratio * ramp_weight * jax.nn.sigmoid(shifted)[None, :] * live[:, None]
    pulled = kl_scale * gap * inverse
    mean_grad = latent_grad + pulled
    logvar_grad = latent_grad * 0.5 * jnp.exp(0.5 * latent_logvar) * noise + kl_scale * 0.5 * (
        grown * inverse - 1.0
    )
    encoded_grad = jnp.concatenate([mean_grad, logvar_grad], axis=1).astype(jnp.bfloat16)
    prior_mean_grad = jnp.dot(onehot.T, -pulled, precision=lax.Precision.HIGHEST)
    prior_logvar_grad = jnp.dot(
        onehot.T,
        kl_scale * 0.5 * (1.0 - (grown + gap * gap) * inverse),
        precision=lax.Precision.HIGHEST,
    )
    end_grad = across(encoded_grad, encoder_full)
    branch_grad = end_grad.astype(jnp.bfloat16)
    encoder_term = low(contract_rows(end_low, encoded_grad))
    encoder_bias_grad = jnp.sum(encoded_grad.astype(jnp.float32), axis=0)
    down_term = low(contract_rows(active, branch_grad))
    down_bias_grad = jnp.sum(branch_grad.astype(jnp.float32), axis=0)
    down_pack = jnp.concatenate(
        [
            encoder_term.reshape(devices, rows, D),
            down_term.reshape(devices, 4 * rows, D),
        ],
        axis=1,
    ).reshape(-1, D)
    down_pack = halves_scatter(down_pack, 5 * rows, False)
    encoder_weight_grad = down_pack[:rows]
    down_weight_grad = down_pack[rows:]
    active_grad = across(branch_grad, down_full)
    gelu_value, gelu_back = jax.vjp(lambda value: jax.nn.gelu(value, approximate=True), pre)
    pre_grad = gelu_back(active_grad)[0].astype(jnp.bfloat16)
    up_weight_grad = halves_scatter(low(contract_rows(normed_second, pre_grad)), rows, False)
    up_bias_grad = jnp.sum(pre_grad.astype(jnp.float32), axis=0)
    second_out_grad = across(pre_grad, up_full)
    norm_value, second_back = jax.vjp(layer_norm, middle_state, gain_second, shift_second)
    state_part, second_gain_grad, second_shift_grad = second_back(second_out_grad)
    middle_grad = end_grad + state_part
    attend_grad = middle_grad.astype(jnp.bfloat16)
    output_term = low(contract_rows(context, attend_grad))
    context_grad = across(attend_grad, output_full).astype(jnp.bfloat16)
    joint_grad = attention_backward(joint, allowed, logsum, context_grad)
    joint_term = low(contract_rows(normed_first, joint_grad))
    joint_pack = halves_scatter(jnp.concatenate([joint_term, output_term], axis=1), rows, True)
    joint_weight_grad = joint_pack[:, : 3 * D]
    output_weight_grad = joint_pack[:, 3 * D :]
    first_out_grad = across(joint_grad, joint_full)
    first_value, first_back = jax.vjp(layer_norm, start_state, gain_first, shift_first)
    start_part, first_gain_grad, first_shift_grad = first_back(first_out_grad)
    start_grad = middle_grad + start_part
    start_low = start_grad.astype(jnp.bfloat16)
    start_group = group_gather(start_low).reshape(GROUP * row_count, D)
    embed_term = low(contract_rows(start_group, cells_group))
    embed_block = low(ring_scatter(by_ring(embed_term.reshape(total, GROUP * rows, CHUNK))))
    cells_half = low(matmul(start_group, embed_cols) - wide(recon_grad))

    def to_owners(blocks):
        pieces = [blocks[0]] + [swap(blocks[m], m) for m in range(1, GROUP)]
        return jnp.concatenate(by_quarter(pieces, quarter), axis=1)[:, :GENES]

    cells_grad = to_owners(cells_half.reshape(GROUP, row_count, CHUNK))
    embed_block = embed_block.reshape(GROUP, rows, CHUNK)
    decoder_block = decoder_block.reshape(GROUP, thin, CHUNK)
    blocks = jnp.concatenate([embed_block, decoder_block], axis=1)
    blocks = [pick(blocks, quarter ^ m) for m in range(GROUP)]
    weight_grads = wide(to_owners(jnp.stack(blocks)))
    embed_grad, decoder_grad = weight_grads[:rows], weight_grads[rows:]

    def prior_rows(values):
        return values.reshape(kinds, devices, -1).transpose(1, 0, 2).reshape(devices, -1)

    vectors = [
        up_bias_grad,
        down_bias_grad,
        first_gain_grad,
        first_shift_grad,
        second_gain_grad,
        second_shift_grad,
        encoder_bias_grad,
    ]
    packed = jnp.concatenate(
        [vector.reshape(devices, -1) for vector in vectors]
        + [prior_rows(prior_mean_grad), prior_rows(prior_logvar_grad)],
        axis=1,
    )
    packed = scatter_all(packed)
    ends = [0]
    for vector in vectors:
        ends.append(ends[-1] + vector.shape[0] // devices)
    vector_grads = [packed[ends[i] : ends[i + 1]] for i in range(len(vectors))]
    prior_size = kinds * LATENT // devices
    prior_mean_out = packed[ends[-1] : ends[-1] + prior_size].reshape(kinds, -1)
    prior_logvar_out = packed[ends[-1] + prior_size :].reshape(kinds, -1)
    recon_total = sum_all(jnp.full((1, 128), recon_local, jnp.float32))[0, 0]
    loss = (recon_total / count + ramp_weight * jnp.sum(free)) / GENES
    return (
        loss,
        cells_grad,
        embed_grad,
        joint_weight_grad,
        output_weight_grad,
        up_weight_grad,
        vector_grads[0],
        down_weight_grad,
        vector_grads[1],
        vector_grads[2],
        vector_grads[3],
        vector_grads[4],
        vector_grads[5],
        encoder_weight_grad,
        vector_grads[6],
        prior_mean_out,
        prior_logvar_out,
        decoder_grad,
    )


def solution(mesh):
    in_specs = (
        P(("dp", "fsdp"), None),
        P(None, ("dp", "fsdp")),
        P(("dp", "fsdp"), None),
        P(("dp", "fsdp"), None),
        P(("dp", "fsdp")),
        P(("dp", "fsdp"), None),
        P(),
        P(("dp", "fsdp"), None),
        P(("dp", "fsdp"), None),
        P(("dp", "fsdp"), None),
        P(("dp", "fsdp"), None),
        P(("dp", "fsdp")),
        P(("dp", "fsdp"), None),
        P(("dp", "fsdp")),
        P(("dp", "fsdp")),
        P(("dp", "fsdp")),
        P(("dp", "fsdp")),
        P(("dp", "fsdp")),
        P(("dp", "fsdp"), None),
        P(("dp", "fsdp")),
        P(None, ("dp", "fsdp")),
        P(None, ("dp", "fsdp")),
        P(("dp", "fsdp"), None),
    )
    out_specs = (
        P(),
        P(("dp", "fsdp"), None),
        P(("dp", "fsdp"), None),
        P(("dp", "fsdp"), None),
        P(("dp", "fsdp"), None),
        P(("dp", "fsdp"), None),
        P(("dp", "fsdp")),
        P(("dp", "fsdp"), None),
        P(("dp", "fsdp")),
        P(("dp", "fsdp")),
        P(("dp", "fsdp")),
        P(("dp", "fsdp")),
        P(("dp", "fsdp")),
        P(("dp", "fsdp"), None),
        P(("dp", "fsdp")),
        P(None, ("dp", "fsdp")),
        P(None, ("dp", "fsdp")),
        P(("dp", "fsdp"), None),
    )
    return jax.shard_map(shards, mesh=mesh, in_specs=in_specs, out_specs=out_specs, check_vma=False)
```

```python
import functools
import math

import jax
import jax.numpy as jnp
from jax import lax
from jax.experimental import pallas as pl
from jax.experimental.pallas import tpu as pltpu
from jax.sharding import PartitionSpec as P

D = 1024
HEAD_DIM = 64
GENES = 13500
LATENT = 512


NEG_SCORE = -1000000000.0
NORM_EPS = 1e-05
FREE_FLOOR = 1.0
FREE_TEMP = 0.25


def layer_norm(hidden, gain, shift):
    center = hidden - jnp.mean(hidden, axis=-1, keepdims=True)
    spread = jnp.mean(center * center, axis=-1, keepdims=True)
    return center * lax.rsqrt(spread + NORM_EPS) * gain + shift


def positions(coordinates):
    quarter = D // 4
    frequency = jnp.exp(jnp.arange(quarter, dtype=jnp.float32) * (-math.log(10000.0) / quarter))
    angle_x = coordinates[0][:, None] * frequency[None, :]
    angle_y = coordinates[1][:, None] * frequency[None, :]
    return jnp.concatenate(
        [jnp.sin(angle_x), jnp.cos(angle_x), jnp.sin(angle_y), jnp.cos(angle_y)], axis=1
    )


def matmul(left, right):
    return jnp.dot(left, right, preferred_element_type=jnp.float32)


def across(left, right):
    return lax.dot_general(
        left, right, (((1,), (1,)), ((), ())), preferred_element_type=jnp.float32
    )


def contract_rows(left, right):
    return lax.dot_general(
        left, right, (((0,), (0,)), ((), ())), preferred_element_type=jnp.float32
    )


def split_heads(joint):
    row_count = joint.shape[0]
    queries = joint[:, :D].reshape(row_count, -1, HEAD_DIM)
    keys = joint[:, D : 2 * D].reshape(row_count, -1, HEAD_DIM)
    values = joint[:, 2 * D :].reshape(row_count, -1, HEAD_DIM)
    return (queries, keys, values)


def masked_scores(queries, keys, allowed):
    scores = jnp.einsum(
        "qhd,khd->hqk", queries, keys, preferred_element_type=jnp.float32
    ) * HEAD_DIM ** (-0.5)
    return jnp.where(allowed[None], scores, NEG_SCORE)


def attention_forward(joint, allowed):
    queries, keys, values = split_heads(joint)
    masked = masked_scores(queries, keys, allowed)
    peak = jnp.max(masked, axis=-1, keepdims=True)
    raised = jnp.exp(masked - peak)
    denom = jnp.sum(raised, axis=-1, keepdims=True)
    probs = raised / denom
    logsum = peak + jnp.log(denom)
    context = jnp.einsum(
        "hqk,khd->qhd", probs.astype(jnp.bfloat16), values, preferred_element_type=jnp.float32
    )
    return (context.reshape(joint.shape[0], D).astype(jnp.bfloat16), logsum)


def attention_backward(joint, allowed, logsum, context_grad):
    row_count = joint.shape[0]
    queries, keys, values = split_heads(joint)
    probs = jnp.exp(masked_scores(queries, keys, allowed) - logsum)
    probs_low = probs.astype(jnp.bfloat16)
    incoming = context_grad.reshape(row_count, -1, HEAD_DIM)
    value_grad = jnp.einsum("hqk,qhd->khd", probs_low, incoming, preferred_element_type=jnp.float32)
    prob_grad = jnp.einsum("qhd,khd->hqk", incoming, values, preferred_element_type=jnp.float32)
    score_grad = (probs * (prob_grad - jnp.sum(probs * prob_grad, axis=-1, keepdims=True))).astype(
        jnp.bfloat16
    )
    query_grad = jnp.einsum(
        "hqk,khd->qhd", score_grad, keys, preferred_element_type=jnp.float32
    ) * HEAD_DIM ** (-0.5)
    key_grad = jnp.einsum(
        "hqk,qhd->khd", score_grad, queries, preferred_element_type=jnp.float32
    ) * HEAD_DIM ** (-0.5)
    return jnp.concatenate(
        [
            query_grad.reshape(row_count, D),
            key_grad.reshape(row_count, D),
            value_grad.reshape(row_count, D),
        ],
        axis=1,
    ).astype(jnp.bfloat16)

AXES = ("dp", "fsdp")
GROUP = 4
CHUNK = 3456
NARROW = 8


def low(values):
    return values.astype(jnp.bfloat16)


def wide(values):
    return values.astype(jnp.float32)


def device_total():
    return lax.axis_size("dp") * lax.axis_size("fsdp")


def device_index():
    return lax.axis_index("dp") * lax.axis_size("fsdp") + lax.axis_index("fsdp")


def swap(values, mask):
    return lax.ppermute(values, AXES, [(i, i ^ mask) for i in range(device_total())])


def same_quarter():
    return [[d for d in range(lax.axis_size("dp")) if d % 2 == odd] for odd in range(2)]


def pick(blocks, index):
    return lax.dynamic_index_in_dim(blocks, index, 0, keepdims=False)


def group_exchange(blocks, quarter):
    return [pick(blocks, quarter)] + [swap(pick(blocks, quarter ^ m), m) for m in range(1, GROUP)]


def group_gather(values):
    pair = jnp.stack([values, swap(values, 2)])
    other = swap(pair, 1)
    return jnp.stack([pair[0], other[0], pair[1], other[1]])


def group_scatter(parts):
    mine = jnp.stack([parts[0], parts[2]])
    theirs = low(jnp.stack([parts[1], parts[3]]))
    summed = wide(mine) + wide(swap(theirs, 1))
    return summed[0] + wide(swap(low(summed[1]), 2))


def by_quarter(pieces, quarter):
    stacked = jnp.stack(pieces)
    return [pick(stacked, quarter ^ j) for j in range(GROUP)]


def gene_chunks(values):
    padded = jnp.pad(values, ((0, 0), (0, GROUP * CHUNK - GENES)))
    return jnp.stack([padded[:, j * CHUNK : (j + 1) * CHUNK] for j in range(GROUP)])


def sum_all(values):
    mask = 1
    while mask < device_total():
        values = values + swap(values, mask)
        mask *= 2
    return values


def scatter_all(values):
    me = device_index()
    mask = 1
    values = values[None]
    while mask < device_total():
        bit = (me // mask) % 2
        rows = values.shape[1]
        split = values.reshape(values.shape[0], rows // 2, 2, values.shape[2])
        keep = lax.dynamic_index_in_dim(split, bit, 2, keepdims=False)
        give = lax.dynamic_index_in_dim(split, 1 - bit, 2, keepdims=False)
        values = keep + swap(give, mask)
        mask *= 2
    return values[0, 0]


MESH = pl.DeviceIdType.MESH


class Where:
    def __init__(self, total):
        dp = lax.axis_index("dp")
        self.total = total
        self.core = lax.axis_index("fsdp")
        self.x = dp % 2
        self.t = dp // 2
        self.quarter = 2 * self.x + self.core
        y, z = self.t % 2, self.t // 2
        self.k = z + y * (total - 1 - 2 * z)
        self.right = (2 * self.owner(-1) + self.x, self.core)
        self.left = (2 * self.owner(1) + self.x, self.core)
        self.peers = [
            None,
            (dp, 1 - self.core),
            (2 * self.t + 1 - self.x, self.core),
            (2 * self.t + 1 - self.x, 1 - self.core),
        ]
        self.quarters = [
            self.quarter,
            2 * self.x + 1 - self.core,
            2 * (1 - self.x) + self.core,
            2 * (1 - self.x) + 1 - self.core,
        ]

    def owner(self, step):
        place = (self.k - step + self.total) % self.total
        y = place // (self.total // 2)
        return 2 * (place + y * (self.total - 1 - 2 * place)) + y

    def meet(self):
        barrier = pltpu.get_barrier_semaphore()
        others = self.peers[1:] + [self.right, self.left]
        for other in others:
            pl.semaphore_signal(barrier, inc=1, device_id=other, device_id_type=MESH)
        pl.semaphore_wait(barrier, len(others))


class Copies:
    def __init__(self, send_sems, recv_sems, local_sems):
        self.send_sems, self.recv_sems, self.local_sems = send_sems, recv_sems, local_sems
        self.remote_count = self.local_count = 0
        self.sent = []

    def send(self, source, target, device):
        at = self.remote_count
        self.remote_count += 1
        copy = pltpu.make_async_remote_copy(
            source,
            target,
            self.send_sems.at[at],
            self.recv_sems.at[at],
            device_id=device,
            device_id_type=MESH,
        )
        copy.start()
        self.sent.append(copy)
        return copy

    def local(self, source, target):
        at = self.local_count
        self.local_count += 1
        copy = pltpu.make_async_copy(source, target, self.local_sems.at[at])
        copy.start()
        return copy

    def finish(self):
        for copy in self.sent:
            copy.wait_send()


def gather_kernel(total, *refs):
    (cells, embed, decoder, joint, small, output, encoder, up, down) = refs[:9]
    (cells_all, embed_all, decoder_all, joint_all, small_all) = refs[9:14]
    (output_all, encoder_all, up_all, down_all) = refs[14:18]
    here = Where(total)
    copies = Copies(*refs[18:])
    here.meet()
    t, x, core = here.t, here.x, here.core
    last = total - 1

    late = [(up, up_all, 1), (output, output_all, 1), (down, down_all, -1), (encoder, encoder_all, -1)]
    towards = {1: here.right, -1: here.left}
    flying = {}
    for n, (own, full, way) in enumerate(late):
        flying["late", n] = copies.send(own, full.at[t, x, core], towards[way])
    shares = []
    for m in (2, 3, 1):
        to, chunk = here.peers[m], here.quarters[m]
        shares.append(copies.send(embed.at[chunk], embed_all.at[t, here.quarter], to))
        shares.append(copies.send(decoder.at[chunk], decoder_all.at[t, here.quarter], to))
    pairs = [
        copies.send(own, full.at[t, x, core], here.peers[2])
        for own, full in ((joint, joint_all), (small, small_all))
    ]
    cell_moves = [
        copies.send(cells.at[here.quarters[m]], cells_all.at[m], here.peers[m]) for m in (2, 3, 1)
    ]
    own_table = [
        copies.local(embed.at[here.quarter], embed_all.at[t, here.quarter]),
        copies.local(decoder.at[here.quarter], decoder_all.at[t, here.quarter]),
    ]
    own_early = [
        copies.local(own, full.at[t, x, core])
        for own, full in ((joint, joint_all), (small, small_all))
    ]
    own_late = [copies.local(own, full.at[t, x, core]) for own, full, _ in late]
    own_cells = copies.local(cells.at[here.quarter], cells_all.at[0])

    def late_step(s):
        for n, (_, full, way) in enumerate(late):
            flying["late", n].wait_recv()
            if s < last:
                block = full.at[here.owner(way * s), x, core]
                flying["late", n] = copies.send(block, block, towards[way])

    def early_block(full, way, s):
        return full.at[here.owner(way * s), 0 if way == 1 else 1, core]

    def table_block(full, way, s):
        return full.at[here.owner(way * s), pl.ds(0 if way == 1 else 2, 2)]

    early = [(full, way, early_block) for full in (joint_all, small_all) for way in (1, -1)]
    tables = [(full, way, table_block) for full in (embed_all, decoder_all) for way in (1, -1)]

    def step(name, items, s):
        if s == 0:
            for copy in {"early": own_early, "table": own_table}[name]:
                copy.wait()
            for copy in {"early": pairs, "table": shares}[name]:
                copy.wait_recv()
        for n, (full, way, block_of) in enumerate(items):
            if s > 0:
                flying[name, n].wait_recv()
            if s < last:
                block = block_of(full, way, s)
                flying[name, n] = copies.send(block, block, towards[way])

    across_x, across_core = [], []
    for slot in range(1, last + 7):
        if slot <= last:
            late_step(slot)
        if slot == last:
            for copy in own_late:
                copy.wait()
            for _, full, _ in late:
                block = full.at[:, x, core]
                across_x.append(copies.send(block, block, here.peers[2]))
        if 0 <= slot - 2 <= last:
            step("early", early, slot - 2)
        if slot - 2 == last:
            for full in (joint_all, small_all):
                block = full.at[:, :, core]
                across_core.append(copies.send(block, block, here.peers[1]))
        if 0 <= slot - 3 <= last:
            step("table", tables, slot - 3)
    for copy, (_, full, _) in zip(across_x, late):
        copy.wait_recv()
        block = full.at[:, :, core]
        across_core.append(copies.send(block, block, here.peers[1]))
    for copy in cell_moves + across_core:
        copy.wait_recv()
    own_cells.wait()
    copies.finish()


def gather_weights(cells, embed, decoder, joint, small, output, encoder, up, down):
    total = device_total() // GROUP
    own = [joint, small, output, encoder, up, down]
    tables = [embed, decoder]
    operands = [cells] + tables + own
    shapes = (
        [cells.shape]
        + [(total,) + v.shape for v in tables]
        + [(total, 2, 2) + v.shape for v in own]
    )
    remote = 15 + 12 * (total - 1) + 10
    return pl.pallas_call(
        functools.partial(gather_kernel, total),
        out_shape=[jax.ShapeDtypeStruct(s, jnp.bfloat16) for s in shapes],
        in_specs=[pl.BlockSpec(memory_space=pl.ANY)] * len(operands),
        out_specs=[pl.BlockSpec(memory_space=pl.ANY)] * len(operands),
        scratch_shapes=[
            pltpu.SemaphoreType.DMA((remote,)),
            pltpu.SemaphoreType.DMA((remote,)),
            pltpu.SemaphoreType.DMA((9,)),
        ],
        compiler_params=pltpu.CompilerParams(
            collective_id=1, has_side_effects=True, vmem_limit_bytes=8 * 2**20
        ),
        name="gather_weights",
    )(*operands)


def add_rows(target, first, second, dtype):
    rows, columns = target.shape
    step = min(rows, 16 if columns > 2048 else 32)

    @pl.loop(0, rows // step)
    def _(i):
        part = pl.ds(pl.multiple_of(i * step, step), step)
        target[part, :] = (wide(first[part, :]) + wide(second[part, :])).astype(dtype)


def scatter_kernel(total, *refs):
    (embed, decoder, joint, output, encoder, up, down, cells) = refs[:8]
    (embed_out, decoder_out, cells_out) = refs[8:11]
    (joint_out, output_out, encoder_out, up_out, down_out) = refs[11:16]
    (chip_joint, chip_output, chip_encoder, chip_up, chip_down) = refs[16:21]
    (stage_up, stage_down) = refs[21:23]
    (sum_output, sum_encoder, sum_up, sum_down) = refs[23:27]
    (hop_embed, hop_decoder, hop_joint) = refs[27:30]
    (hop_output, hop_encoder, hop_up, hop_down) = refs[30:34]
    (local_embed, local_decoder) = refs[34:36]
    (last_embed, last_decoder, last_joint, other_joint) = refs[36:40]
    here = Where(total)
    copies = Copies(*refs[40:])
    here.meet()
    x, core, last = here.x, here.core, total - 1
    towards = {1: here.right, -1: here.left}
    flying = {}

    tables = []
    for term, hops, local, result in (
        (embed, hop_embed, local_embed, last_embed),
        (decoder, hop_decoder, local_decoder, last_decoder),
    ):
        for way in (1, -1):
            tables.append((term, hops, local, result, way, 0 if way == 1 else 1))

    def table_block(term, way, side, h):
        return term.at[here.owner(way * h), pl.ds(2 * side, 2)]

    def fetch(n, h):
        term, _, local, _, way, side = tables[n]
        flying["local", n, h] = copies.local(
            table_block(term, way, side, h + 1), local.at[h % 2, side]
        )

    for n, (term, hops, _, _, way, side) in enumerate(tables):
        flying["table", n] = copies.send(
            table_block(term, way, side, 1), hops.at[0, side], towards[way]
        )
    halves = {}
    for name, term, chip in (
        ("up", up, chip_up),
        ("down", down, chip_down),
        ("output", output, chip_output),
        ("encoder", encoder, chip_encoder),
        ("joint", joint, chip_joint),
    ):
        halves[name] = copies.send(term.at[:, :, 1 - core], chip, here.peers[1])
    loads = {
        "up": copies.local(up.at[:, :, core], stage_up),
        "down": copies.local(down.at[:, :, core], stage_down),
    }
    for h in (1, 2):
        for n in range(len(tables)):
            fetch(n, h)

    def table_hop(h):
        for n, (term, hops, local, result, way, side) in enumerate(tables):
            flying["table", n].wait_recv()
            flying["local", n, h].wait()
            for row in range(2):
                arrived = hops.at[h - 1, side, row]
                target = arrived if h < last else result.at[2 * side + row]
                add_rows(target, arrived, local.at[h % 2, side, row], jnp.bfloat16)
            if h < last:
                flying["table", n] = copies.send(
                    hops.at[h - 1, side], hops.at[h, side], towards[way]
                )
            if h + 2 <= last:
                fetch(n, h + 2)

    def chip_sum(name, chip, staged):
        halves[name].wait_recv()
        loads[name].wait()

        @pl.loop(0, total)
        def _(t):
            for side in range(2):
                add_rows(chip.at[t, side], chip.at[t, side], staged.at[t, side], jnp.bfloat16)

    across = {}

    def cross(name, chip, sums):
        across[name] = copies.send(chip.at[:, 1 - x], sums, here.peers[2])

    chip_sum("up", chip_up, stage_up)
    cross("up", chip_up, sum_up)
    staged_joint = stage_up.at[:, :, :, pl.ds(0, joint.shape[-1])]
    loads["joint"] = copies.local(joint.at[:, :, core], staged_joint)
    chip_sum("down", chip_down, stage_down)
    cross("down", chip_down, sum_down)
    slim = output.shape[3]
    staged_output = stage_down.at[:, :, pl.ds(0, slim)]
    staged_encoder = stage_down.at[:, :, pl.ds(slim, slim)]
    loads["output"] = copies.local(output.at[:, :, core], staged_output)
    loads["encoder"] = copies.local(encoder.at[:, :, core], staged_encoder)
    table_hop(1)
    chip_sum("joint", chip_joint, staged_joint)
    for side, way in ((0, 1), (1, -1)):
        flying["joint", side] = copies.send(
            chip_joint.at[here.owner(way), side], hop_joint.at[0, side], towards[way]
        )
    chip_sum("output", chip_output, staged_output)
    cross("output", chip_output, sum_output)
    chip_sum("encoder", chip_encoder, staged_encoder)
    cross("encoder", chip_encoder, sum_encoder)
    moves = [copies.send(cells.at[m], cells_out.at[here.quarter], here.peers[m]) for m in (2, 3, 1)]
    own = [copies.local(cells.at[0], cells_out.at[here.quarter])]

    def joint_hop(h):
        for side, way in ((0, 1), (1, -1)):
            flying["joint", side].wait_recv()
            arrived = hop_joint.at[h - 1, side]
            target = arrived if h < last else last_joint.at[side]
            local = chip_joint.at[here.owner(way * (h + 1)), side]
            add_rows(target, arrived, local, jnp.bfloat16)
            if h < last:
                flying["joint", side] = copies.send(arrived, hop_joint.at[h, side], towards[way])

    late = [
        ("up", sum_up, chip_up, hop_up, up_out, 1),
        ("down", sum_down, chip_down, hop_down, down_out, -1),
        ("output", sum_output, chip_output, hop_output, output_out, 1),
        ("encoder", sum_encoder, chip_encoder, hop_encoder, encoder_out, -1),
    ]

    def late_start():
        for name, sums, chip, hops, _, way in late:
            across[name].wait_recv()

            @pl.loop(0, total)
            def _(t):
                add_rows(sums.at[t], sums.at[t], chip.at[t, x], jnp.bfloat16)

            flying["late", name] = copies.send(sums.at[here.owner(way)], hops.at[0], towards[way])

    def late_hop(h):
        for name, sums, _, hops, result, way in late:
            flying["late", name].wait_recv()
            local = sums.at[here.owner(way * (h + 1))]
            if h < last:
                add_rows(hops.at[h - 1], hops.at[h - 1], local, jnp.bfloat16)
                flying["late", name] = copies.send(hops.at[h - 1], hops.at[h], towards[way])
            else:
                add_rows(result, hops.at[h - 1], local, jnp.float32)

    joint_hop(1)
    for h in range(2, last + 1):
        table_hop(h)
        joint_hop(h)
    for result, out in ((last_embed, embed_out), (last_decoder, decoder_out)):
        for m in (2, 3, 1):
            moves.append(
                copies.send(
                    result.at[here.quarters[m]], out.at[here.quarter], here.peers[m]
                )
            )
        own.append(copies.local(result.at[here.quarter], out.at[here.quarter]))
    joint_move = copies.send(last_joint.at[1 - x], other_joint, here.peers[2])
    late_start()
    for h in range(1, last + 1):
        late_hop(h)
    joint_move.wait_recv()
    add_rows(joint_out, last_joint.at[x], other_joint, jnp.float32)
    for copy in moves:
        copy.wait_recv()
    for copy in own:
        copy.wait()
    copies.finish()


def scatter_sums(embed, decoder, joint, output, encoder, up, down, cells):
    total = device_total() // GROUP
    last = total - 1
    operands = [embed, decoder, joint, output, encoder, up, down, cells]
    middle = [joint, output, encoder, up, down]
    thin = jnp.bfloat16
    out_shape = [jax.ShapeDtypeStruct(v.shape[1:], thin) for v in (embed, decoder)]
    out_shape += [jax.ShapeDtypeStruct(cells.shape, thin)]
    out_shape += [jax.ShapeDtypeStruct(v.shape[3:], jnp.float32) for v in middle]
    chips = [(total, 2) + v.shape[3:] for v in middle]
    sums = [(total,) + v.shape[3:] for v in middle[1:]]
    hops = [(last, 2, 2) + v.shape[2:] for v in (embed, decoder)]
    hops += [(last, 2) + joint.shape[3:]] + [(last,) + v.shape[3:] for v in middle[1:]]
    local = [(2, 2, 2) + v.shape[2:] for v in (embed, decoder)]
    results = [v.shape[1:] for v in (embed, decoder)] + [(2,) + joint.shape[3:], joint.shape[3:]]
    buffers = chips + [chips[3], chips[4]] + sums + hops + local + results
    remote, here = 12 + 6 * last + 4 * last + 7, 4 * last + 8
    return pl.pallas_call(
        functools.partial(scatter_kernel, total),
        out_shape=out_shape,
        in_specs=[pl.BlockSpec(memory_space=pl.ANY)] * len(operands),
        out_specs=[pl.BlockSpec(memory_space=pl.ANY)] * 3
        + [pl.BlockSpec(memory_space=pltpu.VMEM)] * 5,
        scratch_shapes=[pltpu.VMEM(shape, thin) for shape in buffers]
        + [
            pltpu.SemaphoreType.DMA((remote,)),
            pltpu.SemaphoreType.DMA((remote,)),
            pltpu.SemaphoreType.DMA((here,)),
        ],
        compiler_params=pltpu.CompilerParams(
            collective_id=2, has_side_effects=True, vmem_limit_bytes=60 * 2**20
        ),
        name="scatter_sums",
    )(*operands)


def scatter_plain(embed, decoder, joint, output, encoder, up, down, cells):
    quarter = device_index() % GROUP

    def sent(blocks):
        pieces = [pick(blocks, 0)] + [swap(blocks[m], m) for m in range(1, GROUP)]
        return jnp.stack(by_quarter(pieces, quarter))

    def table(term):
        block = lax.psum_scatter(
            term, "dp", axis_index_groups=same_quarter(), scatter_dimension=0, tiled=False
        )
        return sent(jnp.stack(by_quarter(list(block), quarter)))

    def middle(term):
        rows = term.reshape((device_total(),) + term.shape[3:])
        return wide(lax.psum_scatter(rows, AXES, scatter_dimension=0, tiled=False))

    return [table(embed), table(decoder), sent(cells)] + [
        middle(v) for v in (joint, output, encoder, up, down)
    ]


def gather_plain(cells, embed, decoder, *own):
    quarter = device_index() % GROUP
    total = device_total() // GROUP
    groups = same_quarter()

    def table(values):
        block = jnp.stack(by_quarter(group_exchange(values, quarter), quarter))
        return lax.all_gather(block, "dp", axis_index_groups=groups, axis=0, tiled=False)

    cells_all = jnp.stack(group_exchange(cells, quarter))
    return [cells_all, table(embed), table(decoder)] + [
        lax.all_gather(v, AXES, axis=0, tiled=False) for v in own
    ]


def shards(
    cells,
    coordinates,
    slide_ids,
    live_mask,
    components,
    noise,
    ramp_weight,
    embed_weight,
    query_key_value,
    output_weight,
    up_weight,
    up_bias,
    down_weight,
    down_bias,
    first_gain,
    first_shift,
    second_gain,
    second_shift,
    encoder_weight,
    encoder_bias,
    prior_mean,
    prior_logvar,
    decoder_weight,
):
    row_count = cells.shape[0]
    devices = device_total()
    total = devices // GROUP
    me = device_index()
    quarter = me % GROUP
    rows = embed_weight.shape[0]
    thin = decoder_weight.shape[0]
    cell_total = row_count * devices
    live = live_mask[0].astype(jnp.float32)
    slides = slide_ids[0]
    places = jnp.arange(row_count)
    allowed = (slides[:, None] == slides[None, :]) & (
        (live[None, :] > 0.5) | (places[:, None] == places[None, :])
    )
    onehot = (
        components[:, None] == jnp.arange(prior_mean.shape[0], dtype=jnp.int32)[None, :]
    ).astype(jnp.float32)

    live_group = group_gather(live_mask).reshape(-1).astype(jnp.float32)
    small = jnp.concatenate(
        [
            up_bias.reshape(rows, 4),
            down_bias.reshape(rows, 1),
            first_gain.reshape(rows, 1),
            first_shift.reshape(rows, 1),
            second_gain.reshape(rows, 1),
            second_shift.reshape(rows, 1),
            encoder_bias.reshape(rows, 1),
            prior_mean.reshape(rows, 8),
            prior_logvar.reshape(rows, 8),
            jnp.full((rows, 1), jnp.sum(live), jnp.bfloat16),
        ],
        axis=1,
    )
    small_columns = small.shape[1]
    small = jnp.pad(small, ((0, 0), (0, 128 - small_columns)))
    gather = gather_weights if total <= NARROW else gather_plain
    cells_group, embed_cols, decoder_cols, *middle = gather(
        gene_chunks(cells),
        gene_chunks(embed_weight),
        gene_chunks(decoder_weight),
        query_key_value,
        small,
        output_weight,
        encoder_weight,
        up_weight,
        down_weight,
    )
    cells_group = cells_group.reshape(GROUP * row_count, CHUNK)
    embed_cols = embed_cols.reshape(-1, CHUNK)
    decoder_cols = decoder_cols.reshape(-1, CHUNK)
    middle = [full.reshape(-1, full.shape[-1]) for full in middle]
    joint_full, small_full, output_full, encoder_full, up_full, down_full = middle
    small_full = wide(small_full)
    up_bias_full = small_full[:, 0:4].reshape(-1)
    down_bias_full = small_full[:, 4]
    gain_first = small_full[:, 5]
    shift_first = small_full[:, 6]
    gain_second = small_full[:, 7]
    shift_second = small_full[:, 8]
    encoder_bias_full = small_full[:, 9]
    kinds = prior_mean.shape[0]

    def prior_full(columns):
        return columns.reshape(devices, kinds, -1).transpose(1, 0, 2).reshape(kinds, LATENT)

    prior_mean_full = prior_full(small_full[:, 10:18])
    prior_logvar_full = prior_full(small_full[:, 18:26])
    count = jnp.sum(small_full.reshape(devices, rows, 128)[:, 0, 26])

    embedded = low(across(cells_group, embed_cols))
    embedded = embedded.reshape(GROUP, row_count, D)
    embedded = group_scatter(embedded)
    start_state = embedded + positions(coordinates)
    normed_first = layer_norm(start_state, gain_first, shift_first).astype(jnp.bfloat16)
    joint = matmul(normed_first, joint_full).astype(jnp.bfloat16)
    context, logsum = attention_forward(joint, allowed)
    middle_state = start_state + matmul(context, output_full)
    normed_second = layer_norm(middle_state, gain_second, shift_second).astype(jnp.bfloat16)
    pre = matmul(normed_second, up_full) + up_bias_full
    active = jax.nn.gelu(pre, approximate=True).astype(jnp.bfloat16)
    end_state = middle_state + (matmul(active, down_full) + down_bias_full)
    end_low = end_state.astype(jnp.bfloat16)
    encoded = matmul(end_low, encoder_full) + encoder_bias_full
    latent_mean = encoded[:, :LATENT]
    latent_logvar = encoded[:, LATENT:]
    latent = (latent_mean + jnp.exp(0.5 * latent_logvar) * noise).astype(jnp.bfloat16)
    latent_group = group_gather(latent).reshape(GROUP * row_count, LATENT)

    center = jnp.dot(onehot, prior_mean_full, precision=lax.Precision.HIGHEST)
    scale = jnp.dot(onehot, prior_logvar_full, precision=lax.Precision.HIGHEST)
    gap = latent_mean - center
    inverse = jnp.exp(-scale)
    grown = jnp.exp(latent_logvar)
    diverge = 0.5 * (scale - latent_logvar + (grown + gap * gap) * inverse - 1.0)
    kl_mean = sum_all(jnp.sum(live[:, None] * diverge, axis=0, keepdims=True))[0] / count

    recon = matmul(latent_group, decoder_cols)
    miss = recon - wide(cells_group)
    recon_local = jnp.sum(live_group * (0.5 * jnp.sum(miss * miss, axis=1)))
    shifted = (kl_mean - FREE_FLOOR) / FREE_TEMP
    free = FREE_FLOOR + FREE_TEMP * jax.nn.softplus(shifted)
    ratio = cell_total / count
    recon_grad = low(ratio * live_group[:, None] * miss)
    decoder_term = low(contract_rows(latent_group, recon_grad))
    latent_grad = low(across(recon_grad, decoder_cols))
    latent_grad = latent_grad.reshape(GROUP, row_count, LATENT)
    latent_grad = wide(low(group_scatter(latent_grad)))

    kl_scale = ratio * ramp_weight * jax.nn.sigmoid(shifted)[None, :] * live[:, None]
    pulled = kl_scale * gap * inverse
    mean_grad = latent_grad + pulled
    logvar_grad = latent_grad * 0.5 * jnp.exp(0.5 * latent_logvar) * noise + kl_scale * 0.5 * (
        grown * inverse - 1.0
    )
    encoded_grad = jnp.concatenate([mean_grad, logvar_grad], axis=1).astype(jnp.bfloat16)
    prior_mean_grad = jnp.dot(onehot.T, -pulled, precision=lax.Precision.HIGHEST)
    prior_logvar_grad = jnp.dot(
        onehot.T,
        kl_scale * 0.5 * (1.0 - (grown + gap * gap) * inverse),
        precision=lax.Precision.HIGHEST,
    )
    end_grad = across(encoded_grad, encoder_full)
    branch_grad = end_grad.astype(jnp.bfloat16)
    encoder_term = low(contract_rows(end_low, encoded_grad))
    encoder_bias_grad = jnp.sum(encoded_grad.astype(jnp.float32), axis=0)
    down_term = low(contract_rows(active, branch_grad))
    down_bias_grad = jnp.sum(branch_grad.astype(jnp.float32), axis=0)
    active_grad = across(branch_grad, down_full)
    gelu_value, gelu_back = jax.vjp(lambda value: jax.nn.gelu(value, approximate=True), pre)
    pre_grad = gelu_back(active_grad)[0].astype(jnp.bfloat16)
    up_term = low(contract_rows(normed_second, pre_grad))
    up_bias_grad = jnp.sum(pre_grad.astype(jnp.float32), axis=0)
    second_out_grad = across(pre_grad, up_full)
    norm_value, second_back = jax.vjp(layer_norm, middle_state, gain_second, shift_second)
    state_part, second_gain_grad, second_shift_grad = second_back(second_out_grad)
    middle_grad = end_grad + state_part
    attend_grad = middle_grad.astype(jnp.bfloat16)
    output_term = low(contract_rows(context, attend_grad))
    context_grad = across(attend_grad, output_full).astype(jnp.bfloat16)
    joint_grad = attention_backward(joint, allowed, logsum, context_grad)
    joint_term = low(contract_rows(normed_first, joint_grad))
    first_out_grad = across(joint_grad, joint_full)
    first_value, first_back = jax.vjp(layer_norm, start_state, gain_first, shift_first)
    start_part, first_gain_grad, first_shift_grad = first_back(first_out_grad)
    start_grad = middle_grad + start_part
    start_low = start_grad.astype(jnp.bfloat16)
    start_group = group_gather(start_low).reshape(GROUP * row_count, D)
    embed_term = low(contract_rows(start_group, cells_group))
    cells_half = low(matmul(start_group, embed_cols) - wide(recon_grad))

    def by_device(term):
        return term.reshape(total, 2, 2, term.shape[0] // devices, term.shape[1])

    scatter = scatter_sums if total <= NARROW else scatter_plain
    embed_grad, decoder_grad, cells_grad, *middle_grads = scatter(
        embed_term.reshape(total, GROUP, rows, CHUNK),
        decoder_term.reshape(total, GROUP, thin, CHUNK),
        by_device(joint_term),
        by_device(output_term),
        by_device(encoder_term),
        by_device(up_term),
        by_device(down_term),
        cells_half.reshape(GROUP, row_count, CHUNK),
    )

    def all_genes(chunks):
        return jnp.concatenate(list(chunks), axis=1)[:, :GENES]

    cells_grad = all_genes(cells_grad)
    embed_grad = wide(all_genes(embed_grad))
    decoder_grad = wide(all_genes(decoder_grad))
    (
        joint_weight_grad,
        output_weight_grad,
        encoder_weight_grad,
        up_weight_grad,
        down_weight_grad,
    ) = middle_grads

    def prior_rows(values):
        return values.reshape(kinds, devices, -1).transpose(1, 0, 2).reshape(devices, -1)

    vectors = [
        up_bias_grad,
        down_bias_grad,
        first_gain_grad,
        first_shift_grad,
        second_gain_grad,
        second_shift_grad,
        encoder_bias_grad,
    ]
    packed = jnp.concatenate(
        [vector.reshape(devices, -1) for vector in vectors]
        + [prior_rows(prior_mean_grad), prior_rows(prior_logvar_grad)],
        axis=1,
    )
    packed = scatter_all(packed)
    ends = [0]
    for vector in vectors:
        ends.append(ends[-1] + vector.shape[0] // devices)
    vector_grads = [packed[ends[i] : ends[i + 1]] for i in range(len(vectors))]
    prior_size = kinds * LATENT // devices
    prior_mean_out = packed[ends[-1] : ends[-1] + prior_size].reshape(kinds, -1)
    prior_logvar_out = packed[ends[-1] + prior_size :].reshape(kinds, -1)
    recon_total = sum_all(jnp.full((1, 128), recon_local, jnp.float32))[0, 0]
    loss = (recon_total / count + ramp_weight * jnp.sum(free)) / GENES
    return (
        loss,
        cells_grad,
        embed_grad,
        joint_weight_grad,
        output_weight_grad,
        up_weight_grad,
        vector_grads[0],
        down_weight_grad,
        vector_grads[1],
        vector_grads[2],
        vector_grads[3],
        vector_grads[4],
        vector_grads[5],
        encoder_weight_grad,
        vector_grads[6],
        prior_mean_out,
        prior_logvar_out,
        decoder_grad,
    )


def solution(mesh):
    in_specs = (
        P(("dp", "fsdp"), None),
        P(None, ("dp", "fsdp")),
        P(("dp", "fsdp"), None),
        P(("dp", "fsdp"), None),
        P(("dp", "fsdp")),
        P(("dp", "fsdp"), None),
        P(),
        P(("dp", "fsdp"), None),
        P(("dp", "fsdp"), None),
        P(("dp", "fsdp"), None),
        P(("dp", "fsdp"), None),
        P(("dp", "fsdp")),
        P(("dp", "fsdp"), None),
        P(("dp", "fsdp")),
        P(("dp", "fsdp")),
        P(("dp", "fsdp")),
        P(("dp", "fsdp")),
        P(("dp", "fsdp")),
        P(("dp", "fsdp"), None),
        P(("dp", "fsdp")),
        P(None, ("dp", "fsdp")),
        P(None, ("dp", "fsdp")),
        P(("dp", "fsdp"), None),
    )
    out_specs = (
        P(),
        P(("dp", "fsdp"), None),
        P(("dp", "fsdp"), None),
        P(("dp", "fsdp"), None),
        P(("dp", "fsdp"), None),
        P(("dp", "fsdp"), None),
        P(("dp", "fsdp")),
        P(("dp", "fsdp"), None),
        P(("dp", "fsdp")),
        P(("dp", "fsdp")),
        P(("dp", "fsdp")),
        P(("dp", "fsdp")),
        P(("dp", "fsdp")),
        P(("dp", "fsdp"), None),
        P(("dp", "fsdp")),
        P(None, ("dp", "fsdp")),
        P(None, ("dp", "fsdp")),
        P(("dp", "fsdp"), None),
    )
    return jax.shard_map(shards, mesh=mesh, in_specs=in_specs, out_specs=out_specs, check_vma=False)
```

```python
import functools
import math

import jax
import jax.numpy as jnp
from jax import lax
from jax.experimental import pallas as pl
from jax.experimental.pallas import tpu as pltpu
from jax.sharding import PartitionSpec as P

D = 1024
HEAD_DIM = 64
GENES = 13500
LATENT = 512


NEG_SCORE = -1000000000.0
NORM_EPS = 1e-05
FREE_FLOOR = 1.0
FREE_TEMP = 0.25


def layer_norm(hidden, gain, shift):
    center = hidden - jnp.mean(hidden, axis=-1, keepdims=True)
    spread = jnp.mean(center * center, axis=-1, keepdims=True)
    return center * lax.rsqrt(spread + NORM_EPS) * gain + shift


def positions(coordinates):
    quarter = D // 4
    frequency = jnp.exp(jnp.arange(quarter, dtype=jnp.float32) * (-math.log(10000.0) / quarter))
    angle_x = coordinates[0][:, None] * frequency[None, :]
    angle_y = coordinates[1][:, None] * frequency[None, :]
    return jnp.concatenate(
        [jnp.sin(angle_x), jnp.cos(angle_x), jnp.sin(angle_y), jnp.cos(angle_y)], axis=1
    )


def matmul(left, right):
    return jnp.dot(left, right, preferred_element_type=jnp.float32)


def across(left, right):
    return lax.dot_general(
        left, right, (((1,), (1,)), ((), ())), preferred_element_type=jnp.float32
    )


def contract_rows(left, right):
    return lax.dot_general(
        left, right, (((0,), (0,)), ((), ())), preferred_element_type=jnp.float32
    )


def split_heads(joint):
    row_count = joint.shape[0]
    queries = joint[:, :D].reshape(row_count, -1, HEAD_DIM)
    keys = joint[:, D : 2 * D].reshape(row_count, -1, HEAD_DIM)
    values = joint[:, 2 * D :].reshape(row_count, -1, HEAD_DIM)
    return (queries, keys, values)


def masked_scores(queries, keys, allowed):
    scores = jnp.einsum(
        "qhd,khd->hqk", queries, keys, preferred_element_type=jnp.float32
    ) * HEAD_DIM ** (-0.5)
    return jnp.where(allowed[None], scores, NEG_SCORE)


def attention_forward(joint, allowed):
    queries, keys, values = split_heads(joint)
    masked = masked_scores(queries, keys, allowed)
    peak = jnp.max(masked, axis=-1, keepdims=True)
    raised = jnp.exp(masked - peak)
    denom = jnp.sum(raised, axis=-1, keepdims=True)
    probs = raised / denom
    logsum = peak + jnp.log(denom)
    context = jnp.einsum(
        "hqk,khd->qhd", probs.astype(jnp.bfloat16), values, preferred_element_type=jnp.float32
    )
    return (context.reshape(joint.shape[0], D).astype(jnp.bfloat16), logsum)


def attention_backward(joint, allowed, logsum, context_grad):
    row_count = joint.shape[0]
    queries, keys, values = split_heads(joint)
    probs = jnp.exp(masked_scores(queries, keys, allowed) - logsum)
    probs_low = probs.astype(jnp.bfloat16)
    incoming = context_grad.reshape(row_count, -1, HEAD_DIM)
    value_grad = jnp.einsum("hqk,qhd->khd", probs_low, incoming, preferred_element_type=jnp.float32)
    prob_grad = jnp.einsum("qhd,khd->hqk", incoming, values, preferred_element_type=jnp.float32)
    score_grad = (probs * (prob_grad - jnp.sum(probs * prob_grad, axis=-1, keepdims=True))).astype(
        jnp.bfloat16
    )
    query_grad = jnp.einsum(
        "hqk,khd->qhd", score_grad, keys, preferred_element_type=jnp.float32
    ) * HEAD_DIM ** (-0.5)
    key_grad = jnp.einsum(
        "hqk,qhd->khd", score_grad, queries, preferred_element_type=jnp.float32
    ) * HEAD_DIM ** (-0.5)
    return jnp.concatenate(
        [
            query_grad.reshape(row_count, D),
            key_grad.reshape(row_count, D),
            value_grad.reshape(row_count, D),
        ],
        axis=1,
    ).astype(jnp.bfloat16)

AXES = ("dp", "fsdp")
GROUP = 4
CHUNK = 3456
NARROW = 8


def low(values):
    return values.astype(jnp.bfloat16)


def wide(values):
    return values.astype(jnp.float32)


def device_total():
    return lax.axis_size("dp") * lax.axis_size("fsdp")


def device_index():
    return lax.axis_index("dp") * lax.axis_size("fsdp") + lax.axis_index("fsdp")


def swap(values, mask):
    return lax.ppermute(values, AXES, [(i, i ^ mask) for i in range(device_total())])


def same_quarter():
    return [[d for d in range(lax.axis_size("dp")) if d % 2 == odd] for odd in range(2)]


def pick(blocks, index):
    return lax.dynamic_index_in_dim(blocks, index, 0, keepdims=False)


def group_exchange(blocks, quarter):
    return [pick(blocks, quarter)] + [swap(pick(blocks, quarter ^ m), m) for m in range(1, GROUP)]


def group_gather(values):
    pair = jnp.stack([values, swap(values, 2)])
    other = swap(pair, 1)
    return jnp.stack([pair[0], other[0], pair[1], other[1]])


def group_scatter(parts):
    mine = jnp.stack([parts[0], parts[2]])
    theirs = low(jnp.stack([parts[1], parts[3]]))
    summed = wide(mine) + wide(swap(theirs, 1))
    return summed[0] + wide(swap(low(summed[1]), 2))


def by_quarter(pieces, quarter):
    stacked = jnp.stack(pieces)
    return [pick(stacked, quarter ^ j) for j in range(GROUP)]


def gene_chunks(values):
    padded = jnp.pad(values, ((0, 0), (0, GROUP * CHUNK - GENES)))
    return jnp.stack([padded[:, j * CHUNK : (j + 1) * CHUNK] for j in range(GROUP)])


def sum_all(values):
    mask = 1
    while mask < device_total():
        values = values + swap(values, mask)
        mask *= 2
    return values


MESH = pl.DeviceIdType.MESH


class Where:
    def __init__(self, total):
        dp = lax.axis_index("dp")
        self.total = total
        self.core = lax.axis_index("fsdp")
        self.x = dp % 2
        self.t = dp // 2
        self.quarter = 2 * self.x + self.core
        y, z = self.t % 2, self.t // 2
        self.k = z + y * (total - 1 - 2 * z)
        self.right = (2 * self.owner(-1) + self.x, self.core)
        self.left = (2 * self.owner(1) + self.x, self.core)
        self.peers = [
            None,
            (dp, 1 - self.core),
            (2 * self.t + 1 - self.x, self.core),
            (2 * self.t + 1 - self.x, 1 - self.core),
        ]
        self.quarters = [
            self.quarter,
            2 * self.x + 1 - self.core,
            2 * (1 - self.x) + self.core,
            2 * (1 - self.x) + 1 - self.core,
        ]

    def owner(self, step):
        place = (self.k - step + self.total) % self.total
        y = place // (self.total // 2)
        return 2 * (place + y * (self.total - 1 - 2 * place)) + y

    def same(self, step):
        t = (self.t + step) % self.total
        return t, (2 * t + self.x, self.core)

    def meet(self, everyone=False):
        barrier = pltpu.get_barrier_semaphore()
        others = self.peers[1:]
        if everyone:
            others = others + [self.same(step)[1] for step in range(1, self.total)]
        else:
            others = others + [self.right, self.left]
        for other in others:
            pl.semaphore_signal(barrier, inc=1, device_id=other, device_id_type=MESH)
        pl.semaphore_wait(barrier, len(others))


class Copies:
    def __init__(self, send_sems, recv_sems, local_sems):
        self.send_sems, self.recv_sems, self.local_sems = send_sems, recv_sems, local_sems
        self.remote_count = self.local_count = 0
        self.sent = []

    def send(self, source, target, device):
        at = self.remote_count
        self.remote_count += 1
        copy = pltpu.make_async_remote_copy(
            source,
            target,
            self.send_sems.at[at],
            self.recv_sems.at[at],
            device_id=device,
            device_id_type=MESH,
        )
        copy.start()
        self.sent.append(copy)
        return copy

    def local(self, source, target):
        at = self.local_count
        self.local_count += 1
        copy = pltpu.make_async_copy(source, target, self.local_sems.at[at])
        copy.start()
        return copy

    def finish(self):
        for copy in self.sent:
            copy.wait_send()


def gather_kernel(total, *refs):
    (cells, embed, decoder, joint, small, output, encoder, up, down) = refs[:9]
    (cells_all, embed_all, decoder_all, joint_all, small_all) = refs[9:14]
    (output_all, encoder_all, up_all, down_all, embedded) = refs[14:19]
    (held_cells, held_embed, partial, other_core, for_x, other_x) = refs[19:25]
    here = Where(total)
    copies = Copies(*refs[25:])
    here.meet()
    t, x, core = here.t, here.x, here.core
    last = total - 1
    towards = {1: here.right, -1: here.left}
    flying = {}

    late = [(up, up_all, 1), (output, output_all, 1), (down, down_all, -1), (encoder, encoder_all, -1)]
    shares = {
        name: [
            copies.send(own.at[here.quarters[m]], full.at[t, here.quarter], here.peers[m])
            for m in (2, 3, 1)
        ]
        for name, own, full in (("embed", embed, embed_all), ("decoder", decoder, decoder_all))
    }
    for n, (own, full, way) in enumerate(late):
        flying["late", n] = copies.send(own, full.at[t, x, core], towards[way])
    across_x = [copies.send(own, full.at[t, x, core], here.peers[2]) for own, full, _ in late]
    own_cells = copies.local(cells.at[here.quarter], cells_all.at[0])
    cell_moves = [
        copies.send(cells.at[here.quarters[m]], cells_all.at[m], here.peers[m]) for m in (2, 3, 1)
    ]
    shares["early"] = [
        copies.send(own, full.at[t, x, core], here.peers[2])
        for own, full in ((joint, joint_all), (small, small_all))
    ]
    own_copies = {
        "embed": [copies.local(embed.at[here.quarter], embed_all.at[t, here.quarter])],
        "decoder": [copies.local(decoder.at[here.quarter], decoder_all.at[t, here.quarter])],
        "early": [
            copies.local(own, full.at[t, x, core])
            for own, full in ((joint, joint_all), (small, small_all))
        ],
    }
    own_late = [copies.local(own, full.at[t, x, core]) for own, full, _ in late]

    def late_step(s):
        for n, (_, full, way) in enumerate(late):
            flying["late", n].wait_recv()
            block = full.at[here.owner(way * s), x, core]
            if s < last:
                flying["late", n] = copies.send(block, block, towards[way])
            across_x.append(copies.send(block, block, here.peers[2]))

    def early_block(full, way, s):
        return full.at[here.owner(way * s), 0 if way == 1 else 1, core]

    def table_block(full, way, s):
        return full.at[here.owner(way * s), pl.ds(0 if way == 1 else 2, 2)]

    rings = {
        "embed": [(embed_all, way, table_block) for way in (1, -1)],
        "decoder": [(decoder_all, way, table_block) for way in (1, -1)],
        "early": [(full, way, early_block) for full in (joint_all, small_all) for way in (1, -1)],
    }

    def step(name, s):
        if s == 0:
            for copy in own_copies[name]:
                copy.wait()
            for copy in shares[name]:
                copy.wait_recv()
        for n, (full, way, block_of) in enumerate(rings[name]):
            if s > 0:
                flying[name, n].wait_recv()
            if s < last:
                block = block_of(full, way, s)
                flying[name, n] = copies.send(block, block, towards[way])

    holds = {}

    def hold(block):
        holds[block] = copies.local(embed_all.at[block], held_embed.at[block % 2])

    def multiply(block):
        holds[block].wait()
        features = held_embed.shape[1] * held_embed.shape[2]
        table = held_embed[block % 2].reshape(features, held_embed.shape[3])
        for row in range(2):
            for column in range(2):
                partial[row, column, :, pl.ds(block * features, features)] = low(
                    across(held_cells[2 * row + column], table)
                )
        if block + 2 < total:
            hold(block + 2)

    across_core = []
    step("embed", 0)
    for s in range(1, last + 1):
        late_step(s)
        step("embed", s)
        if s == last - 1:
            step("early", 0)
            step("decoder", 0)
    hold(0)
    hold(1)
    for copy in cell_moves:
        copy.wait_recv()
    own_cells.wait()
    held = copies.local(cells_all, held_cells)
    step("early", 1)
    step("decoder", 1)
    held.wait()
    for s in range(2, last + 1):
        multiply(s - 2)
        step("early", s)
        step("decoder", s)
    for block in range(last - 1, total):
        multiply(block)
    sums = copies.send(partial.at[:, 1], other_core, here.peers[1])
    for copy in own_late:
        copy.wait()
    for full in (joint_all, small_all):
        block = full.at[:, :, core]
        across_core.append(copies.send(block, block, here.peers[1]))
    sums.wait_recv()
    for_x[...] = low(wide(partial[1, 0]) + wide(other_core[1]))
    sums = copies.send(for_x, other_x, here.peers[2])
    for copy in across_x:
        copy.wait_recv()
    for _, full, _ in late:
        block = full.at[:, :, core]
        across_core.append(copies.send(block, block, here.peers[1]))
    sums.wait_recv()
    embedded[...] = wide(partial[0, 0]) + wide(other_core[0]) + wide(other_x[...])
    for copy in across_core:
        copy.wait_recv()
    copies.finish()


def gather_weights(cells, embed, decoder, joint, small, output, encoder, up, down):
    total = device_total() // GROUP
    own = [joint, small, output, encoder, up, down]
    tables = [embed, decoder]
    operands = [cells] + tables + own
    shapes = (
        [cells.shape]
        + [(total,) + v.shape for v in tables]
        + [(total, 2, 2) + v.shape for v in own]
    )
    remote = 15 + 12 * (total - 1) + 4 * total + 8
    cell_rows, genes = cells.shape[1:]
    features = total * GROUP * embed.shape[1]
    buffers = [
        cells.shape,
        (2,) + embed.shape,
        (2, 2, cell_rows, features),
        (2, cell_rows, features),
        (cell_rows, features),
        (cell_rows, features),
    ]
    return pl.pallas_call(
        functools.partial(gather_kernel, total),
        out_shape=[jax.ShapeDtypeStruct(s, jnp.bfloat16) for s in shapes]
        + [jax.ShapeDtypeStruct((cell_rows, features), jnp.float32)],
        in_specs=[pl.BlockSpec(memory_space=pl.ANY)] * len(operands),
        out_specs=[pl.BlockSpec(memory_space=pl.ANY)] * len(operands)
        + [pl.BlockSpec(memory_space=pltpu.VMEM)],
        scratch_shapes=[pltpu.VMEM(shape, jnp.bfloat16) for shape in buffers]
        + [
            pltpu.SemaphoreType.DMA((remote,)),
            pltpu.SemaphoreType.DMA((remote,)),
            pltpu.SemaphoreType.DMA((10 + total,)),
        ],
        compiler_params=pltpu.CompilerParams(
            collective_id=1, has_side_effects=True, vmem_limit_bytes=32 * 2**20
        ),
        name="gather_weights",
    )(*operands)


def add_rows(target, first, second, dtype):
    rows, columns = target.shape
    step = min(rows, 16 if columns > 2048 else 32)

    @pl.loop(0, rows // step)
    def _(i):
        part = pl.ds(pl.multiple_of(i * step, step), step)
        target[part, :] = (wide(first[part, :]) + wide(second[part, :])).astype(dtype)


def scatter_kernel(total, *refs):
    (small, recon, *refs) = refs
    (embed, decoder, joint, output, encoder, up, down, cells) = refs[:8]
    (embed_out, decoder_out, cells_out) = refs[8:11]
    (joint_out, output_out, encoder_out, up_out, down_out, small_out, recon_out) = refs[11:18]
    (chip_small, stage_small, sum_small, hop_small, group_recon, all_recon) = refs[18:24]
    refs = refs[24:]
    (chip_joint, chip_output, chip_encoder, chip_up, chip_down) = refs[:5]
    (stage_up, stage_down) = refs[5:7]
    (sum_output, sum_encoder, sum_up, sum_down) = refs[7:11]
    (hop_embed, hop_decoder, hop_joint) = refs[11:14]
    (hop_output, hop_encoder, hop_up, hop_down) = refs[14:18]
    (local_embed, local_decoder) = refs[18:20]
    (last_embed, last_decoder, last_joint, other_joint) = refs[20:24]
    here = Where(total)
    copies = Copies(*refs[24:])
    here.meet()
    x, core, last = here.x, here.core, total - 1
    towards = {1: here.right, -1: here.left}
    flying = {}

    tables = []
    for term, hops, local, result in (
        (embed, hop_embed, local_embed, last_embed),
        (decoder, hop_decoder, local_decoder, last_decoder),
    ):
        for way in (1, -1):
            tables.append((term, hops, local, result, way, 0 if way == 1 else 1))

    def table_block(term, way, side, h):
        return term.at[here.owner(way * h), pl.ds(2 * side, 2)]

    def fetch(n, h):
        term, _, local, _, way, side = tables[n]
        flying["local", n, h] = copies.local(
            table_block(term, way, side, h + 1), local.at[h % 2, side]
        )

    for n, (term, hops, _, _, way, side) in enumerate(tables):
        flying["table", n] = copies.send(
            table_block(term, way, side, 1), hops.at[0, side], towards[way]
        )
    halves = {}
    for name, term, chip in (
        ("up", up, chip_up),
        ("down", down, chip_down),
        ("output", output, chip_output),
        ("encoder", encoder, chip_encoder),
        ("joint", joint, chip_joint),
        ("small", small, chip_small),
    ):
        halves[name] = copies.send(term.at[:, :, 1 - core], chip, here.peers[1])
    group_recon[here.quarter] = recon[...]
    recons = [copies.send(recon, group_recon.at[here.quarter], here.peers[m]) for m in (2, 3, 1)]
    loads = {
        "small": copies.local(small.at[:, :, core], stage_small),
        "up": copies.local(up.at[:, :, core], stage_up),
        "down": copies.local(down.at[:, :, core], stage_down),
    }
    for h in (1, 2):
        for n in range(len(tables)):
            fetch(n, h)

    def table_hop(h):
        for n, (term, hops, local, result, way, side) in enumerate(tables):
            flying["table", n].wait_recv()
            flying["local", n, h].wait()
            for row in range(2):
                arrived = hops.at[h - 1, side, row]
                target = arrived if h < last else result.at[2 * side + row]
                add_rows(target, arrived, local.at[h % 2, side, row], jnp.bfloat16)
            if h < last:
                flying["table", n] = copies.send(
                    hops.at[h - 1, side], hops.at[h, side], towards[way]
                )
            if h + 2 <= last:
                fetch(n, h + 2)

    def chip_sum(name, chip, staged):
        halves[name].wait_recv()
        loads[name].wait()

        @pl.loop(0, total)
        def _(t):
            for side in range(2):
                add_rows(chip.at[t, side], chip.at[t, side], staged.at[t, side], chip.dtype)

    across = {}

    def cross(name, chip, sums):
        across[name] = copies.send(chip.at[:, 1 - x], sums, here.peers[2])

    chip_sum("up", chip_up, stage_up)
    cross("up", chip_up, sum_up)
    staged_joint = stage_up.at[:, :, :, pl.ds(0, joint.shape[-1])]
    loads["joint"] = copies.local(joint.at[:, :, core], staged_joint)
    chip_sum("down", chip_down, stage_down)
    cross("down", chip_down, sum_down)
    slim = output.shape[3]
    staged_output = stage_down.at[:, :, pl.ds(0, slim)]
    staged_encoder = stage_down.at[:, :, pl.ds(slim, slim)]
    loads["output"] = copies.local(output.at[:, :, core], staged_output)
    loads["encoder"] = copies.local(encoder.at[:, :, core], staged_encoder)
    table_hop(1)
    chip_sum("joint", chip_joint, staged_joint)
    for side, way in ((0, 1), (1, -1)):
        flying["joint", side] = copies.send(
            chip_joint.at[here.owner(way), side], hop_joint.at[0, side], towards[way]
        )
    chip_sum("output", chip_output, staged_output)
    cross("output", chip_output, sum_output)
    chip_sum("encoder", chip_encoder, staged_encoder)
    cross("encoder", chip_encoder, sum_encoder)
    chip_sum("small", chip_small, stage_small)
    cross("small", chip_small, sum_small)
    for copy in recons:
        copy.wait_recv()
    all_recon[here.t] = group_recon[0] + group_recon[1] + group_recon[2] + group_recon[3]
    own_recon = all_recon.at[here.t]
    flying["recon"] = copies.send(own_recon, own_recon, here.right)
    moves = [copies.send(cells.at[m], cells_out.at[here.quarter], here.peers[m]) for m in (2, 3, 1)]
    own = [copies.local(cells.at[0], cells_out.at[here.quarter])]

    def recon_hop(h):
        flying["recon"].wait_recv()
        if h < last:
            arrived = all_recon.at[here.owner(h)]
            flying["recon"] = copies.send(arrived, arrived, here.right)

    def joint_hop(h):
        for side, way in ((0, 1), (1, -1)):
            flying["joint", side].wait_recv()
            arrived = hop_joint.at[h - 1, side]
            target = arrived if h < last else last_joint.at[side]
            local = chip_joint.at[here.owner(way * (h + 1)), side]
            add_rows(target, arrived, local, jnp.bfloat16)
            if h < last:
                flying["joint", side] = copies.send(arrived, hop_joint.at[h, side], towards[way])

    late = [
        ("up", sum_up, chip_up, hop_up, up_out, 1),
        ("down", sum_down, chip_down, hop_down, down_out, -1),
        ("output", sum_output, chip_output, hop_output, output_out, 1),
        ("encoder", sum_encoder, chip_encoder, hop_encoder, encoder_out, -1),
        ("small", sum_small, chip_small, hop_small, small_out, 1),
    ]

    def late_start():
        for name, sums, chip, hops, _, way in late:
            across[name].wait_recv()

            @pl.loop(0, total)
            def _(t):
                add_rows(sums.at[t], sums.at[t], chip.at[t, x], sums.dtype)

            flying["late", name] = copies.send(sums.at[here.owner(way)], hops.at[0], towards[way])

    def late_hop(h):
        for name, sums, _, hops, result, way in late:
            flying["late", name].wait_recv()
            local = sums.at[here.owner(way * (h + 1))]
            if h < last:
                add_rows(hops.at[h - 1], hops.at[h - 1], local, hops.dtype)
                flying["late", name] = copies.send(hops.at[h - 1], hops.at[h], towards[way])
            else:
                add_rows(result, hops.at[h - 1], local, jnp.float32)

    joint_hop(1)
    for h in range(2, last + 1):
        table_hop(h)
        joint_hop(h)
    for result, out in ((last_embed, embed_out), (last_decoder, decoder_out)):
        for m in (2, 3, 1):
            moves.append(
                copies.send(
                    result.at[here.quarters[m]], out.at[here.quarter], here.peers[m]
                )
            )
        own.append(copies.local(result.at[here.quarter], out.at[here.quarter]))
    joint_move = copies.send(last_joint.at[1 - x], other_joint, here.peers[2])
    late_start()
    for h in range(1, last + 1):
        late_hop(h)
        recon_hop(h)
    summed = all_recon[0]
    for t in range(1, total):
        summed = summed + all_recon[t]
    recon_out[...] = summed
    joint_move.wait_recv()
    add_rows(joint_out, last_joint.at[x], other_joint, jnp.float32)
    for copy in moves:
        copy.wait_recv()
    for copy in own:
        copy.wait()
    copies.finish()


def scatter_sums(embed, decoder, joint, output, encoder, up, down, small, recon, cells):
    total = device_total() // GROUP
    last = total - 1
    operands = [small, recon, embed, decoder, joint, output, encoder, up, down, cells]
    middle = [joint, output, encoder, up, down]
    thin = jnp.bfloat16
    out_shape = [jax.ShapeDtypeStruct(v.shape[1:], thin) for v in (embed, decoder)]
    out_shape += [jax.ShapeDtypeStruct(cells.shape, thin)]
    out_shape += [jax.ShapeDtypeStruct(v.shape[3:], jnp.float32) for v in middle]
    out_shape += [jax.ShapeDtypeStruct(v, jnp.float32) for v in (small.shape[3:], recon.shape)]
    block = small.shape[3:]
    exact = [(total, 2) + block, (total, 2) + block, (total,) + block, (last,) + block]
    exact += [(GROUP,) + recon.shape, (total,) + recon.shape]
    chips = [(total, 2) + v.shape[3:] for v in middle]
    sums = [(total,) + v.shape[3:] for v in middle[1:]]
    hops = [(last, 2, 2) + v.shape[2:] for v in (embed, decoder)]
    hops += [(last, 2) + joint.shape[3:]] + [(last,) + v.shape[3:] for v in middle[1:]]
    local = [(2, 2, 2) + v.shape[2:] for v in (embed, decoder)]
    results = [v.shape[1:] for v in (embed, decoder)] + [(2,) + joint.shape[3:], joint.shape[3:]]
    buffers = chips + [chips[3], chips[4]] + sums + hops + local + results
    remote, here = 12 + 6 * last + 4 * last + 7 + 5 + 2 * last, 4 * last + 9
    return pl.pallas_call(
        functools.partial(scatter_kernel, total),
        out_shape=out_shape,
        in_specs=[pl.BlockSpec(memory_space=pl.ANY), pl.BlockSpec(memory_space=pltpu.VMEM)]
        + [pl.BlockSpec(memory_space=pl.ANY)] * (len(operands) - 2),
        out_specs=[pl.BlockSpec(memory_space=pl.ANY)] * 3
        + [pl.BlockSpec(memory_space=pltpu.VMEM)] * 7,
        scratch_shapes=[pltpu.VMEM(shape, jnp.float32) for shape in exact]
        + [pltpu.VMEM(shape, thin) for shape in buffers]
        + [
            pltpu.SemaphoreType.DMA((remote,)),
            pltpu.SemaphoreType.DMA((remote,)),
            pltpu.SemaphoreType.DMA((here,)),
        ],
        compiler_params=pltpu.CompilerParams(
            collective_id=2, has_side_effects=True, vmem_limit_bytes=60 * 2**20
        ),
        name="scatter_sums",
    )(*operands)


def scatter_plain(embed, decoder, joint, output, encoder, up, down, small, recon, cells):
    quarter = device_index() % GROUP

    def sent(blocks):
        pieces = [pick(blocks, 0)] + [swap(blocks[m], m) for m in range(1, GROUP)]
        return jnp.stack(by_quarter(pieces, quarter))

    def table(term):
        block = lax.psum_scatter(
            term, "dp", axis_index_groups=same_quarter(), scatter_dimension=0, tiled=False
        )
        return sent(jnp.stack(by_quarter(list(block), quarter)))

    def middle(term):
        rows = term.reshape((device_total(),) + term.shape[3:])
        return wide(lax.psum_scatter(rows, AXES, scatter_dimension=0, tiled=False))

    return [table(embed), table(decoder), sent(cells)] + [
        middle(v) for v in (joint, output, encoder, up, down, small)
    ] + [sum_all(recon)]


SLICE = 384


def latent_kernel(total, *refs):
    (message, spread, ratio, decoder, cells) = refs[:5]
    (recon_grad, decoder_term, latent_grad, spread_sum, recon_sum) = refs[5:10]
    (latents, held_decoder, held_cells, held_grad, held_term, turned, partial) = refs[10:17]
    (leaving, arriving, group_spread, all_spread) = refs[17:21]
    here = Where(total)
    copies = Copies(*refs[21:])
    here.meet(everyone=True)
    moves = [copies.send(message, latents.at[m], here.peers[m]) for m in (2, 3, 1)]
    spreads = [copies.send(spread, group_spread.at[here.quarter], here.peers[m]) for m in (2, 3, 1)]
    loads = [
        copies.local(message, latents.at[0]),
        copies.local(decoder, held_decoder),
        copies.local(cells, held_cells),
    ]
    group_spread[here.quarter] = spread[...]
    for copy in spreads:
        copy.wait_recv()
    all_spread[here.t] = (
        group_spread[0] + group_spread[1] + group_spread[2] + group_spread[3]
    )
    spreads = []
    for away in range(1, total):
        own = all_spread.at[here.t]
        spreads.append(copies.send(own, own, here.same(away)[1]))
    for copy in loads:
        copy.wait()
    for copy in moves:
        copy.wait_recv()
    rows = message.shape[0]
    size = held_decoder.shape[0]
    for m in range(GROUP):
        turned[:, m * rows : (m + 1) * rows] = low(wide(latents[m, :, :size]).T)
    partial[...] = jnp.zeros_like(partial)
    recon_sum[...] = jnp.zeros_like(recon_sum)

    @pl.loop(0, CHUNK // SLICE)
    def _(i):
        part = pl.ds(pl.multiple_of(i * SLICE, 128), SLICE)
        table = held_decoder[:, part]
        for m in range(GROUP):
            live = wide(latents[m, :, size : size + 128])
            live = jnp.concatenate([live] * (SLICE // 128), axis=1)
            miss = matmul(latents[m, :, :size], table) - wide(held_cells[m, :, part])
            weighted = live * miss
            recon_sum[...] += jnp.sum((weighted * miss).reshape(rows // 8, 8, SLICE), axis=0)
            grad = low(ratio[0, 0] * weighted)
            held_grad[m, :, part] = grad
            partial[m] += across(grad, table)
        held_term[:, part] = low(matmul(turned[...], held_grad[:, :, part].reshape(GROUP * rows, SLICE)))

    leaving[...] = low(partial[...])
    moves = [copies.send(leaving.at[m], arriving.at[m - 1], here.peers[m]) for m in (2, 3, 1)]
    stores = [copies.local(held_grad, recon_grad), copies.local(held_term, decoder_term)]
    for copy in spreads:
        copy.wait_recv()
    summed = all_spread[0]
    for t in range(1, total):
        summed = summed + all_spread[t]
    spread_sum[...] = summed
    for copy in moves:
        copy.wait_recv()
    latent_grad[...] = (
        (partial[0] + wide(arriving[0])) + (wide(arriving[1]) + wide(arriving[2]))
    )
    for copy in stores:
        copy.wait()
    copies.finish()


def latent_step(message, spread, ratio, decoder, cells):
    total = device_total() // GROUP
    rows, size = message.shape[0], decoder.shape[0]
    thin = jnp.bfloat16
    vmem = pl.BlockSpec(memory_space=pltpu.VMEM)
    anywhere = pl.BlockSpec(memory_space=pl.ANY)
    remote = 9 + total - 1
    return pl.pallas_call(
        functools.partial(latent_kernel, total),
        out_shape=[
            jax.ShapeDtypeStruct(cells.shape, thin),
            jax.ShapeDtypeStruct(decoder.shape, thin),
            jax.ShapeDtypeStruct((rows, size), jnp.float32),
            jax.ShapeDtypeStruct(spread.shape, jnp.float32),
            jax.ShapeDtypeStruct((8, SLICE), jnp.float32),
        ],
        in_specs=[vmem, vmem, pl.BlockSpec(memory_space=pltpu.SMEM), anywhere, anywhere],
        out_specs=[anywhere, anywhere, vmem, vmem, vmem],
        scratch_shapes=[
            pltpu.VMEM((GROUP,) + message.shape, thin),
            pltpu.VMEM(decoder.shape, thin),
            pltpu.VMEM(cells.shape, thin),
            pltpu.VMEM(cells.shape, thin),
            pltpu.VMEM(decoder.shape, thin),
            pltpu.VMEM((size, GROUP * rows), thin),
            pltpu.VMEM((GROUP, rows, size), jnp.float32),
            pltpu.VMEM((GROUP, rows, size), thin),
            pltpu.VMEM((GROUP - 1, rows, size), thin),
            pltpu.VMEM((GROUP,) + spread.shape, jnp.float32),
            pltpu.VMEM((total,) + spread.shape, jnp.float32),
            pltpu.SemaphoreType.DMA((remote,)),
            pltpu.SemaphoreType.DMA((remote,)),
            pltpu.SemaphoreType.DMA((5,)),
        ],
        compiler_params=pltpu.CompilerParams(
            collective_id=3, has_side_effects=True, vmem_limit_bytes=40 * 2**20
        ),
        name="latent_step",
    )(message, spread, ratio, decoder, cells)


def latent_plain(message, spread, ratio, decoder, cells):
    size = decoder.shape[0]
    gathered = group_gather(message).reshape(-1, message.shape[1])
    latents, live = gathered[:, :size], wide(gathered[:, size : size + 1])
    miss = matmul(latents, decoder) - wide(cells.reshape(-1, CHUNK))
    grad = low(ratio[0, 0] * live * miss)
    recon_sum = jnp.sum((live * miss * miss).reshape(-1, 8, CHUNK), axis=0)
    latent_grad = group_scatter(low(across(grad, decoder)).reshape(GROUP, -1, size))
    term = low(contract_rows(latents, grad))
    return grad.reshape(cells.shape), term, latent_grad, sum_all(spread), recon_sum


def gather_plain(cells, embed, decoder, *own):
    quarter = device_index() % GROUP
    total = device_total() // GROUP
    groups = same_quarter()

    def table(values):
        block = jnp.stack(by_quarter(group_exchange(values, quarter), quarter))
        return lax.all_gather(block, "dp", axis_index_groups=groups, axis=0, tiled=False)

    cells_all = jnp.stack(group_exchange(cells, quarter))
    embed_all = table(embed)
    rows, genes = cells.shape[1:]
    embedded = low(across(cells_all.reshape(-1, genes), embed_all.reshape(-1, genes)))
    embedded = group_scatter(embedded.reshape(GROUP, rows, -1))
    middle = [lax.all_gather(v, AXES, axis=0, tiled=False) for v in own]
    return [cells_all, embed_all, table(decoder)] + middle + [embedded]


def shards(
    cells,
    coordinates,
    slide_ids,
    live_mask,
    components,
    noise,
    ramp_weight,
    embed_weight,
    query_key_value,
    output_weight,
    up_weight,
    up_bias,
    down_weight,
    down_bias,
    first_gain,
    first_shift,
    second_gain,
    second_shift,
    encoder_weight,
    encoder_bias,
    prior_mean,
    prior_logvar,
    decoder_weight,
):
    row_count = cells.shape[0]
    devices = device_total()
    total = devices // GROUP
    me = device_index()
    quarter = me % GROUP
    rows = embed_weight.shape[0]
    thin = decoder_weight.shape[0]
    cell_total = row_count * devices
    live = live_mask[0].astype(jnp.float32)
    slides = slide_ids[0]
    places = jnp.arange(row_count)
    allowed = (slides[:, None] == slides[None, :]) & (
        (live[None, :] > 0.5) | (places[:, None] == places[None, :])
    )
    onehot = (
        components[:, None] == jnp.arange(prior_mean.shape[0], dtype=jnp.int32)[None, :]
    ).astype(jnp.float32)

    small = jnp.concatenate(
        [
            up_bias.reshape(rows, 4),
            down_bias.reshape(rows, 1),
            first_gain.reshape(rows, 1),
            first_shift.reshape(rows, 1),
            second_gain.reshape(rows, 1),
            second_shift.reshape(rows, 1),
            encoder_bias.reshape(rows, 1),
            jnp.concatenate([prior_mean, prior_logvar]).reshape(rows, 16),
            jnp.full((rows, 1), jnp.sum(live), jnp.bfloat16),
        ],
        axis=1,
    )
    small_columns = small.shape[1]
    small = jnp.pad(small, ((0, 0), (0, 128 - small_columns)))
    gather = gather_weights if total <= NARROW else gather_plain
    cells_group, embed_cols, decoder_cols, *middle, embedded = gather(
        gene_chunks(cells),
        gene_chunks(embed_weight),
        gene_chunks(decoder_weight),
        query_key_value,
        small,
        output_weight,
        encoder_weight,
        up_weight,
        down_weight,
    )
    cells_rows = cells_group.reshape(GROUP * row_count, CHUNK)
    embed_cols = embed_cols.reshape(-1, CHUNK)
    decoder_cols = decoder_cols.reshape(-1, CHUNK)
    middle = [full.reshape(-1, full.shape[-1]) for full in middle]
    joint_full, small_full, output_full, encoder_full, up_full, down_full = middle
    small_full = wide(small_full)
    up_bias_full = small_full[:, 0:4].reshape(-1)
    down_bias_full = small_full[:, 4]
    gain_first = small_full[:, 5]
    shift_first = small_full[:, 6]
    gain_second = small_full[:, 7]
    shift_second = small_full[:, 8]
    encoder_bias_full = small_full[:, 9]
    kinds = prior_mean.shape[0]

    prior_full = small_full[:, 10:26].reshape(devices, 2 * kinds, -1)
    prior_full = prior_full.transpose(1, 0, 2).reshape(2 * kinds, LATENT)
    prior_mean_full, prior_logvar_full = prior_full[:kinds], prior_full[kinds:]
    count = jnp.sum(small_full.reshape(devices, rows, 128)[:, 0, 26])

    start_state = embedded + positions(coordinates)
    normed_first = layer_norm(start_state, gain_first, shift_first).astype(jnp.bfloat16)
    joint = matmul(normed_first, joint_full).astype(jnp.bfloat16)
    context, logsum = attention_forward(joint, allowed)
    middle_state = start_state + matmul(context, output_full)
    normed_second = layer_norm(middle_state, gain_second, shift_second).astype(jnp.bfloat16)
    pre = matmul(normed_second, up_full) + up_bias_full
    active = jax.nn.gelu(pre, approximate=True).astype(jnp.bfloat16)
    end_state = middle_state + (matmul(active, down_full) + down_bias_full)
    end_low = end_state.astype(jnp.bfloat16)
    encoded = matmul(end_low, encoder_full) + encoder_bias_full
    latent_mean = encoded[:, :LATENT]
    latent_logvar = encoded[:, LATENT:]
    latent = (latent_mean + jnp.exp(0.5 * latent_logvar) * noise).astype(jnp.bfloat16)
    center = jnp.dot(onehot, prior_mean_full, precision=lax.Precision.HIGHEST)
    scale = jnp.dot(onehot, prior_logvar_full, precision=lax.Precision.HIGHEST)
    gap = latent_mean - center
    inverse = jnp.exp(-scale)
    grown = jnp.exp(latent_logvar)
    diverge = 0.5 * (scale - latent_logvar + (grown + gap * gap) * inverse - 1.0)
    ratio = cell_total / count
    spread = jnp.broadcast_to(jnp.sum(live[:, None] * diverge, axis=0, keepdims=True), (8, LATENT))
    message = jnp.concatenate(
        [latent, jnp.broadcast_to(low(live)[:, None], (row_count, 128))], axis=1
    )
    latent_pass = latent_step if total <= NARROW else latent_plain
    recon_grad, decoder_term, latent_grad, spread_sum, recon_sum = latent_pass(
        message, spread, ratio.reshape(1, 1), decoder_cols, cells_group
    )
    kl_mean = spread_sum[0] / count
    shifted = (kl_mean - FREE_FLOOR) / FREE_TEMP
    free = FREE_FLOOR + FREE_TEMP * jax.nn.softplus(shifted)
    latent_grad = wide(low(latent_grad))

    kl_scale = ratio * ramp_weight * jax.nn.sigmoid(shifted)[None, :] * live[:, None]
    pulled = kl_scale * gap * inverse
    mean_grad = latent_grad + pulled
    logvar_grad = latent_grad * 0.5 * jnp.exp(0.5 * latent_logvar) * noise + kl_scale * 0.5 * (
        grown * inverse - 1.0
    )
    encoded_grad = jnp.concatenate([mean_grad, logvar_grad], axis=1).astype(jnp.bfloat16)
    prior_mean_grad = jnp.dot(onehot.T, -pulled, precision=lax.Precision.HIGHEST)
    prior_logvar_grad = jnp.dot(
        onehot.T,
        kl_scale * 0.5 * (1.0 - (grown + gap * gap) * inverse),
        precision=lax.Precision.HIGHEST,
    )
    end_grad = across(encoded_grad, encoder_full)
    branch_grad = end_grad.astype(jnp.bfloat16)
    encoder_term = low(contract_rows(end_low, encoded_grad))
    encoder_bias_grad = jnp.sum(encoded_grad.astype(jnp.float32), axis=0)
    down_term = low(contract_rows(active, branch_grad))
    down_bias_grad = jnp.sum(branch_grad.astype(jnp.float32), axis=0)
    active_grad = across(branch_grad, down_full)
    gelu_value, gelu_back = jax.vjp(lambda value: jax.nn.gelu(value, approximate=True), pre)
    pre_grad = gelu_back(active_grad)[0].astype(jnp.bfloat16)
    up_term = low(contract_rows(normed_second, pre_grad))
    up_bias_grad = jnp.sum(pre_grad.astype(jnp.float32), axis=0)
    second_out_grad = across(pre_grad, up_full)
    norm_value, second_back = jax.vjp(layer_norm, middle_state, gain_second, shift_second)
    state_part, second_gain_grad, second_shift_grad = second_back(second_out_grad)
    middle_grad = end_grad + state_part
    attend_grad = middle_grad.astype(jnp.bfloat16)
    output_term = low(contract_rows(context, attend_grad))
    context_grad = across(attend_grad, output_full).astype(jnp.bfloat16)
    joint_grad = attention_backward(joint, allowed, logsum, context_grad)
    joint_term = low(contract_rows(normed_first, joint_grad))
    first_out_grad = across(joint_grad, joint_full)
    first_value, first_back = jax.vjp(layer_norm, start_state, gain_first, shift_first)
    start_part, first_gain_grad, first_shift_grad = first_back(first_out_grad)
    start_grad = middle_grad + start_part
    start_low = start_grad.astype(jnp.bfloat16)
    start_group = group_gather(start_low).reshape(GROUP * row_count, D)
    embed_term = low(contract_rows(start_group, cells_rows))
    cells_half = low(
        matmul(start_group, embed_cols) - wide(recon_grad.reshape(GROUP * row_count, CHUNK))
    )

    vectors = [
        up_bias_grad,
        down_bias_grad,
        first_gain_grad,
        first_shift_grad,
        second_gain_grad,
        second_shift_grad,
        encoder_bias_grad,
    ]
    priors = jnp.concatenate([prior_mean_grad, prior_logvar_grad])
    priors = priors.reshape(2 * kinds, devices, -1).transpose(1, 0, 2).reshape(devices, -1)
    prior_size = priors.shape[1]
    packed = jnp.concatenate([v.reshape(devices, -1) for v in vectors] + [priors], axis=1)
    packed = jnp.pad(packed, ((0, 0), (0, 1024 - packed.shape[1])))
    packed = packed.reshape(total, 2, 2, 8, 128)

    def by_device(term):
        return term.reshape(total, 2, 2, term.shape[0] // devices, term.shape[1])

    scatter = scatter_sums if total <= NARROW else scatter_plain
    embed_grad, decoder_grad, cells_grad, *middle_grads, small_sum, recon_total = scatter(
        embed_term.reshape(total, GROUP, rows, CHUNK),
        decoder_term.reshape(total, GROUP, thin, CHUNK),
        by_device(joint_term),
        by_device(output_term),
        by_device(encoder_term),
        by_device(up_term),
        by_device(down_term),
        packed,
        recon_sum,
        cells_half.reshape(GROUP, row_count, CHUNK),
    )

    def all_genes(chunks):
        return jnp.concatenate(list(chunks), axis=1)[:, :GENES]

    cells_grad = all_genes(cells_grad)
    embed_grad = wide(all_genes(embed_grad))
    decoder_grad = wide(all_genes(decoder_grad))
    (
        joint_weight_grad,
        output_weight_grad,
        encoder_weight_grad,
        up_weight_grad,
        down_weight_grad,
    ) = middle_grads

    ends = [0]
    for vector in vectors:
        ends.append(ends[-1] + vector.shape[0] // devices)
    packed = small_sum.reshape(-1)
    vector_grads = [packed[ends[i] : ends[i + 1]] for i in range(len(vectors))]
    prior_out = packed[ends[-1] : ends[-1] + prior_size].reshape(2, kinds, -1)
    recon_total = 0.5 * jnp.sum(recon_total)
    loss = (recon_total / count + ramp_weight * jnp.sum(free)) / GENES
    return (
        loss,
        cells_grad,
        embed_grad,
        joint_weight_grad,
        output_weight_grad,
        up_weight_grad,
        vector_grads[0],
        down_weight_grad,
        vector_grads[1],
        vector_grads[2],
        vector_grads[3],
        vector_grads[4],
        vector_grads[5],
        encoder_weight_grad,
        vector_grads[6],
        prior_out[0],
        prior_out[1],
        decoder_grad,
    )


def solution(mesh):
    in_specs = (
        P(("dp", "fsdp"), None),
        P(None, ("dp", "fsdp")),
        P(("dp", "fsdp"), None),
        P(("dp", "fsdp"), None),
        P(("dp", "fsdp")),
        P(("dp", "fsdp"), None),
        P(),
        P(("dp", "fsdp"), None),
        P(("dp", "fsdp"), None),
        P(("dp", "fsdp"), None),
        P(("dp", "fsdp"), None),
        P(("dp", "fsdp")),
        P(("dp", "fsdp"), None),
        P(("dp", "fsdp")),
        P(("dp", "fsdp")),
        P(("dp", "fsdp")),
        P(("dp", "fsdp")),
        P(("dp", "fsdp")),
        P(("dp", "fsdp"), None),
        P(("dp", "fsdp")),
        P(None, ("dp", "fsdp")),
        P(None, ("dp", "fsdp")),
        P(("dp", "fsdp"), None),
    )
    out_specs = (
        P(),
        P(("dp", "fsdp"), None),
        P(("dp", "fsdp"), None),
        P(("dp", "fsdp"), None),
        P(("dp", "fsdp"), None),
        P(("dp", "fsdp"), None),
        P(("dp", "fsdp")),
        P(("dp", "fsdp"), None),
        P(("dp", "fsdp")),
        P(("dp", "fsdp")),
        P(("dp", "fsdp")),
        P(("dp", "fsdp")),
        P(("dp", "fsdp")),
        P(("dp", "fsdp"), None),
        P(("dp", "fsdp")),
        P(None, ("dp", "fsdp")),
        P(None, ("dp", "fsdp")),
        P(("dp", "fsdp"), None),
    )
    return jax.shard_map(shards, mesh=mesh, in_specs=in_specs, out_specs=out_specs, check_vma=False)
```

```python
import functools
import math

import jax
import jax.numpy as jnp
from jax import lax
from jax.experimental import pallas as pl
from jax.experimental.pallas import tpu as pltpu
from jax.sharding import PartitionSpec as P

D = 1024
HEAD_DIM = 64
GENES = 13500
LATENT = 512


NEG_SCORE = -1000000000.0
NORM_EPS = 1e-05
FREE_FLOOR = 1.0
FREE_TEMP = 0.25


def layer_norm(hidden, gain, shift):
    center = hidden - jnp.mean(hidden, axis=-1, keepdims=True)
    spread = jnp.mean(center * center, axis=-1, keepdims=True)
    return center * lax.rsqrt(spread + NORM_EPS) * gain + shift


def positions(coordinates):
    quarter = D // 4
    frequency = jnp.exp(jnp.arange(quarter, dtype=jnp.float32) * (-math.log(10000.0) / quarter))
    angle_x = coordinates[0][:, None] * frequency[None, :]
    angle_y = coordinates[1][:, None] * frequency[None, :]
    return jnp.concatenate(
        [jnp.sin(angle_x), jnp.cos(angle_x), jnp.sin(angle_y), jnp.cos(angle_y)], axis=1
    )


def matmul(left, right):
    return jnp.dot(left, right, preferred_element_type=jnp.float32)


def across(left, right):
    return lax.dot_general(
        left, right, (((1,), (1,)), ((), ())), preferred_element_type=jnp.float32
    )


def contract_rows(left, right):
    return lax.dot_general(
        left, right, (((0,), (0,)), ((), ())), preferred_element_type=jnp.float32
    )


def split_heads(joint):
    row_count = joint.shape[0]
    queries = joint[:, :D].reshape(row_count, -1, HEAD_DIM)
    keys = joint[:, D : 2 * D].reshape(row_count, -1, HEAD_DIM)
    values = joint[:, 2 * D :].reshape(row_count, -1, HEAD_DIM)
    return (queries, keys, values)


def masked_scores(queries, keys, allowed):
    scores = jnp.einsum(
        "qhd,khd->hqk", queries, keys, preferred_element_type=jnp.float32
    ) * HEAD_DIM ** (-0.5)
    return jnp.where(allowed[None], scores, NEG_SCORE)


def attention_forward(joint, allowed):
    queries, keys, values = split_heads(joint)
    masked = masked_scores(queries, keys, allowed)
    peak = jnp.max(masked, axis=-1, keepdims=True)
    raised = jnp.exp(masked - peak)
    denom = jnp.sum(raised, axis=-1, keepdims=True)
    probs = raised / denom
    logsum = peak + jnp.log(denom)
    context = jnp.einsum(
        "hqk,khd->qhd", probs.astype(jnp.bfloat16), values, preferred_element_type=jnp.float32
    )
    return (context.reshape(joint.shape[0], D).astype(jnp.bfloat16), logsum)


def attention_backward(joint, allowed, logsum, context_grad):
    row_count = joint.shape[0]
    queries, keys, values = split_heads(joint)
    probs = jnp.exp(masked_scores(queries, keys, allowed) - logsum)
    probs_low = probs.astype(jnp.bfloat16)
    incoming = context_grad.reshape(row_count, -1, HEAD_DIM)
    value_grad = jnp.einsum("hqk,qhd->khd", probs_low, incoming, preferred_element_type=jnp.float32)
    prob_grad = jnp.einsum("qhd,khd->hqk", incoming, values, preferred_element_type=jnp.float32)
    score_grad = (probs * (prob_grad - jnp.sum(probs * prob_grad, axis=-1, keepdims=True))).astype(
        jnp.bfloat16
    )
    query_grad = jnp.einsum(
        "hqk,khd->qhd", score_grad, keys, preferred_element_type=jnp.float32
    ) * HEAD_DIM ** (-0.5)
    key_grad = jnp.einsum(
        "hqk,qhd->khd", score_grad, queries, preferred_element_type=jnp.float32
    ) * HEAD_DIM ** (-0.5)
    return jnp.concatenate(
        [
            query_grad.reshape(row_count, D),
            key_grad.reshape(row_count, D),
            value_grad.reshape(row_count, D),
        ],
        axis=1,
    ).astype(jnp.bfloat16)

AXES = ("dp", "fsdp")
GROUP = 4
CHUNK = 3456
SLICE = 384
NARROW = 8


def low(values):
    return values.astype(jnp.bfloat16)


def wide(values):
    return values.astype(jnp.float32)


def device_total():
    return lax.axis_size("dp") * lax.axis_size("fsdp")


def device_index():
    return lax.axis_index("dp") * lax.axis_size("fsdp") + lax.axis_index("fsdp")


def swap(values, mask):
    return lax.ppermute(values, AXES, [(i, i ^ mask) for i in range(device_total())])


def same_quarter():
    return [[d for d in range(lax.axis_size("dp")) if d % 2 == odd] for odd in range(2)]


def pick(blocks, index):
    return lax.dynamic_index_in_dim(blocks, index, 0, keepdims=False)


def group_exchange(blocks, quarter):
    return [pick(blocks, quarter)] + [swap(pick(blocks, quarter ^ m), m) for m in range(1, GROUP)]


def group_gather(values):
    pair = jnp.stack([values, swap(values, 2)])
    other = swap(pair, 1)
    return jnp.stack([pair[0], other[0], pair[1], other[1]])


def group_scatter(parts):
    mine = jnp.stack([parts[0], parts[2]])
    theirs = low(jnp.stack([parts[1], parts[3]]))
    summed = wide(mine) + wide(swap(theirs, 1))
    return summed[0] + wide(swap(low(summed[1]), 2))


def by_quarter(pieces, quarter):
    stacked = jnp.stack(pieces)
    return [pick(stacked, quarter ^ j) for j in range(GROUP)]


def gene_chunks(values):
    padded = jnp.pad(values, ((0, 0), (0, GROUP * CHUNK - GENES)))
    return jnp.stack([padded[:, j * CHUNK : (j + 1) * CHUNK] for j in range(GROUP)])


def sum_all(values):
    mask = 1
    while mask < device_total():
        values = values + swap(values, mask)
        mask *= 2
    return values


MESH = pl.DeviceIdType.MESH


class Where:
    def __init__(self, total):
        dp = lax.axis_index("dp")
        self.total = total
        self.core = lax.axis_index("fsdp")
        self.x = dp % 2
        self.t = dp // 2
        self.quarter = 2 * self.x + self.core
        y, z = self.t % 2, self.t // 2
        self.k = z + y * (total - 1 - 2 * z)
        self.right = (2 * self.owner(-1) + self.x, self.core)
        self.left = (2 * self.owner(1) + self.x, self.core)
        self.peers = [
            None,
            (dp, 1 - self.core),
            (2 * self.t + 1 - self.x, self.core),
            (2 * self.t + 1 - self.x, 1 - self.core),
        ]
        self.quarters = [
            self.quarter,
            2 * self.x + 1 - self.core,
            2 * (1 - self.x) + self.core,
            2 * (1 - self.x) + 1 - self.core,
        ]

    def owner(self, step):
        place = (self.k - step + self.total) % self.total
        y = place // (self.total // 2)
        return 2 * (place + y * (self.total - 1 - 2 * place)) + y

    def same(self, step):
        t = (self.t + step) % self.total
        return t, (2 * t + self.x, self.core)

    def meet(self, everyone=False):
        barrier = pltpu.get_barrier_semaphore()
        others = self.peers[1:]
        if everyone:
            others = others + [self.same(step)[1] for step in range(1, self.total)]
        else:
            others = others + [self.right, self.left]
        for other in others:
            pl.semaphore_signal(barrier, inc=1, device_id=other, device_id_type=MESH)
        pl.semaphore_wait(barrier, len(others))


class Copies:
    def __init__(self, send_sems, recv_sems, local_sems):
        self.send_sems, self.recv_sems, self.local_sems = send_sems, recv_sems, local_sems
        self.remote_count = self.local_count = 0
        self.sent = []

    def send(self, source, target, device):
        at = self.remote_count
        self.remote_count += 1
        copy = pltpu.make_async_remote_copy(
            source,
            target,
            self.send_sems.at[at],
            self.recv_sems.at[at],
            device_id=device,
            device_id_type=MESH,
        )
        copy.start()
        self.sent.append(copy)
        return copy

    def local(self, source, target):
        at = self.local_count
        self.local_count += 1
        copy = pltpu.make_async_copy(source, target, self.local_sems.at[at])
        copy.start()
        return copy

    def free(self, copy):
        copy.wait_send()
        self.sent = [other for other in self.sent if other is not copy]

    def finish(self):
        for copy in self.sent:
            copy.wait_send()


def gather_kernel(total, *refs):
    (cells, embed, decoder, joint, small, output, encoder, up, down) = refs[:9]
    (cells_all, embed_all, decoder_all, joint_all, small_all) = refs[9:14]
    (output_all, encoder_all, up_all, down_all, embedded) = refs[14:19]
    (held_cells, held_embed, partial, other_core, for_x, other_x) = refs[19:25]
    here = Where(total)
    copies = Copies(*refs[25:])
    here.meet()
    t, x, core = here.t, here.x, here.core
    last = total - 1
    towards = {1: here.right, -1: here.left}
    flying = {}

    late = [(up, up_all, 1), (output, output_all, 1), (down, down_all, -1), (encoder, encoder_all, -1)]
    shares = {
        name: [
            copies.send(own.at[here.quarters[m]], full.at[t, here.quarter], here.peers[m])
            for m in (2, 3, 1)
        ]
        for name, own, full in (("embed", embed, embed_all), ("decoder", decoder, decoder_all))
    }
    for n, (own, full, way) in enumerate(late):
        flying["late", n] = copies.send(own, full.at[t, x, core], towards[way])
    across_x = [copies.send(own, full.at[t, x, core], here.peers[2]) for own, full, _ in late]
    own_cells = copies.local(cells.at[here.quarter], cells_all.at[0])
    cell_moves = [
        copies.send(cells.at[here.quarters[m]], cells_all.at[m], here.peers[m]) for m in (2, 3, 1)
    ]
    shares["early"] = [
        copies.send(own, full.at[t, x, core], here.peers[2])
        for own, full in ((joint, joint_all), (small, small_all))
    ]
    own_copies = {
        "embed": [copies.local(embed.at[here.quarter], embed_all.at[t, here.quarter])],
        "decoder": [copies.local(decoder.at[here.quarter], decoder_all.at[t, here.quarter])],
        "early": [
            copies.local(own, full.at[t, x, core])
            for own, full in ((joint, joint_all), (small, small_all))
        ],
    }
    own_late = [copies.local(own, full.at[t, x, core]) for own, full, _ in late]

    def late_step(s):
        for n, (_, full, way) in enumerate(late):
            flying["late", n].wait_recv()
            block = full.at[here.owner(way * s), x, core]
            if s < last:
                flying["late", n] = copies.send(block, block, towards[way])
            across_x.append(copies.send(block, block, here.peers[2]))

    def early_block(full, way, s):
        return full.at[here.owner(way * s), 0 if way == 1 else 1, core]

    def table_block(full, way, s):
        return full.at[here.owner(way * s), pl.ds(0 if way == 1 else 2, 2)]

    rings = {
        "embed": [(embed_all, way, table_block) for way in (1, -1)],
        "decoder": [(decoder_all, way, table_block) for way in (1, -1)],
        "early": [(full, way, early_block) for full in (joint_all, small_all) for way in (1, -1)],
    }

    def step(name, s):
        if s == 0:
            for copy in own_copies[name]:
                copy.wait()
            for copy in shares[name]:
                copy.wait_recv()
        for n, (full, way, block_of) in enumerate(rings[name]):
            if s > 0:
                flying[name, n].wait_recv()
            if s < last:
                block = block_of(full, way, s)
                flying[name, n] = copies.send(block, block, towards[way])

    holds = {}

    def hold(block):
        holds[block] = copies.local(embed_all.at[block], held_embed.at[block % 2])

    def multiply(block):
        holds[block].wait()
        features = held_embed.shape[1] * held_embed.shape[2]
        table = held_embed[block % 2].reshape(features, held_embed.shape[3])
        for row in range(2):
            for column in range(2):
                partial[row, column, :, pl.ds(block * features, features)] = low(
                    across(held_cells[2 * row + column], table)
                )
        if block + 2 < total:
            hold(block + 2)

    across_core = []

    def to_core(copies_of, block_of):
        for copy, (_, full, way) in zip(copies_of, late):
            copy.wait_recv()
            block = block_of(full, way)
            across_core.append(copies.send(block, block, here.peers[1]))

    def crossed(s):
        to_core(
            across_x[len(late) * s : len(late) * (s + 1)],
            lambda full, way: full.at[here.owner(way * s), 1 - x, core],
        )

    for s in range(1, last + 1):
        late_step(s)
        if s == 1:
            step("embed", 0)
        step("embed", s)
        if s == last - 1:
            step("early", 0)
            step("decoder", 0)
    hold(0)
    hold(1)
    for copy in own_late:
        copy.wait()
    for _, full, _ in late:
        block = full.at[:, x, core]
        across_core.append(copies.send(block, block, here.peers[1]))
    for copy in cell_moves:
        copy.wait_recv()
    own_cells.wait()
    held = copies.local(cells_all, held_cells)
    step("early", 1)
    step("decoder", 1)
    held.wait()
    for s in range(2, last + 1):
        multiply(s - 2)
        step("early", s)
        step("decoder", s)
        crossed(s - 2)
    for block in range(last - 1, total):
        multiply(block)
    sums = copies.send(partial.at[:, 1], other_core, here.peers[1])
    for full in (joint_all, small_all):
        block = full.at[:, :, core]
        across_core.append(copies.send(block, block, here.peers[1]))
    sums.wait_recv()
    for_x[...] = low(wide(partial[1, 0]) + wide(other_core[1]))
    sums = copies.send(for_x, other_x, here.peers[2])
    for s in range(last - 1, total):
        crossed(s)
    sums.wait_recv()
    embedded[...] = wide(partial[0, 0]) + wide(other_core[0]) + wide(other_x[...])
    for copy in across_core:
        copy.wait_recv()
    copies.finish()


def gather_weights(cells, embed, decoder, joint, small, output, encoder, up, down):
    total = device_total() // GROUP
    own = [joint, small, output, encoder, up, down]
    tables = [embed, decoder]
    operands = [cells] + tables + own
    shapes = (
        [cells.shape]
        + [(total,) + v.shape for v in tables]
        + [(total, 2, 2) + v.shape for v in own]
    )
    remote = 15 + 12 * (total - 1) + 8 * total + 8
    cell_rows, genes = cells.shape[1:]
    features = total * GROUP * embed.shape[1]
    buffers = [
        cells.shape,
        (2,) + embed.shape,
        (2, 2, cell_rows, features),
        (2, cell_rows, features),
        (cell_rows, features),
        (cell_rows, features),
    ]
    return pl.pallas_call(
        functools.partial(gather_kernel, total),
        out_shape=[jax.ShapeDtypeStruct(s, jnp.bfloat16) for s in shapes]
        + [jax.ShapeDtypeStruct((cell_rows, features), jnp.float32)],
        in_specs=[pl.BlockSpec(memory_space=pl.ANY)] * len(operands),
        out_specs=[pl.BlockSpec(memory_space=pl.ANY)] * len(operands)
        + [pl.BlockSpec(memory_space=pltpu.VMEM)],
        scratch_shapes=[pltpu.VMEM(shape, jnp.bfloat16) for shape in buffers]
        + [
            pltpu.SemaphoreType.DMA((remote,)),
            pltpu.SemaphoreType.DMA((remote,)),
            pltpu.SemaphoreType.DMA((10 + total,)),
        ],
        compiler_params=pltpu.CompilerParams(
            collective_id=1, has_side_effects=True, vmem_limit_bytes=32 * 2**20
        ),
        name="gather_weights",
    )(*operands)


def add_rows(target, first, second, dtype):
    rows, columns = target.shape
    step = min(rows, 16 if columns > 2048 else 32)

    @pl.loop(0, rows // step)
    def _(i):
        part = pl.ds(pl.multiple_of(i * step, step), step)
        target[part, :] = (wide(first[part, :]) + wide(second[part, :])).astype(dtype)


def product(target, left, right, accumulate):
    total, _, rows, columns = target.shape
    step = 256 // (2 * rows)
    width = 512

    @pl.loop(0, total // step)
    def _(i):
        blocks = pl.ds(i * step, step)
        part = left(i * 2 * step, 2 * step)

        @pl.loop(0, columns // width)
        def _(n):
            across_columns = pl.ds(pl.multiple_of(n * width, width), width)
            value = matmul(part, right[:, across_columns]).reshape(step, 2, rows, width)
            if accumulate:
                value = value + wide(target[blocks, :, :, across_columns])
            target[blocks, :, :, across_columns] = low(value)


MIDDLE = ("joint", "output", "encoder", "up", "down")


def scatter_kernel(total, *refs):
    (recon, start, small, decoder, cells, table, grads) = refs[:7]
    left = dict(zip(MIDDLE, refs[7:12]))
    right = dict(zip(MIDDLE, refs[12:17]))
    (embed_out, decoder_out, cells_out, embed, back) = refs[17:22]
    results = dict(zip(MIDDLE, refs[22:27]))
    (small_out, recon_out) = refs[27:29]
    (chip_small, stage_small, sum_small, hop_small, group_recon, all_recon) = refs[29:35]
    chip = dict(zip(MIDDLE, refs[35:40]))
    (send_up, send_down) = refs[40:42]
    sums = dict(zip(MIDDLE[1:], refs[42:46]))
    (hop_embed, hop_decoder, hop_joint) = refs[46:49]
    hops_of = dict(zip(MIDDLE[1:], refs[49:53]))
    (local_embed, local_decoder) = refs[53:55]
    (other_joint, starts, turned) = refs[55:58]
    (in_cells, in_table, in_grads, out_term, out_back, blocks) = refs[58:64]
    here = Where(total)
    copies = Copies(*refs[64:67])
    stream_sems = refs[67]
    here.meet()
    x, core, last = here.x, here.core, total - 1
    towards = {1: here.right, -1: here.left}
    flying = {}

    def lanes(term, hops, local):
        return [(term, hops, local, way, side) for side, way in ((0, 1), (1, -1))]

    tables = {
        "embed": lanes(embed, hop_embed, local_embed),
        "decoder": lanes(decoder, hop_decoder, local_decoder),
    }

    def table_block(term, way, side, h):
        return term.at[here.owner(way * h), pl.ds(2 * side, 2)]

    def fetch(name, h):
        for n, (term, _, local, way, side) in enumerate(tables[name]):
            flying["local", name, n, h] = copies.local(
                table_block(term, way, side, h + 1), local.at[h % 2, side]
            )

    def table_start(name):
        for n, (term, hops, _, way, side) in enumerate(tables[name]):
            flying[name, n] = copies.send(
                table_block(term, way, side, 1), hops.at[0, side], towards[way]
            )
        fetch(name, 1)
        fetch(name, 2)

    def table_hop(name, h):
        for n, (_, hops, local, way, side) in enumerate(tables[name]):
            flying[name, n].wait_recv()
            flying["local", name, n, h].wait()
            for row in range(2):
                arrived = hops.at[h - 1, side, row]
                add_rows(arrived, arrived, local.at[h % 2, side, row], jnp.bfloat16)
            if h < last:
                flying[name, n] = copies.send(hops.at[h - 1, side], hops.at[h, side], towards[way])
        if h + 2 <= last:
            fetch(name, h + 2)

    table_start("decoder")
    moves = [copies.send(start, starts.at[m], here.peers[m]) for m in (2, 3, 1)]
    starts[0] = start[...]
    group_recon[here.quarter] = recon[...]
    recons = [copies.send(recon, group_recon.at[here.quarter], here.peers[m]) for m in (2, 3, 1)]
    halves = {"small": copies.send(small.at[:, :, 1 - core], chip_small, here.peers[1])}
    own_small = copies.local(small.at[:, :, core], stage_small)

    def half(name, which):
        source = left[name]
        if results[name].shape[0] == 128:

            def wide_blocks(first, size):
                lanes = [
                    pl.ds(pl.multiple_of((2 * (first + n) + which) * 128, 128), 128)
                    for n in range(size)
                ]
                return jnp.concatenate([low(wide(source[:, part]).T) for part in lanes])

            return wide_blocks
        blocks[...] = low(wide(source[...]).T).reshape(blocks.shape)

        def narrow_blocks(first, size):
            return blocks[pl.ds(first, size), which].reshape(-1, blocks.shape[-1])

        return narrow_blocks

    def give(name, buffer):
        product(buffer, half(name, 1 - core), right[name], False)
        halves[name] = copies.send(buffer, chip[name], here.peers[1])

    across = {}

    def cross(name, held, target):
        across[name] = copies.send(held.at[:, 1 - x], target, here.peers[2])

    def take(name):
        halves[name].wait_recv()
        product(chip[name], half(name, core), right[name], True)
        if name in sums:
            cross(name, chip[name], sums[name])

    give("up", send_up)
    give("down", send_down)
    table_hop("decoder", 1)
    take("up")
    copies.free(halves["up"])
    give("joint", send_up.at[:, :, :, pl.ds(0, right["joint"].shape[1])])
    table_hop("decoder", 2)
    take("down")
    copies.free(halves["down"])
    slim = results["output"].shape[0]
    give("output", send_down.at[:, :, pl.ds(0, slim)])
    give("encoder", send_down.at[:, :, pl.ds(slim, slim)])
    table_hop("decoder", 3)
    take("joint")
    for side, way in ((0, 1), (1, -1)):
        flying["joint", side] = copies.send(
            chip["joint"].at[here.owner(way), side], hop_joint.at[0, side], towards[way]
        )
    take("output")
    take("encoder")
    own_small.wait()
    halves["small"].wait_recv()

    @pl.loop(0, total)
    def _(t):
        for side in range(2):
            held = chip_small.at[t, side]
            add_rows(held, held, stage_small.at[t, side], jnp.float32)

    cross("small", chip_small, sum_small)
    for copy in recons:
        copy.wait_recv()
    all_recon[here.t] = group_recon[0] + group_recon[1] + group_recon[2] + group_recon[3]
    own_recon = all_recon.at[here.t]
    flying["recon"] = copies.send(own_recon, own_recon, here.right)
    table_hop("decoder", 4)

    for copy in moves:
        copy.wait_recv()
    moves = []
    rows, rows_of_t = start.shape[0], turned.shape[0] // total
    for m in range(GROUP):
        turned[:, m * rows : (m + 1) * rows] = low(wide(starts[m]).T)

    def moved(i, pairs, first):
        part = pl.ds(pl.multiple_of(i * SLICE, 128), SLICE)
        slot = i % 2
        return [
            pltpu.make_async_copy(*ends(part, slot), stream_sems.at[first + n, slot])
            for n, ends in enumerate(pairs)
        ]

    def loads_of(i):
        return moved(
            i,
            [
                lambda part, slot: (cells.at[:, :, part], in_cells.at[slot]),
                lambda part, slot: (table.at[:, part], in_table.at[slot]),
                lambda part, slot: (grads.at[:, :, part], in_grads.at[slot]),
            ],
            0,
        )

    def stores_of(i):
        return moved(
            i,
            [
                lambda part, slot: (out_term.at[slot], embed.at[:, :, :, part]),
                lambda part, slot: (out_back.at[slot], back.at[:, :, part]),
            ],
            3,
        )

    count = CHUNK // SLICE
    for copy in loads_of(0):
        copy.start()

    def stream(first, end):
        @pl.loop(first, end)
        def _(i):
            slot = i % 2
            @pl.when(i + 1 < count)
            def _():
                for copy in loads_of(i + 1):
                    copy.start()

            for copy in loads_of(i):
                copy.wait()

            @pl.when(i >= 2)
            def _():
                for copy in stores_of(i - 2):
                    copy.wait()

            for t in range(total):
                term = matmul(
                    turned[pl.ds(t * rows_of_t, rows_of_t), :],
                    in_cells[slot].reshape(GROUP * rows, SLICE),
                )
                out_term[slot, t] = low(term).reshape(out_term.shape[2:])
            for m in range(GROUP):
                out_back[slot, m] = low(matmul(starts[m], in_table[slot]) - wide(in_grads[slot, m]))
            for copy in stores_of(i):
                copy.start()

    stream(0, count // 3)
    table_hop("decoder", 5)
    stream(count // 3, 2 * count // 3)
    table_hop("decoder", 6)
    stream(2 * count // 3, count)
    for i in (count - 2, count - 1):
        for copy in stores_of(i):
            copy.wait()
    table_start("embed")
    moves = [copies.send(back.at[m], cells_out.at[here.quarter], here.peers[m]) for m in (2, 3, 1)]
    own = [copies.local(back.at[0], cells_out.at[here.quarter])]
    table_hop("decoder", last)

    def send_back(hops, out):
        done = [hops.at[last - 1, quarter // 2, quarter % 2] for quarter in here.quarters]
        for m in (2, 3, 1):
            moves.append(copies.send(done[m], out.at[here.quarter], here.peers[m]))
        own.append(copies.local(done[0], out.at[here.quarter]))

    send_back(hop_decoder, decoder_out)

    def recon_hop(h):
        flying["recon"].wait_recv()
        if h < last:
            arrived = all_recon.at[here.owner(h)]
            flying["recon"] = copies.send(arrived, arrived, here.right)

    def joint_hop(h):
        for side, way in ((0, 1), (1, -1)):
            flying["joint", side].wait_recv()
            arrived = hop_joint.at[h - 1, side]
            local = chip["joint"].at[here.owner(way * (h + 1)), side]
            add_rows(arrived, arrived, local, jnp.bfloat16)
            if h < last:
                flying["joint", side] = copies.send(arrived, hop_joint.at[h, side], towards[way])

    late = [
        (name, sums[name], chip[name], hops_of[name], results[name], way)
        for name, way in (("up", 1), ("down", -1), ("output", 1), ("encoder", -1))
    ] + [("small", sum_small, chip_small, hop_small, small_out, 1)]

    def late_start():
        for name, summed, held, hops, _, way in late:
            across[name].wait_recv()

            @pl.loop(0, total)
            def _(t):
                add_rows(summed.at[t], summed.at[t], held.at[t, x], summed.dtype)

            flying["late", name] = copies.send(summed.at[here.owner(way)], hops.at[0], towards[way])

    def late_hop(h):
        for name, summed, _, hops, result, way in late:
            flying["late", name].wait_recv()
            local = summed.at[here.owner(way * (h + 1))]
            if h < last:
                add_rows(hops.at[h - 1], hops.at[h - 1], local, hops.dtype)
                flying["late", name] = copies.send(hops.at[h - 1], hops.at[h], towards[way])
            else:
                add_rows(result, hops.at[h - 1], local, jnp.float32)

    for h in range(1, last + 1):
        joint_hop(h)
        table_hop("embed", h)
        recon_hop(h)
    send_back(hop_embed, embed_out)
    done_joint = hop_joint.at[last - 1]
    joint_move = copies.send(done_joint.at[1 - x], other_joint, here.peers[2])
    late_start()
    for h in range(1, last + 1):
        late_hop(h)
    summed = all_recon[0]
    for t in range(1, total):
        summed = summed + all_recon[t]
    recon_out[...] = summed
    joint_move.wait_recv()
    add_rows(results["joint"], done_joint.at[x], other_joint, jnp.float32)
    for copy in moves:
        copy.wait_recv()
    for copy in own:
        copy.wait()
    copies.finish()


def scatter_sums(pairs, start, decoder, cells, table, grads, small, recon):
    total = device_total() // GROUP
    last = total - 1
    rows, features = start.shape
    thin = jnp.bfloat16
    share = features // (total * GROUP)
    lefts, rights, shapes = [], [], []
    for before, after in pairs:
        block = before.shape[1] // device_total()
        lefts.append(before)
        rights.append(after)
        shapes.append((block, after.shape[1]))
    operands = [recon, start, small, decoder, cells, table, grads] + lefts + rights
    decoder_share = decoder.shape[1:]
    embed_share = (GROUP, share, CHUNK)
    out_shape = [
        jax.ShapeDtypeStruct(v, thin)
        for v in (embed_share, decoder_share, cells.shape, (total,) + embed_share, cells.shape)
    ]
    block = small.shape[3:]
    out_shape += [jax.ShapeDtypeStruct(v, jnp.float32) for v in shapes + [block, recon.shape]]
    exact = [(total, 2) + block, (total, 2) + block, (total,) + block, (last,) + block]
    exact += [(GROUP,) + recon.shape, (total,) + recon.shape]
    chips = [(total, 2) + v for v in shapes]
    buffers = chips + [chips[3], chips[4]] + [(total,) + v for v in shapes[1:]]
    buffers += [(last, 2, 2) + v[1:] for v in (embed_share, decoder_share)]
    buffers += [(last, 2) + shapes[0]] + [(last,) + v for v in shapes[1:]]
    buffers += [(2, 2, 2) + v[1:] for v in (embed_share, decoder_share)]
    buffers += [shapes[0], (GROUP,) + start.shape, (features, GROUP * rows)]
    buffers += [(2, GROUP, rows, SLICE), (2, features, SLICE), (2, GROUP, rows, SLICE)]
    buffers += [(2, total, GROUP, share, SLICE), (2, GROUP, rows, SLICE)]
    buffers += [(2 * total, 2, shapes[0][0], rows)]
    remote, here = 12 + 6 * last + 4 * last + 15 + 2 * last, 4 * last + 9
    anywhere, vmem = pl.BlockSpec(memory_space=pl.ANY), pl.BlockSpec(memory_space=pltpu.VMEM)
    outs = pl.pallas_call(
        functools.partial(scatter_kernel, total),
        out_shape=out_shape,
        in_specs=[vmem] * 2 + [anywhere] * 5 + [vmem] * 10,
        out_specs=[anywhere] * 5 + [vmem] * 7,
        scratch_shapes=[pltpu.VMEM(shape, jnp.float32) for shape in exact]
        + [pltpu.VMEM(shape, thin) for shape in buffers]
        + [
            pltpu.SemaphoreType.DMA((remote,)),
            pltpu.SemaphoreType.DMA((remote,)),
            pltpu.SemaphoreType.DMA((here,)),
            pltpu.SemaphoreType.DMA((5, 2)),
        ],
        compiler_params=pltpu.CompilerParams(
            collective_id=2, has_side_effects=True, vmem_limit_bytes=60 * 2**20
        ),
        name="scatter_sums",
    )(*operands)
    return outs[:3] + outs[5:]


def scatter_plain(pairs, start, decoder, cells, table, grads, small, recon):
    quarter = device_index() % GROUP
    total = device_total() // GROUP
    starts = group_gather(start).reshape(-1, start.shape[1])
    wide_cells = cells.reshape(-1, CHUNK)
    embed = low(contract_rows(starts, wide_cells)).reshape(total, GROUP, -1, CHUNK)
    back = low(matmul(starts, table) - wide(grads.reshape(-1, CHUNK))).reshape(cells.shape)

    def sent(blocks):
        pieces = [pick(blocks, 0)] + [swap(blocks[m], m) for m in range(1, GROUP)]
        return jnp.stack(by_quarter(pieces, quarter))

    def table_sum(term):
        block = lax.psum_scatter(
            term, "dp", axis_index_groups=same_quarter(), scatter_dimension=0, tiled=False
        )
        return sent(jnp.stack(by_quarter(list(block), quarter)))

    def middle(term):
        rows = term.reshape((device_total(), -1) + term.shape[-1:])
        return wide(lax.psum_scatter(rows, AXES, scatter_dimension=0, tiled=False))

    terms = [low(contract_rows(before, after)) for before, after in pairs]
    small = small.reshape((device_total(),) + small.shape[3:])
    return (
        [table_sum(embed), table_sum(decoder), sent(back)]
        + [middle(term) for term in terms]
        + [lax.psum_scatter(small, AXES, scatter_dimension=0, tiled=False), sum_all(recon)]
    )


def latent_kernel(total, *refs):
    (message, spread, ratio, decoder, cells) = refs[:5]
    (recon_grad, decoder_term, latent_grad, spread_sum, recon_sum) = refs[5:10]
    (latents, held_decoder, held_cells, held_grad, held_term, turned, partial) = refs[10:17]
    (leaving, arriving, group_spread, all_spread) = refs[17:21]
    here = Where(total)
    copies = Copies(*refs[21:])
    here.meet(everyone=True)
    moves = [copies.send(message, latents.at[m], here.peers[m]) for m in (2, 3, 1)]
    spreads = [copies.send(spread, group_spread.at[here.quarter], here.peers[m]) for m in (2, 3, 1)]
    loads = [
        copies.local(message, latents.at[0]),
        copies.local(decoder, held_decoder),
        copies.local(cells, held_cells),
    ]
    group_spread[here.quarter] = spread[...]
    for copy in spreads:
        copy.wait_recv()
    all_spread[here.t] = (
        group_spread[0] + group_spread[1] + group_spread[2] + group_spread[3]
    )
    spreads = []
    for away in range(1, total):
        own = all_spread.at[here.t]
        spreads.append(copies.send(own, own, here.same(away)[1]))
    for copy in loads:
        copy.wait()
    for copy in moves:
        copy.wait_recv()
    rows = message.shape[0]
    size = held_decoder.shape[0]
    for m in range(GROUP):
        turned[:, m * rows : (m + 1) * rows] = low(wide(latents[m, :, :size]).T)
    partial[...] = jnp.zeros_like(partial)
    recon_sum[...] = jnp.zeros_like(recon_sum)

    @pl.loop(0, CHUNK // SLICE)
    def _(i):
        part = pl.ds(pl.multiple_of(i * SLICE, 128), SLICE)
        table = held_decoder[:, part]
        for m in range(GROUP):
            live = wide(latents[m, :, size : size + 128])
            live = jnp.concatenate([live] * (SLICE // 128), axis=1)
            miss = matmul(latents[m, :, :size], table) - wide(held_cells[m, :, part])
            weighted = live * miss
            recon_sum[...] += jnp.sum((weighted * miss).reshape(rows // 8, 8, SLICE), axis=0)
            grad = low(ratio[0, 0] * weighted)
            held_grad[m, :, part] = grad
            partial[m] += across(grad, table)
        held_term[:, part] = low(matmul(turned[...], held_grad[:, :, part].reshape(GROUP * rows, SLICE)))

    leaving[...] = low(partial[...])
    moves = [copies.send(leaving.at[m], arriving.at[m - 1], here.peers[m]) for m in (2, 3, 1)]
    stores = [copies.local(held_grad, recon_grad), copies.local(held_term, decoder_term)]
    for copy in spreads:
        copy.wait_recv()
    summed = all_spread[0]
    for t in range(1, total):
        summed = summed + all_spread[t]
    spread_sum[...] = summed
    for copy in moves:
        copy.wait_recv()
    latent_grad[...] = (
        (partial[0] + wide(arriving[0])) + (wide(arriving[1]) + wide(arriving[2]))
    )
    for copy in stores:
        copy.wait()
    copies.finish()


def latent_step(message, spread, ratio, decoder, cells):
    total = device_total() // GROUP
    rows, size = message.shape[0], decoder.shape[0]
    thin = jnp.bfloat16
    vmem = pl.BlockSpec(memory_space=pltpu.VMEM)
    anywhere = pl.BlockSpec(memory_space=pl.ANY)
    remote = 9 + total - 1
    return pl.pallas_call(
        functools.partial(latent_kernel, total),
        out_shape=[
            jax.ShapeDtypeStruct(cells.shape, thin),
            jax.ShapeDtypeStruct(decoder.shape, thin),
            jax.ShapeDtypeStruct((rows, size), jnp.float32),
            jax.ShapeDtypeStruct(spread.shape, jnp.float32),
            jax.ShapeDtypeStruct((8, SLICE), jnp.float32),
        ],
        in_specs=[vmem, vmem, pl.BlockSpec(memory_space=pltpu.SMEM), anywhere, anywhere],
        out_specs=[anywhere, anywhere, vmem, vmem, vmem],
        scratch_shapes=[
            pltpu.VMEM((GROUP,) + message.shape, thin),
            pltpu.VMEM(decoder.shape, thin),
            pltpu.VMEM(cells.shape, thin),
            pltpu.VMEM(cells.shape, thin),
            pltpu.VMEM(decoder.shape, thin),
            pltpu.VMEM((size, GROUP * rows), thin),
            pltpu.VMEM((GROUP, rows, size), jnp.float32),
            pltpu.VMEM((GROUP, rows, size), thin),
            pltpu.VMEM((GROUP - 1, rows, size), thin),
            pltpu.VMEM((GROUP,) + spread.shape, jnp.float32),
            pltpu.VMEM((total,) + spread.shape, jnp.float32),
            pltpu.SemaphoreType.DMA((remote,)),
            pltpu.SemaphoreType.DMA((remote,)),
            pltpu.SemaphoreType.DMA((5,)),
        ],
        compiler_params=pltpu.CompilerParams(
            collective_id=3, has_side_effects=True, vmem_limit_bytes=40 * 2**20
        ),
        name="latent_step",
    )(message, spread, ratio, decoder, cells)


def latent_plain(message, spread, ratio, decoder, cells):
    size = decoder.shape[0]
    gathered = group_gather(message).reshape(-1, message.shape[1])
    latents, live = gathered[:, :size], wide(gathered[:, size : size + 1])
    miss = matmul(latents, decoder) - wide(cells.reshape(-1, CHUNK))
    grad = low(ratio[0, 0] * live * miss)
    recon_sum = jnp.sum((live * miss * miss).reshape(-1, 8, CHUNK), axis=0)
    latent_grad = group_scatter(low(across(grad, decoder)).reshape(GROUP, -1, size))
    term = low(contract_rows(latents, grad))
    return grad.reshape(cells.shape), term, latent_grad, sum_all(spread), recon_sum


def gather_plain(cells, embed, decoder, *own):
    quarter = device_index() % GROUP
    total = device_total() // GROUP
    groups = same_quarter()

    def table(values):
        block = jnp.stack(by_quarter(group_exchange(values, quarter), quarter))
        return lax.all_gather(block, "dp", axis_index_groups=groups, axis=0, tiled=False)

    cells_all = jnp.stack(group_exchange(cells, quarter))
    embed_all = table(embed)
    rows, genes = cells.shape[1:]
    embedded = low(across(cells_all.reshape(-1, genes), embed_all.reshape(-1, genes)))
    embedded = group_scatter(embedded.reshape(GROUP, rows, -1))
    middle = [lax.all_gather(v, AXES, axis=0, tiled=False) for v in own]
    return [cells_all, embed_all, table(decoder)] + middle + [embedded]


def shards(
    cells,
    coordinates,
    slide_ids,
    live_mask,
    components,
    noise,
    ramp_weight,
    embed_weight,
    query_key_value,
    output_weight,
    up_weight,
    up_bias,
    down_weight,
    down_bias,
    first_gain,
    first_shift,
    second_gain,
    second_shift,
    encoder_weight,
    encoder_bias,
    prior_mean,
    prior_logvar,
    decoder_weight,
):
    row_count = cells.shape[0]
    devices = device_total()
    total = devices // GROUP
    me = device_index()
    quarter = me % GROUP
    rows = embed_weight.shape[0]
    thin = decoder_weight.shape[0]
    cell_total = row_count * devices
    live = live_mask[0].astype(jnp.float32)
    slides = slide_ids[0]
    places = jnp.arange(row_count)
    allowed = (slides[:, None] == slides[None, :]) & (
        (live[None, :] > 0.5) | (places[:, None] == places[None, :])
    )
    onehot = (
        components[:, None] == jnp.arange(prior_mean.shape[0], dtype=jnp.int32)[None, :]
    ).astype(jnp.float32)

    kinds = prior_mean.shape[0]
    vectors = [down_bias, first_gain, first_shift, second_gain, second_shift, encoder_bias]
    lone = jnp.full((1,), jnp.sum(live), jnp.bfloat16)
    small = jnp.concatenate(
        [
            jnp.pad(v, ((0, 0), (0, 128 - v.shape[1])))
            for v in [prior_mean, prior_logvar]
            + [v.reshape(1, -1) for v in [up_bias] + vectors + [lone]]
        ]
    )
    small = jnp.pad(small, ((0, 48 - small.shape[0]), (0, 0)))
    gather = gather_weights if total <= NARROW else gather_plain
    cells_group, embed_cols, decoder_cols, *middle, embedded = gather(
        gene_chunks(cells),
        gene_chunks(embed_weight),
        gene_chunks(decoder_weight),
        query_key_value,
        small,
        output_weight,
        encoder_weight,
        up_weight,
        down_weight,
    )
    embed_cols = embed_cols.reshape(-1, CHUNK)
    decoder_cols = decoder_cols.reshape(-1, CHUNK)
    middle = [full.reshape(-1, full.shape[-1]) for full in middle]
    joint_full, small_full, output_full, encoder_full, up_full, down_full = middle
    small_full = wide(small_full.reshape(devices, 48, 128))
    up_bias_full = small_full[:, 2 * kinds, : 4 * rows].reshape(1, -1)
    vectors = small_full[:, 2 * kinds + 1 : 2 * kinds + 7, :rows].transpose(1, 0, 2).reshape(6, D)
    down_bias_full, gain_first, shift_first, gain_second, shift_second, encoder_bias_full = vectors
    prior_full = small_full[:, : 2 * kinds, : prior_mean.shape[1]]
    prior_full = prior_full.transpose(1, 0, 2).reshape(2 * kinds, LATENT)
    prior_mean_full, prior_logvar_full = prior_full[:kinds], prior_full[kinds:]
    count = jnp.sum(small_full[:, 2 * kinds + 7, 0])

    start_state = embedded + positions(coordinates)
    normed_first = layer_norm(start_state, gain_first, shift_first).astype(jnp.bfloat16)
    joint = matmul(normed_first, joint_full).astype(jnp.bfloat16)
    context, logsum = attention_forward(joint, allowed)
    middle_state = start_state + matmul(context, output_full)
    normed_second = layer_norm(middle_state, gain_second, shift_second).astype(jnp.bfloat16)
    pre = matmul(normed_second, up_full) + up_bias_full
    active = jax.nn.gelu(pre, approximate=True).astype(jnp.bfloat16)
    end_state = middle_state + (matmul(active, down_full) + down_bias_full)
    end_low = end_state.astype(jnp.bfloat16)
    encoded = matmul(end_low, encoder_full) + encoder_bias_full
    latent_mean = encoded[:, :LATENT]
    latent_logvar = encoded[:, LATENT:]
    latent = (latent_mean + jnp.exp(0.5 * latent_logvar) * noise).astype(jnp.bfloat16)
    center = jnp.dot(onehot, prior_mean_full, precision=lax.Precision.HIGHEST)
    scale = jnp.dot(onehot, prior_logvar_full, precision=lax.Precision.HIGHEST)
    gap = latent_mean - center
    inverse = jnp.exp(-scale)
    grown = jnp.exp(latent_logvar)
    diverge = 0.5 * (scale - latent_logvar + (grown + gap * gap) * inverse - 1.0)
    ratio = cell_total / count
    spread = jnp.broadcast_to(jnp.sum(live[:, None] * diverge, axis=0, keepdims=True), (8, LATENT))
    message = jnp.concatenate(
        [latent, jnp.broadcast_to(low(live)[:, None], (row_count, 128))], axis=1
    )
    latent_pass = latent_step if total <= NARROW else latent_plain
    recon_grad, decoder_term, latent_grad, spread_sum, recon_sum = latent_pass(
        message, spread, ratio.reshape(1, 1), decoder_cols, cells_group
    )
    kl_mean = spread_sum[0] / count
    shifted = (kl_mean - FREE_FLOOR) / FREE_TEMP
    free = FREE_FLOOR + FREE_TEMP * jax.nn.softplus(shifted)
    latent_grad = wide(low(latent_grad))

    kl_scale = ratio * ramp_weight * jax.nn.sigmoid(shifted)[None, :] * live[:, None]
    pulled = kl_scale * gap * inverse
    mean_grad = latent_grad + pulled
    logvar_grad = latent_grad * 0.5 * jnp.exp(0.5 * latent_logvar) * noise + kl_scale * 0.5 * (
        grown * inverse - 1.0
    )
    encoded_grad = jnp.concatenate([mean_grad, logvar_grad], axis=1).astype(jnp.bfloat16)
    prior_mean_grad = jnp.dot(onehot.T, -pulled, precision=lax.Precision.HIGHEST)
    prior_logvar_grad = jnp.dot(
        onehot.T,
        kl_scale * 0.5 * (1.0 - (grown + gap * gap) * inverse),
        precision=lax.Precision.HIGHEST,
    )
    end_grad = across(encoded_grad, encoder_full)
    branch_grad = end_grad.astype(jnp.bfloat16)
    encoder_bias_grad = jnp.sum(encoded_grad.astype(jnp.float32), axis=0)
    down_bias_grad = jnp.sum(branch_grad.astype(jnp.float32), axis=0)
    active_grad = across(branch_grad, down_full)
    gelu_value, gelu_back = jax.vjp(lambda value: jax.nn.gelu(value, approximate=True), pre)
    pre_grad = gelu_back(active_grad)[0].astype(jnp.bfloat16)
    up_bias_grad = jnp.sum(pre_grad.astype(jnp.float32), axis=0)
    second_out_grad = across(pre_grad, up_full)
    norm_value, second_back = jax.vjp(layer_norm, middle_state, gain_second, shift_second)
    state_part, second_gain_grad, second_shift_grad = second_back(second_out_grad)
    middle_grad = end_grad + state_part
    attend_grad = middle_grad.astype(jnp.bfloat16)
    context_grad = across(attend_grad, output_full).astype(jnp.bfloat16)
    joint_grad = attention_backward(joint, allowed, logsum, context_grad)
    first_out_grad = across(joint_grad, joint_full)
    first_value, first_back = jax.vjp(layer_norm, start_state, gain_first, shift_first)
    start_part, first_gain_grad, first_shift_grad = first_back(first_out_grad)
    start_grad = middle_grad + start_part
    start_low = start_grad.astype(jnp.bfloat16)
    vectors = [
        up_bias_grad,
        down_bias_grad,
        first_gain_grad,
        first_shift_grad,
        second_gain_grad,
        second_shift_grad,
        encoder_bias_grad,
    ]
    priors = jnp.concatenate([prior_mean_grad, prior_logvar_grad])
    priors = priors.reshape(2 * kinds, devices, -1).transpose(1, 0, 2).reshape(devices, -1)
    prior_size = priors.shape[1]
    packed = jnp.concatenate([v.reshape(devices, -1) for v in vectors] + [priors], axis=1)
    packed = jnp.pad(packed, ((0, 0), (0, 1024 - packed.shape[1])))
    packed = packed.reshape(total, 2, 2, 8, 128)

    scatter = scatter_sums if total <= NARROW else scatter_plain
    embed_grad, decoder_grad, cells_grad, *middle_grads, small_sum, recon_total = scatter(
        [
            (normed_first, joint_grad),
            (context, attend_grad),
            (end_low, encoded_grad),
            (normed_second, pre_grad),
            (active, branch_grad),
        ],
        start_low,
        decoder_term.reshape(total, GROUP, thin, CHUNK),
        cells_group,
        embed_cols,
        recon_grad,
        packed,
        recon_sum,
    )

    def all_genes(chunks):
        return chunks.transpose(1, 0, 2).reshape(chunks.shape[1], -1)[:, :GENES]

    cells_grad = all_genes(cells_grad)
    embed_grad = wide(all_genes(embed_grad))
    decoder_grad = wide(all_genes(decoder_grad))
    (
        joint_weight_grad,
        output_weight_grad,
        encoder_weight_grad,
        up_weight_grad,
        down_weight_grad,
    ) = middle_grads

    ends = [0]
    for vector in vectors:
        ends.append(ends[-1] + vector.shape[0] // devices)
    packed = small_sum.reshape(-1)
    vector_grads = [packed[ends[i] : ends[i + 1]] for i in range(len(vectors))]
    prior_out = packed[ends[-1] : ends[-1] + prior_size].reshape(2, kinds, -1)
    recon_total = 0.5 * jnp.sum(recon_total)
    loss = (recon_total / count + ramp_weight * jnp.sum(free)) / GENES
    return (
        loss,
        cells_grad,
        embed_grad,
        joint_weight_grad,
        output_weight_grad,
        up_weight_grad,
        vector_grads[0],
        down_weight_grad,
        vector_grads[1],
        vector_grads[2],
        vector_grads[3],
        vector_grads[4],
        vector_grads[5],
        encoder_weight_grad,
        vector_grads[6],
        prior_out[0],
        prior_out[1],
        decoder_grad,
    )


def solution(mesh):
    in_specs = (
        P(("dp", "fsdp"), None),
        P(None, ("dp", "fsdp")),
        P(("dp", "fsdp"), None),
        P(("dp", "fsdp"), None),
        P(("dp", "fsdp")),
        P(("dp", "fsdp"), None),
        P(),
        P(("dp", "fsdp"), None),
        P(("dp", "fsdp"), None),
        P(("dp", "fsdp"), None),
        P(("dp", "fsdp"), None),
        P(("dp", "fsdp")),
        P(("dp", "fsdp"), None),
        P(("dp", "fsdp")),
        P(("dp", "fsdp")),
        P(("dp", "fsdp")),
        P(("dp", "fsdp")),
        P(("dp", "fsdp")),
        P(("dp", "fsdp"), None),
        P(("dp", "fsdp")),
        P(None, ("dp", "fsdp")),
        P(None, ("dp", "fsdp")),
        P(("dp", "fsdp"), None),
    )
    out_specs = (
        P(),
        P(("dp", "fsdp"), None),
        P(("dp", "fsdp"), None),
        P(("dp", "fsdp"), None),
        P(("dp", "fsdp"), None),
        P(("dp", "fsdp"), None),
        P(("dp", "fsdp")),
        P(("dp", "fsdp"), None),
        P(("dp", "fsdp")),
        P(("dp", "fsdp")),
        P(("dp", "fsdp")),
        P(("dp", "fsdp")),
        P(("dp", "fsdp")),
        P(("dp", "fsdp"), None),
        P(("dp", "fsdp")),
        P(None, ("dp", "fsdp")),
        P(None, ("dp", "fsdp")),
        P(("dp", "fsdp"), None),
    )
    return jax.shard_map(shards, mesh=mesh, in_specs=in_specs, out_specs=out_specs, check_vma=False)
```

```python
import functools
import math

import jax
import jax.numpy as jnp
from jax import lax
from jax.experimental import pallas as pl
from jax.experimental.pallas import tpu as pltpu
from jax.sharding import PartitionSpec as P

D = 1024
HEAD_DIM = 64
GENES = 13500
LATENT = 512


NEG_SCORE = -1000000000.0
NORM_EPS = 1e-05
FREE_FLOOR = 1.0
FREE_TEMP = 0.25


def layer_norm(hidden, gain, shift):
    center = hidden - jnp.mean(hidden, axis=-1, keepdims=True)
    spread = jnp.mean(center * center, axis=-1, keepdims=True)
    return center * lax.rsqrt(spread + NORM_EPS) * gain + shift


def positions(coordinates):
    quarter = D // 4
    frequency = jnp.exp(jnp.arange(quarter, dtype=jnp.float32) * (-math.log(10000.0) / quarter))
    angle_x = coordinates[0][:, None] * frequency[None, :]
    angle_y = coordinates[1][:, None] * frequency[None, :]
    return jnp.concatenate(
        [jnp.sin(angle_x), jnp.cos(angle_x), jnp.sin(angle_y), jnp.cos(angle_y)], axis=1
    )


def matmul(left, right):
    return jnp.dot(left, right, preferred_element_type=jnp.float32)


def across(left, right):
    return lax.dot_general(
        left, right, (((1,), (1,)), ((), ())), preferred_element_type=jnp.float32
    )


def contract_rows(left, right):
    return lax.dot_general(
        left, right, (((0,), (0,)), ((), ())), preferred_element_type=jnp.float32
    )


def split_heads(joint):
    row_count = joint.shape[0]
    queries = joint[:, :D].reshape(row_count, -1, HEAD_DIM)
    keys = joint[:, D : 2 * D].reshape(row_count, -1, HEAD_DIM)
    values = joint[:, 2 * D :].reshape(row_count, -1, HEAD_DIM)
    return (queries, keys, values)


def masked_scores(queries, keys, allowed):
    scores = jnp.einsum(
        "qhd,khd->hqk", queries, keys, preferred_element_type=jnp.float32
    ) * HEAD_DIM ** (-0.5)
    return jnp.where(allowed[None], scores, NEG_SCORE)


def attention_forward(joint, allowed):
    queries, keys, values = split_heads(joint)
    masked = masked_scores(queries, keys, allowed)
    peak = jnp.max(masked, axis=-1, keepdims=True)
    raised = jnp.exp(masked - peak)
    denom = jnp.sum(raised, axis=-1, keepdims=True)
    probs = raised / denom
    logsum = peak + jnp.log(denom)
    context = jnp.einsum(
        "hqk,khd->qhd", probs.astype(jnp.bfloat16), values, preferred_element_type=jnp.float32
    )
    return (context.reshape(joint.shape[0], D).astype(jnp.bfloat16), logsum)


def attention_backward(joint, allowed, logsum, context_grad):
    row_count = joint.shape[0]
    queries, keys, values = split_heads(joint)
    probs = jnp.exp(masked_scores(queries, keys, allowed) - logsum)
    probs_low = probs.astype(jnp.bfloat16)
    incoming = context_grad.reshape(row_count, -1, HEAD_DIM)
    value_grad = jnp.einsum("hqk,qhd->khd", probs_low, incoming, preferred_element_type=jnp.float32)
    prob_grad = jnp.einsum("qhd,khd->hqk", incoming, values, preferred_element_type=jnp.float32)
    score_grad = (probs * (prob_grad - jnp.sum(probs * prob_grad, axis=-1, keepdims=True))).astype(
        jnp.bfloat16
    )
    query_grad = jnp.einsum(
        "hqk,khd->qhd", score_grad, keys, preferred_element_type=jnp.float32
    ) * HEAD_DIM ** (-0.5)
    key_grad = jnp.einsum(
        "hqk,qhd->khd", score_grad, queries, preferred_element_type=jnp.float32
    ) * HEAD_DIM ** (-0.5)
    return jnp.concatenate(
        [
            query_grad.reshape(row_count, D),
            key_grad.reshape(row_count, D),
            value_grad.reshape(row_count, D),
        ],
        axis=1,
    ).astype(jnp.bfloat16)

AXES = ("dp", "fsdp")
GROUP = 4
CHUNK = 3456
SLICE = 384
NARROW = 8


def low(values):
    return values.astype(jnp.bfloat16)


def wide(values):
    return values.astype(jnp.float32)


def device_total():
    return lax.axis_size("dp") * lax.axis_size("fsdp")


def device_index():
    return lax.axis_index("dp") * lax.axis_size("fsdp") + lax.axis_index("fsdp")


def swap(values, mask):
    return lax.ppermute(values, AXES, [(i, i ^ mask) for i in range(device_total())])


def same_quarter():
    return [[d for d in range(lax.axis_size("dp")) if d % 2 == odd] for odd in range(2)]


def pick(blocks, index):
    return lax.dynamic_index_in_dim(blocks, index, 0, keepdims=False)


def group_exchange(blocks, quarter):
    return [pick(blocks, quarter)] + [swap(pick(blocks, quarter ^ m), m) for m in range(1, GROUP)]


def group_gather(values):
    pair = jnp.stack([values, swap(values, 2)])
    other = swap(pair, 1)
    return jnp.stack([pair[0], other[0], pair[1], other[1]])


def group_scatter(parts):
    mine = jnp.stack([parts[0], parts[2]])
    theirs = low(jnp.stack([parts[1], parts[3]]))
    summed = wide(mine) + wide(swap(theirs, 1))
    return summed[0] + wide(swap(low(summed[1]), 2))


def by_quarter(pieces, quarter):
    stacked = jnp.stack(pieces)
    return [pick(stacked, quarter ^ j) for j in range(GROUP)]


def gene_chunks(values):
    padded = jnp.pad(values, ((0, 0), (0, GROUP * CHUNK - GENES)))
    return jnp.stack([padded[:, j * CHUNK : (j + 1) * CHUNK] for j in range(GROUP)])


def sum_all(values):
    mask = 1
    while mask < device_total():
        values = values + swap(values, mask)
        mask *= 2
    return values


MESH = pl.DeviceIdType.MESH


class Where:
    def __init__(self, total):
        dp = lax.axis_index("dp")
        self.total = total
        self.core = lax.axis_index("fsdp")
        self.x = dp % 2
        self.t = dp // 2
        self.quarter = 2 * self.x + self.core
        y, z = self.t % 2, self.t // 2
        self.k = z + y * (total - 1 - 2 * z)
        self.right = (2 * self.owner(-1) + self.x, self.core)
        self.left = (2 * self.owner(1) + self.x, self.core)
        self.peers = [
            None,
            (dp, 1 - self.core),
            (2 * self.t + 1 - self.x, self.core),
            (2 * self.t + 1 - self.x, 1 - self.core),
        ]
        self.quarters = [
            self.quarter,
            2 * self.x + 1 - self.core,
            2 * (1 - self.x) + self.core,
            2 * (1 - self.x) + 1 - self.core,
        ]

    def owner(self, step):
        place = (self.k - step + self.total) % self.total
        y = place // (self.total // 2)
        return 2 * (place + y * (self.total - 1 - 2 * place)) + y

    def same(self, step):
        t = (self.t + step) % self.total
        return t, (2 * t + self.x, self.core)

    def meet(self, everyone=False):
        barrier = pltpu.get_barrier_semaphore()
        others = self.peers[1:]
        if everyone:
            others = others + [self.same(step)[1] for step in range(1, self.total)]
        else:
            others = others + [self.right, self.left]
        for other in others:
            pl.semaphore_signal(barrier, inc=1, device_id=other, device_id_type=MESH)
        pl.semaphore_wait(barrier, len(others))


class Copies:
    def __init__(self, send_sems, recv_sems, local_sems):
        self.send_sems, self.recv_sems, self.local_sems = send_sems, recv_sems, local_sems
        self.remote_count = self.local_count = 0
        self.sent = []

    def send(self, source, target, device):
        at = self.remote_count
        self.remote_count += 1
        copy = pltpu.make_async_remote_copy(
            source,
            target,
            self.send_sems.at[at],
            self.recv_sems.at[at],
            device_id=device,
            device_id_type=MESH,
        )
        copy.start()
        self.sent.append(copy)
        return copy

    def local(self, source, target):
        at = self.local_count
        self.local_count += 1
        copy = pltpu.make_async_copy(source, target, self.local_sems.at[at])
        copy.start()
        return copy

    def free(self, copy):
        copy.wait_send()
        self.sent = [other for other in self.sent if other is not copy]

    def finish(self):
        for copy in self.sent:
            copy.wait_send()


def gather_kernel(total, *refs):
    (cells, embed, decoder, joint, small, output, encoder, up, down) = refs[:9]
    (cells_all, embed_all, decoder_all, joint_all, small_all) = refs[9:14]
    (output_all, encoder_all, up_all, down_all, embedded) = refs[14:19]
    (held_cells, held_embed, partial, other_core, for_x, other_x) = refs[19:25]
    here = Where(total)
    copies = Copies(*refs[25:])
    here.meet()
    t, x, core = here.t, here.x, here.core
    last = total - 1
    towards = {1: here.right, -1: here.left}
    flying = {}

    late = [(up, up_all, 1), (output, output_all, 1), (down, down_all, -1), (encoder, encoder_all, -1)]
    shares = {
        name: [
            copies.send(own.at[here.quarters[m]], full.at[t, here.quarter], here.peers[m])
            for m in (2, 3, 1)
        ]
        for name, own, full in (("embed", embed, embed_all), ("decoder", decoder, decoder_all))
    }
    for n, (own, full, way) in enumerate(late):
        flying["late", n] = copies.send(own, full.at[t, x, core], towards[way])
    across_x = [copies.send(own, full.at[t, x, core], here.peers[2]) for own, full, _ in late]
    own_cells = copies.local(cells.at[here.quarter], cells_all.at[0])
    cell_moves = [
        copies.send(cells.at[here.quarters[m]], cells_all.at[m], here.peers[m]) for m in (2, 3, 1)
    ]
    shares["early"] = [
        copies.send(own, full.at[t, x, core], here.peers[2])
        for own, full in ((joint, joint_all), (small, small_all))
    ]
    own_copies = {
        "embed": [copies.local(embed.at[here.quarter], embed_all.at[t, here.quarter])],
        "decoder": [copies.local(decoder.at[here.quarter], decoder_all.at[t, here.quarter])],
        "early": [
            copies.local(own, full.at[t, x, core])
            for own, full in ((joint, joint_all), (small, small_all))
        ],
    }
    own_late = [copies.local(own, full.at[t, x, core]) for own, full, _ in late]

    def late_step(s):
        for n, (_, full, way) in enumerate(late):
            flying["late", n].wait_recv()
            block = full.at[here.owner(way * s), x, core]
            if s < last:
                flying["late", n] = copies.send(block, block, towards[way])
            across_x.append(copies.send(block, block, here.peers[2]))

    def early_block(full, way, s):
        return full.at[here.owner(way * s), 0 if way == 1 else 1, core]

    def table_block(full, way, s):
        return full.at[here.owner(way * s), pl.ds(0 if way == 1 else 2, 2)]

    rings = {
        "embed": [(embed_all, way, table_block) for way in (1, -1)],
        "decoder": [(decoder_all, way, table_block) for way in (1, -1)],
        "early": [(full, way, early_block) for full in (joint_all, small_all) for way in (1, -1)],
    }

    def step(name, s):
        if s == 0:
            for copy in own_copies[name]:
                copy.wait()
            for copy in shares[name]:
                copy.wait_recv()
        for n, (full, way, block_of) in enumerate(rings[name]):
            if s > 0:
                flying[name, n].wait_recv()
            if s < last:
                block = block_of(full, way, s)
                flying[name, n] = copies.send(block, block, towards[way])

    holds = {}

    def hold(block):
        holds[block] = copies.local(embed_all.at[block], held_embed.at[block % 2])

    def multiply(block):
        holds[block].wait()
        features = held_embed.shape[1] * held_embed.shape[2]
        table = held_embed[block % 2].reshape(features, held_embed.shape[3])
        for row in range(2):
            for column in range(2):
                partial[row, column, :, pl.ds(block * features, features)] = low(
                    across(held_cells[2 * row + column], table)
                )
        if block + 2 < total:
            hold(block + 2)

    across_core = []

    def to_core(copies_of, block_of):
        for copy, (_, full, way) in zip(copies_of, late):
            copy.wait_recv()
            block = block_of(full, way)
            across_core.append(copies.send(block, block, here.peers[1]))

    def crossed(s):
        to_core(
            across_x[len(late) * s : len(late) * (s + 1)],
            lambda full, way: full.at[here.owner(way * s), 1 - x, core],
        )

    for s in range(1, last + 1):
        late_step(s)
        if s == 1:
            step("embed", 0)
        step("embed", s)
        if s == last - 1:
            step("early", 0)
            step("decoder", 0)
    hold(0)
    hold(1)
    for copy in own_late:
        copy.wait()
    for _, full, _ in late:
        block = full.at[:, x, core]
        across_core.append(copies.send(block, block, here.peers[1]))
    for copy in cell_moves:
        copy.wait_recv()
    own_cells.wait()
    held = copies.local(cells_all, held_cells)
    step("early", 1)
    step("decoder", 1)
    held.wait()
    for s in range(2, last + 1):
        multiply(s - 2)
        step("early", s)
        step("decoder", s)
        crossed(s - 2)
    for block in range(last - 1, total):
        multiply(block)
    sums = copies.send(partial.at[:, 1], other_core, here.peers[1])
    for full in (joint_all, small_all):
        block = full.at[:, :, core]
        across_core.append(copies.send(block, block, here.peers[1]))
    sums.wait_recv()
    for_x[...] = low(wide(partial[1, 0]) + wide(other_core[1]))
    sums = copies.send(for_x, other_x, here.peers[2])
    for s in range(last - 1, total):
        crossed(s)
    sums.wait_recv()
    embedded[...] = wide(partial[0, 0]) + wide(other_core[0]) + wide(other_x[...])
    for copy in across_core:
        copy.wait_recv()
    copies.finish()


def gather_weights(cells, embed, decoder, joint, small, output, encoder, up, down):
    total = device_total() // GROUP
    own = [joint, small, output, encoder, up, down]
    tables = [embed, decoder]
    operands = [cells] + tables + own
    shapes = (
        [cells.shape]
        + [(total,) + v.shape for v in tables]
        + [(total, 2, 2) + v.shape for v in own]
    )
    remote = 15 + 12 * (total - 1) + 8 * total + 8
    cell_rows, genes = cells.shape[1:]
    features = total * GROUP * embed.shape[1]
    buffers = [
        cells.shape,
        (2,) + embed.shape,
        (2, 2, cell_rows, features),
        (2, cell_rows, features),
        (cell_rows, features),
        (cell_rows, features),
    ]
    return pl.pallas_call(
        functools.partial(gather_kernel, total),
        out_shape=[jax.ShapeDtypeStruct(s, jnp.bfloat16) for s in shapes]
        + [jax.ShapeDtypeStruct((cell_rows, features), jnp.float32)],
        in_specs=[pl.BlockSpec(memory_space=pl.ANY)] * len(operands),
        out_specs=[pl.BlockSpec(memory_space=pl.ANY)] * len(operands)
        + [pl.BlockSpec(memory_space=pltpu.VMEM)],
        scratch_shapes=[pltpu.VMEM(shape, jnp.bfloat16) for shape in buffers]
        + [
            pltpu.SemaphoreType.DMA((remote,)),
            pltpu.SemaphoreType.DMA((remote,)),
            pltpu.SemaphoreType.DMA((10 + total,)),
        ],
        compiler_params=pltpu.CompilerParams(
            collective_id=1, has_side_effects=True, vmem_limit_bytes=20 * 2**20
        ),
        name="gather_weights",
    )(*operands)


def add_rows(target, first, second, dtype):
    rows, columns = target.shape
    step = min(rows, 16 if columns > 2048 else 32)

    @pl.loop(0, rows // step)
    def _(i):
        part = pl.ds(pl.multiple_of(i * step, step), step)
        target[part, :] = (wide(first[part, :]) + wide(second[part, :])).astype(dtype)


def product(target, left, right, accumulate):
    total, _, rows, columns = target.shape
    step = 256 // (2 * rows)
    width = 512

    @pl.loop(0, total // step)
    def _(i):
        blocks = pl.ds(i * step, step)
        part = left(i * 2 * step, 2 * step)

        @pl.loop(0, columns // width)
        def _(n):
            across_columns = pl.ds(pl.multiple_of(n * width, width), width)
            value = matmul(part, right[:, across_columns]).reshape(step, 2, rows, width)
            if accumulate:
                value = value + wide(target[blocks, :, :, across_columns])
            target[blocks, :, :, across_columns] = low(value)


MIDDLE = ("joint", "output", "encoder", "up", "down")


def scatter_kernel(total, *refs):
    (recon, start, small, decoder, cells, table, grads) = refs[:7]
    left = dict(zip(MIDDLE, refs[7:12]))
    right = dict(zip(MIDDLE, refs[12:17]))
    (embed_out, decoder_out, cells_out, embed, back) = refs[17:22]
    results = dict(zip(MIDDLE, refs[22:27]))
    (small_out, recon_out) = refs[27:29]
    (chip_small, stage_small, sum_small, hop_small, group_recon, all_recon) = refs[29:35]
    chip = dict(zip(MIDDLE, refs[35:40]))
    (send_up, send_down) = refs[40:42]
    sums = dict(zip(MIDDLE[1:], refs[42:46]))
    (hop_embed, hop_decoder, hop_joint) = refs[46:49]
    hops_of = dict(zip(MIDDLE[1:], refs[49:53]))
    (local_embed, local_decoder) = refs[53:55]
    (other_joint, starts, turned) = refs[55:58]
    (in_cells, in_table, in_grads, out_term, out_back, blocks) = refs[58:64]
    here = Where(total)
    copies = Copies(*refs[64:67])
    stream_sems = refs[67]
    here.meet()
    x, core, last = here.x, here.core, total - 1
    towards = {1: here.right, -1: here.left}
    flying = {}

    def lanes(term, hops, local):
        return [(term, hops, local, way, side) for side, way in ((0, 1), (1, -1))]

    tables = {
        "embed": lanes(embed, hop_embed, local_embed),
        "decoder": lanes(decoder, hop_decoder, local_decoder),
    }

    def table_block(term, way, side, h):
        return term.at[here.owner(way * h), pl.ds(2 * side, 2)]

    def fetch(name, h):
        for n, (term, _, local, way, side) in enumerate(tables[name]):
            flying["local", name, n, h] = copies.local(
                table_block(term, way, side, h + 1), local.at[h % 2, side]
            )

    def table_start(name):
        for n, (term, hops, _, way, side) in enumerate(tables[name]):
            flying[name, n] = copies.send(
                table_block(term, way, side, 1), hops.at[0, side], towards[way]
            )
        fetch(name, 1)
        fetch(name, 2)

    def table_hop(name, h):
        for n, (_, hops, local, way, side) in enumerate(tables[name]):
            flying[name, n].wait_recv()
            flying["local", name, n, h].wait()
            for row in range(2):
                arrived = hops.at[h - 1, side, row]
                add_rows(arrived, arrived, local.at[h % 2, side, row], jnp.bfloat16)
            if h < last:
                flying[name, n] = copies.send(hops.at[h - 1, side], hops.at[h, side], towards[way])
        if h + 2 <= last:
            fetch(name, h + 2)

    table_start("decoder")
    moves = [copies.send(start, starts.at[m], here.peers[m]) for m in (2, 1)]
    starts[0] = start[...]
    group_recon[here.quarter] = recon[...]
    recons = [copies.send(recon, group_recon.at[here.quarter], here.peers[m]) for m in (2, 3, 1)]
    halves = {"small": copies.send(small.at[:, :, 1 - core], chip_small, here.peers[1])}
    own_small = copies.local(small.at[:, :, core], stage_small)

    def half(name, which):
        source = left[name]
        if results[name].shape[0] == 128:

            def wide_blocks(first, size):
                lanes = [
                    pl.ds(pl.multiple_of((2 * (first + n) + which) * 128, 128), 128)
                    for n in range(size)
                ]
                return jnp.concatenate([low(wide(source[:, part]).T) for part in lanes])

            return wide_blocks
        blocks[...] = low(wide(source[...]).T).reshape(blocks.shape)

        def narrow_blocks(first, size):
            return blocks[pl.ds(first, size), which].reshape(-1, blocks.shape[-1])

        return narrow_blocks

    def give(name, buffer):
        product(buffer, half(name, 1 - core), right[name], False)
        halves[name] = copies.send(buffer, chip[name], here.peers[1])

    across = {}

    def cross(name, held, target):
        across[name] = copies.send(held.at[:, 1 - x], target, here.peers[2])

    def take(name):
        halves[name].wait_recv()
        product(chip[name], half(name, core), right[name], True)
        if name in sums:
            cross(name, chip[name], sums[name])

    give("up", send_up)
    give("down", send_down)
    moves[0].wait_recv()
    moves[0] = copies.send(starts.at[2], starts.at[3], here.peers[1])
    table_hop("decoder", 1)
    take("up")
    copies.free(halves["up"])
    give("joint", send_up.at[:, :, :, pl.ds(0, right["joint"].shape[1])])
    table_hop("decoder", 2)
    take("down")
    copies.free(halves["down"])
    slim = results["output"].shape[0]
    give("output", send_down.at[:, :, pl.ds(0, slim)])
    give("encoder", send_down.at[:, :, pl.ds(slim, slim)])
    table_hop("decoder", 3)
    take("joint")
    for side, way in ((0, 1), (1, -1)):
        flying["joint", side] = copies.send(
            chip["joint"].at[here.owner(way), side], hop_joint.at[0, side], towards[way]
        )
    take("output")
    take("encoder")
    own_small.wait()
    halves["small"].wait_recv()

    @pl.loop(0, total)
    def _(t):
        for side in range(2):
            held = chip_small.at[t, side]
            add_rows(held, held, stage_small.at[t, side], jnp.float32)

    cross("small", chip_small, sum_small)
    for copy in recons:
        copy.wait_recv()
    all_recon[here.t] = group_recon[0] + group_recon[1] + group_recon[2] + group_recon[3]
    own_recon = all_recon.at[here.t]
    flying["recon"] = copies.send(own_recon, own_recon, here.right)
    table_hop("decoder", 4)

    def joint_hop(h):
        for side, way in ((0, 1), (1, -1)):
            flying["joint", side].wait_recv()
            arrived = hop_joint.at[h - 1, side]
            local = chip["joint"].at[here.owner(way * (h + 1)), side]
            add_rows(arrived, arrived, local, jnp.bfloat16)
            if h < last:
                flying["joint", side] = copies.send(arrived, hop_joint.at[h, side], towards[way])

    for copy in moves:
        copy.wait_recv()
    moves = []
    rows, rows_of_t = start.shape[0], turned.shape[0] // total
    for m in range(GROUP):
        turned[:, m * rows : (m + 1) * rows] = low(wide(starts[m]).T)

    def moved(i, pairs, first):
        part = pl.ds(pl.multiple_of(i * SLICE, 128), SLICE)
        slot = i % 2
        return [
            pltpu.make_async_copy(*ends(part, slot), stream_sems.at[first + n, slot])
            for n, ends in enumerate(pairs)
        ]

    def loads_of(i):
        return moved(
            i,
            [
                lambda part, slot: (cells.at[:, :, part], in_cells.at[slot]),
                lambda part, slot: (table.at[:, part], in_table.at[slot]),
                lambda part, slot: (grads.at[:, :, part], in_grads.at[slot]),
            ],
            0,
        )

    def stores_of(i):
        return moved(
            i,
            [
                lambda part, slot: (out_term.at[slot], embed.at[:, :, :, part]),
                lambda part, slot: (out_back.at[slot], back.at[:, :, part]),
            ],
            3,
        )

    count = CHUNK // SLICE
    for copy in loads_of(0):
        copy.start()

    def stream(first, end):
        @pl.loop(first, end)
        def _(i):
            slot = i % 2
            @pl.when(i + 1 < count)
            def _():
                for copy in loads_of(i + 1):
                    copy.start()

            for copy in loads_of(i):
                copy.wait()

            @pl.when(i >= 2)
            def _():
                for copy in stores_of(i - 2):
                    copy.wait()

            for t in range(total):
                term = matmul(
                    turned[pl.ds(t * rows_of_t, rows_of_t), :],
                    in_cells[slot].reshape(GROUP * rows, SLICE),
                )
                out_term[slot, t] = low(term).reshape(out_term.shape[2:])
            for m in range(GROUP):
                out_back[slot, m] = low(matmul(starts[m], in_table[slot]) - wide(in_grads[slot, m]))
            for copy in stores_of(i):
                copy.start()

    joint_hop(1)
    stream(0, count // 3)
    table_hop("decoder", 5)
    joint_hop(2)
    stream(count // 3, 2 * count // 3)
    table_hop("decoder", 6)
    joint_hop(3)
    stream(2 * count // 3, count)
    for i in (count - 2, count - 1):
        for copy in stores_of(i):
            copy.wait()
    table_start("embed")
    moves = [copies.send(back.at[m], cells_out.at[here.quarter], here.peers[m]) for m in (2, 3, 1)]
    own = [copies.local(back.at[0], cells_out.at[here.quarter])]
    table_hop("decoder", last)

    def send_back(hops, out):
        done = [hops.at[last - 1, quarter // 2, quarter % 2] for quarter in here.quarters]
        for m in (2, 3, 1):
            moves.append(copies.send(done[m], out.at[here.quarter], here.peers[m]))
        own.append(copies.local(done[0], out.at[here.quarter]))

    send_back(hop_decoder, decoder_out)

    def recon_hop(h):
        flying["recon"].wait_recv()
        if h < last:
            arrived = all_recon.at[here.owner(h)]
            flying["recon"] = copies.send(arrived, arrived, here.right)

    late = [
        (name, sums[name], chip[name], hops_of[name], results[name], way)
        for name, way in (("up", 1), ("down", -1), ("output", 1), ("encoder", -1))
    ] + [("small", sum_small, chip_small, hop_small, small_out, 1)]

    def late_start():
        for name, summed, held, hops, _, way in late:
            across[name].wait_recv()

            @pl.loop(0, total)
            def _(t):
                add_rows(summed.at[t], summed.at[t], held.at[t, x], summed.dtype)

            flying["late", name] = copies.send(summed.at[here.owner(way)], hops.at[0], towards[way])

    def late_hop(h):
        for name, summed, _, hops, result, way in late:
            flying["late", name].wait_recv()
            local = summed.at[here.owner(way * (h + 1))]
            if h < last:
                add_rows(hops.at[h - 1], hops.at[h - 1], local, hops.dtype)
                flying["late", name] = copies.send(hops.at[h - 1], hops.at[h], towards[way])
            else:
                add_rows(result, hops.at[h - 1], local, jnp.float32)

    for h in range(1, last + 1):
        if h + 3 <= last:
            joint_hop(h + 3)
        table_hop("embed", h)
        recon_hop(h)
    send_back(hop_embed, embed_out)
    done_joint = hop_joint.at[last - 1]
    joint_move = copies.send(done_joint.at[1 - x], other_joint, here.peers[2])
    late_start()
    for h in range(1, last + 1):
        late_hop(h)
    summed = all_recon[0]
    for t in range(1, total):
        summed = summed + all_recon[t]
    recon_out[...] = summed
    joint_move.wait_recv()
    add_rows(results["joint"], done_joint.at[x], other_joint, jnp.float32)
    for copy in moves:
        copy.wait_recv()
    for copy in own:
        copy.wait()
    copies.finish()


def scatter_sums(pairs, start, decoder, cells, table, grads, small, recon):
    total = device_total() // GROUP
    last = total - 1
    rows, features = start.shape
    thin = jnp.bfloat16
    share = features // (total * GROUP)
    lefts, rights, shapes = [], [], []
    for before, after in pairs:
        block = before.shape[1] // device_total()
        lefts.append(before)
        rights.append(after)
        shapes.append((block, after.shape[1]))
    operands = [recon, start, small, decoder, cells, table, grads] + lefts + rights
    decoder_share = decoder.shape[1:]
    embed_share = (GROUP, share, CHUNK)
    out_shape = [
        jax.ShapeDtypeStruct(v, thin)
        for v in (embed_share, decoder_share, cells.shape, (total,) + embed_share, cells.shape)
    ]
    block = small.shape[3:]
    out_shape += [jax.ShapeDtypeStruct(v, jnp.float32) for v in shapes + [block, recon.shape]]
    exact = [(total, 2) + block, (total, 2) + block, (total,) + block, (last,) + block]
    exact += [(GROUP,) + recon.shape, (total,) + recon.shape]
    chips = [(total, 2) + v for v in shapes]
    buffers = chips + [chips[3], chips[4]] + [(total,) + v for v in shapes[1:]]
    buffers += [(last, 2, 2) + v[1:] for v in (embed_share, decoder_share)]
    buffers += [(last, 2) + shapes[0]] + [(last,) + v for v in shapes[1:]]
    buffers += [(2, 2, 2) + v[1:] for v in (embed_share, decoder_share)]
    buffers += [shapes[0], (GROUP,) + start.shape, (features, GROUP * rows)]
    buffers += [(2, GROUP, rows, SLICE), (2, features, SLICE), (2, GROUP, rows, SLICE)]
    buffers += [(2, total, GROUP, share, SLICE), (2, GROUP, rows, SLICE)]
    buffers += [(2 * total, 2, shapes[0][0], rows)]
    remote, here = 12 + 6 * last + 4 * last + 15 + 2 * last, 4 * last + 9
    anywhere, vmem = pl.BlockSpec(memory_space=pl.ANY), pl.BlockSpec(memory_space=pltpu.VMEM)
    outs = pl.pallas_call(
        functools.partial(scatter_kernel, total),
        out_shape=out_shape,
        in_specs=[vmem] * 2 + [anywhere] * 5 + [vmem] * 10,
        out_specs=[anywhere] * 5 + [vmem] * 7,
        scratch_shapes=[pltpu.VMEM(shape, jnp.float32) for shape in exact]
        + [pltpu.VMEM(shape, thin) for shape in buffers]
        + [
            pltpu.SemaphoreType.DMA((remote,)),
            pltpu.SemaphoreType.DMA((remote,)),
            pltpu.SemaphoreType.DMA((here,)),
            pltpu.SemaphoreType.DMA((5, 2)),
        ],
        compiler_params=pltpu.CompilerParams(
            collective_id=2, has_side_effects=True, vmem_limit_bytes=60 * 2**20
        ),
        name="scatter_sums",
    )(*operands)
    return outs[:3] + outs[5:]


def scatter_plain(pairs, start, decoder, cells, table, grads, small, recon):
    quarter = device_index() % GROUP
    total = device_total() // GROUP
    starts = group_gather(start).reshape(-1, start.shape[1])
    wide_cells = cells.reshape(-1, CHUNK)
    embed = low(contract_rows(starts, wide_cells)).reshape(total, GROUP, -1, CHUNK)
    back = low(matmul(starts, table) - wide(grads.reshape(-1, CHUNK))).reshape(cells.shape)

    def sent(blocks):
        pieces = [pick(blocks, 0)] + [swap(blocks[m], m) for m in range(1, GROUP)]
        return jnp.stack(by_quarter(pieces, quarter))

    def table_sum(term):
        block = lax.psum_scatter(
            term, "dp", axis_index_groups=same_quarter(), scatter_dimension=0, tiled=False
        )
        return sent(jnp.stack(by_quarter(list(block), quarter)))

    def middle(term):
        rows = term.reshape((device_total(), -1) + term.shape[-1:])
        return wide(lax.psum_scatter(rows, AXES, scatter_dimension=0, tiled=False))

    terms = [low(contract_rows(before, after)) for before, after in pairs]
    small = small.reshape((device_total(),) + small.shape[3:])
    return (
        [table_sum(embed), table_sum(decoder), sent(back)]
        + [middle(term) for term in terms]
        + [lax.psum_scatter(small, AXES, scatter_dimension=0, tiled=False), sum_all(recon)]
    )


def latent_kernel(total, *refs):
    (message, spread, ratio, decoder, cells) = refs[:5]
    (recon_grad, decoder_term, latent_grad, spread_sum, recon_sum) = refs[5:10]
    (latents, held_decoder, held_cells, held_grad, held_term, turned, partial) = refs[10:17]
    (leaving, arriving, group_spread, all_spread) = refs[17:21]
    here = Where(total)
    copies = Copies(*refs[21:])
    here.meet(everyone=True)
    arrivals = {m: copies.send(message, latents.at[m], here.peers[m]) for m in (1, 2, 3)}
    spreads = [copies.send(spread, group_spread.at[here.quarter], here.peers[m]) for m in (2, 3, 1)]
    loads = [
        copies.local(message, latents.at[0]),
        copies.local(decoder, held_decoder),
        copies.local(cells, held_cells),
    ]
    group_spread[here.quarter] = spread[...]
    for copy in spreads:
        copy.wait_recv()
    all_spread[here.t] = (
        group_spread[0] + group_spread[1] + group_spread[2] + group_spread[3]
    )
    spreads = []
    for away in range(1, total):
        own = all_spread.at[here.t]
        spreads.append(copies.send(own, own, here.same(away)[1]))
    for copy in loads:
        copy.wait()
    rows = message.shape[0]
    size = held_decoder.shape[0]
    partial[...] = jnp.zeros_like(partial)
    recon_sum[...] = jnp.zeros_like(recon_sum)

    both = 2 * rows

    def reconstruct(pair):
        at = pl.ds(2 * pair, 2)
        for m in (2 * pair, 2 * pair + 1):
            turned[:, m * rows : (m + 1) * rows] = low(wide(latents[m, :, :size]).T)
        values = latents[at, :, :size].reshape(both, size)
        live = wide(latents[at, :, size : size + 128]).reshape(both, 128)
        live = jnp.concatenate([live] * (SLICE // 128), axis=1)

        @pl.loop(0, CHUNK // SLICE)
        def _(i):
            part = pl.ds(pl.multiple_of(i * SLICE, 128), SLICE)
            table = held_decoder[:, part]
            miss = matmul(values, table) - wide(held_cells[at, :, part]).reshape(both, SLICE)
            weighted = live * miss
            recon_sum[...] += jnp.sum((weighted * miss).reshape(both // 8, 8, SLICE), axis=0)
            grad = low(ratio[0, 0] * weighted)
            held_grad[at, :, part] = grad.reshape(2, rows, SLICE)
            partial[at] += across(grad, table).reshape(2, rows, size)

    arrivals[1].wait_recv()
    reconstruct(0)
    leaving[1] = low(partial[1])
    returns = [copies.send(leaving.at[1], arriving.at[0], here.peers[1])]
    for m in (2, 3):
        arrivals[m].wait_recv()
    reconstruct(1)
    for m in (2, 3):
        leaving[m] = low(partial[m])
        returns.append(copies.send(leaving.at[m], arriving.at[m - 1], here.peers[m]))

    @pl.loop(0, CHUNK // SLICE)
    def _(i):
        part = pl.ds(pl.multiple_of(i * SLICE, 128), SLICE)
        grads = held_grad[:, :, part].reshape(GROUP * rows, SLICE)
        held_term[:, part] = low(matmul(turned[...], grads))

    stores = [copies.local(held_grad, recon_grad), copies.local(held_term, decoder_term)]
    for copy in spreads:
        copy.wait_recv()
    summed = all_spread[0]
    for t in range(1, total):
        summed = summed + all_spread[t]
    spread_sum[...] = summed
    for copy in returns:
        copy.wait_recv()
    latent_grad[...] = (
        (partial[0] + wide(arriving[0])) + (wide(arriving[1]) + wide(arriving[2]))
    )
    for copy in stores:
        copy.wait()
    copies.finish()


def latent_step(message, spread, ratio, decoder, cells):
    total = device_total() // GROUP
    rows, size = message.shape[0], decoder.shape[0]
    thin = jnp.bfloat16
    vmem = pl.BlockSpec(memory_space=pltpu.VMEM)
    anywhere = pl.BlockSpec(memory_space=pl.ANY)
    remote = 9 + total - 1
    return pl.pallas_call(
        functools.partial(latent_kernel, total),
        out_shape=[
            jax.ShapeDtypeStruct(cells.shape, thin),
            jax.ShapeDtypeStruct(decoder.shape, thin),
            jax.ShapeDtypeStruct((rows, size), jnp.float32),
            jax.ShapeDtypeStruct(spread.shape, jnp.float32),
            jax.ShapeDtypeStruct((8, SLICE), jnp.float32),
        ],
        in_specs=[vmem, vmem, pl.BlockSpec(memory_space=pltpu.SMEM), anywhere, anywhere],
        out_specs=[anywhere, anywhere, vmem, vmem, vmem],
        scratch_shapes=[
            pltpu.VMEM((GROUP,) + message.shape, thin),
            pltpu.VMEM(decoder.shape, thin),
            pltpu.VMEM(cells.shape, thin),
            pltpu.VMEM(cells.shape, thin),
            pltpu.VMEM(decoder.shape, thin),
            pltpu.VMEM((size, GROUP * rows), thin),
            pltpu.VMEM((GROUP, rows, size), jnp.float32),
            pltpu.VMEM((GROUP, rows, size), thin),
            pltpu.VMEM((GROUP - 1, rows, size), thin),
            pltpu.VMEM((GROUP,) + spread.shape, jnp.float32),
            pltpu.VMEM((total,) + spread.shape, jnp.float32),
            pltpu.SemaphoreType.DMA((remote,)),
            pltpu.SemaphoreType.DMA((remote,)),
            pltpu.SemaphoreType.DMA((5,)),
        ],
        compiler_params=pltpu.CompilerParams(
            collective_id=3, has_side_effects=True, vmem_limit_bytes=40 * 2**20
        ),
        name="latent_step",
    )(message, spread, ratio, decoder, cells)


def latent_plain(message, spread, ratio, decoder, cells):
    size = decoder.shape[0]
    gathered = group_gather(message).reshape(-1, message.shape[1])
    latents, live = gathered[:, :size], wide(gathered[:, size : size + 1])
    miss = matmul(latents, decoder) - wide(cells.reshape(-1, CHUNK))
    grad = low(ratio[0, 0] * live * miss)
    recon_sum = jnp.sum((live * miss * miss).reshape(-1, 8, CHUNK), axis=0)
    latent_grad = group_scatter(low(across(grad, decoder)).reshape(GROUP, -1, size))
    term = low(contract_rows(latents, grad))
    return grad.reshape(cells.shape), term, latent_grad, sum_all(spread), recon_sum


def gather_plain(cells, embed, decoder, *own):
    quarter = device_index() % GROUP
    total = device_total() // GROUP
    groups = same_quarter()

    def table(values):
        block = jnp.stack(by_quarter(group_exchange(values, quarter), quarter))
        return lax.all_gather(block, "dp", axis_index_groups=groups, axis=0, tiled=False)

    cells_all = jnp.stack(group_exchange(cells, quarter))
    embed_all = table(embed)
    rows, genes = cells.shape[1:]
    embedded = low(across(cells_all.reshape(-1, genes), embed_all.reshape(-1, genes)))
    embedded = group_scatter(embedded.reshape(GROUP, rows, -1))
    middle = [lax.all_gather(v, AXES, axis=0, tiled=False) for v in own]
    return [cells_all, embed_all, table(decoder)] + middle + [embedded]


def shards(
    cells,
    coordinates,
    slide_ids,
    live_mask,
    components,
    noise,
    ramp_weight,
    embed_weight,
    query_key_value,
    output_weight,
    up_weight,
    up_bias,
    down_weight,
    down_bias,
    first_gain,
    first_shift,
    second_gain,
    second_shift,
    encoder_weight,
    encoder_bias,
    prior_mean,
    prior_logvar,
    decoder_weight,
):
    row_count = cells.shape[0]
    devices = device_total()
    total = devices // GROUP
    me = device_index()
    quarter = me % GROUP
    rows = embed_weight.shape[0]
    thin = decoder_weight.shape[0]
    cell_total = row_count * devices
    live = live_mask[0].astype(jnp.float32)
    slides = slide_ids[0]
    places = jnp.arange(row_count)
    allowed = (slides[:, None] == slides[None, :]) & (
        (live[None, :] > 0.5) | (places[:, None] == places[None, :])
    )
    onehot = (
        components[:, None] == jnp.arange(prior_mean.shape[0], dtype=jnp.int32)[None, :]
    ).astype(jnp.float32)

    kinds = prior_mean.shape[0]
    vectors = [down_bias, first_gain, first_shift, second_gain, second_shift, encoder_bias]
    lone = jnp.full((1,), jnp.sum(live), jnp.bfloat16)
    small = jnp.concatenate(
        [
            jnp.pad(v, ((0, 0), (0, 128 - v.shape[1])))
            for v in [prior_mean, prior_logvar]
            + [v.reshape(1, -1) for v in [up_bias] + vectors + [lone]]
        ]
    )
    small = jnp.pad(small, ((0, 48 - small.shape[0]), (0, 0)))
    gather = gather_weights if total <= NARROW else gather_plain
    cells_group, embed_cols, decoder_cols, *middle, embedded = gather(
        gene_chunks(cells),
        gene_chunks(embed_weight),
        gene_chunks(decoder_weight),
        query_key_value,
        small,
        output_weight,
        encoder_weight,
        up_weight,
        down_weight,
    )
    embed_cols = embed_cols.reshape(-1, CHUNK)
    decoder_cols = decoder_cols.reshape(-1, CHUNK)
    middle = [full.reshape(-1, full.shape[-1]) for full in middle]
    joint_full, small_full, output_full, encoder_full, up_full, down_full = middle
    small_full = wide(small_full.reshape(devices, 48, 128))
    up_bias_full = small_full[:, 2 * kinds, : 4 * rows].reshape(1, -1)
    vectors = small_full[:, 2 * kinds + 1 : 2 * kinds + 7, :rows].transpose(1, 0, 2).reshape(6, D)
    down_bias_full, gain_first, shift_first, gain_second, shift_second, encoder_bias_full = vectors
    prior_full = small_full[:, : 2 * kinds, : prior_mean.shape[1]]
    prior_full = prior_full.transpose(1, 0, 2).reshape(2 * kinds, LATENT)
    prior_mean_full, prior_logvar_full = prior_full[:kinds], prior_full[kinds:]
    count = jnp.sum(small_full[:, 2 * kinds + 7, 0])

    start_state = embedded + positions(coordinates)
    normed_first = layer_norm(start_state, gain_first, shift_first).astype(jnp.bfloat16)
    joint = matmul(normed_first, joint_full).astype(jnp.bfloat16)
    context, logsum = attention_forward(joint, allowed)
    middle_state = start_state + matmul(context, output_full)
    normed_second = layer_norm(middle_state, gain_second, shift_second).astype(jnp.bfloat16)
    pre = matmul(normed_second, up_full) + up_bias_full
    active = jax.nn.gelu(pre, approximate=True).astype(jnp.bfloat16)
    end_state = middle_state + (matmul(active, down_full) + down_bias_full)
    end_low = end_state.astype(jnp.bfloat16)
    encoded = matmul(end_low, encoder_full) + encoder_bias_full
    latent_mean = encoded[:, :LATENT]
    latent_logvar = encoded[:, LATENT:]
    latent = (latent_mean + jnp.exp(0.5 * latent_logvar) * noise).astype(jnp.bfloat16)
    center = jnp.dot(onehot, prior_mean_full, precision=lax.Precision.HIGHEST)
    scale = jnp.dot(onehot, prior_logvar_full, precision=lax.Precision.HIGHEST)
    gap = latent_mean - center
    inverse = jnp.exp(-scale)
    grown = jnp.exp(latent_logvar)
    diverge = 0.5 * (scale - latent_logvar + (grown + gap * gap) * inverse - 1.0)
    ratio = cell_total / count
    spread = jnp.broadcast_to(jnp.sum(live[:, None] * diverge, axis=0, keepdims=True), (8, LATENT))
    message = jnp.concatenate(
        [latent, jnp.broadcast_to(low(live)[:, None], (row_count, 128))], axis=1
    )
    latent_pass = latent_step if total <= NARROW else latent_plain
    recon_grad, decoder_term, latent_grad, spread_sum, recon_sum = latent_pass(
        message, spread, ratio.reshape(1, 1), decoder_cols, cells_group
    )
    kl_mean = spread_sum[0] / count
    shifted = (kl_mean - FREE_FLOOR) / FREE_TEMP
    free = FREE_FLOOR + FREE_TEMP * jax.nn.softplus(shifted)
    latent_grad = wide(low(latent_grad))

    kl_scale = ratio * ramp_weight * jax.nn.sigmoid(shifted)[None, :] * live[:, None]
    pulled = kl_scale * gap * inverse
    mean_grad = latent_grad + pulled
    logvar_grad = latent_grad * 0.5 * jnp.exp(0.5 * latent_logvar) * noise + kl_scale * 0.5 * (
        grown * inverse - 1.0
    )
    encoded_grad = jnp.concatenate([mean_grad, logvar_grad], axis=1).astype(jnp.bfloat16)
    prior_mean_grad = jnp.dot(onehot.T, -pulled, precision=lax.Precision.HIGHEST)
    prior_logvar_grad = jnp.dot(
        onehot.T,
        kl_scale * 0.5 * (1.0 - (grown + gap * gap) * inverse),
        precision=lax.Precision.HIGHEST,
    )
    end_grad = across(encoded_grad, encoder_full)
    branch_grad = end_grad.astype(jnp.bfloat16)
    encoder_bias_grad = jnp.sum(encoded_grad.astype(jnp.float32), axis=0)
    down_bias_grad = jnp.sum(branch_grad.astype(jnp.float32), axis=0)
    active_grad = across(branch_grad, down_full)
    gelu_value, gelu_back = jax.vjp(lambda value: jax.nn.gelu(value, approximate=True), pre)
    pre_grad = gelu_back(active_grad)[0].astype(jnp.bfloat16)
    up_bias_grad = jnp.sum(pre_grad.astype(jnp.float32), axis=0)
    second_out_grad = across(pre_grad, up_full)
    norm_value, second_back = jax.vjp(layer_norm, middle_state, gain_second, shift_second)
    state_part, second_gain_grad, second_shift_grad = second_back(second_out_grad)
    middle_grad = end_grad + state_part
    attend_grad = middle_grad.astype(jnp.bfloat16)
    context_grad = across(attend_grad, output_full).astype(jnp.bfloat16)
    joint_grad = attention_backward(joint, allowed, logsum, context_grad)
    first_out_grad = across(joint_grad, joint_full)
    first_value, first_back = jax.vjp(layer_norm, start_state, gain_first, shift_first)
    start_part, first_gain_grad, first_shift_grad = first_back(first_out_grad)
    start_grad = middle_grad + start_part
    start_low = start_grad.astype(jnp.bfloat16)
    vectors = [
        up_bias_grad,
        down_bias_grad,
        first_gain_grad,
        first_shift_grad,
        second_gain_grad,
        second_shift_grad,
        encoder_bias_grad,
    ]
    priors = jnp.concatenate([prior_mean_grad, prior_logvar_grad])
    priors = priors.reshape(2 * kinds, devices, -1).transpose(1, 0, 2).reshape(devices, -1)
    prior_size = priors.shape[1]
    packed = jnp.concatenate([v.reshape(devices, -1) for v in vectors] + [priors], axis=1)
    packed = jnp.pad(packed, ((0, 0), (0, 1024 - packed.shape[1])))
    packed = packed.reshape(total, 2, 2, 8, 128)

    scatter = scatter_sums if total <= NARROW else scatter_plain
    embed_grad, decoder_grad, cells_grad, *middle_grads, small_sum, recon_total = scatter(
        [
            (normed_first, joint_grad),
            (context, attend_grad),
            (end_low, encoded_grad),
            (normed_second, pre_grad),
            (active, branch_grad),
        ],
        start_low,
        decoder_term.reshape(total, GROUP, thin, CHUNK),
        cells_group,
        embed_cols,
        recon_grad,
        packed,
        recon_sum,
    )

    def all_genes(chunks):
        return chunks.transpose(1, 0, 2).reshape(chunks.shape[1], -1)[:, :GENES]

    cells_grad = all_genes(cells_grad)
    embed_grad = wide(all_genes(embed_grad))
    decoder_grad = wide(all_genes(decoder_grad))
    (
        joint_weight_grad,
        output_weight_grad,
        encoder_weight_grad,
        up_weight_grad,
        down_weight_grad,
    ) = middle_grads

    ends = [0]
    for vector in vectors:
        ends.append(ends[-1] + vector.shape[0] // devices)
    packed = small_sum.reshape(-1)
    vector_grads = [packed[ends[i] : ends[i + 1]] for i in range(len(vectors))]
    prior_out = packed[ends[-1] : ends[-1] + prior_size].reshape(2, kinds, -1)
    recon_total = 0.5 * jnp.sum(recon_total)
    loss = (recon_total / count + ramp_weight * jnp.sum(free)) / GENES
    return (
        loss,
        cells_grad,
        embed_grad,
        joint_weight_grad,
        output_weight_grad,
        up_weight_grad,
        vector_grads[0],
        down_weight_grad,
        vector_grads[1],
        vector_grads[2],
        vector_grads[3],
        vector_grads[4],
        vector_grads[5],
        encoder_weight_grad,
        vector_grads[6],
        prior_out[0],
        prior_out[1],
        decoder_grad,
    )


def solution(mesh):
    in_specs = (
        P(("dp", "fsdp"), None),
        P(None, ("dp", "fsdp")),
        P(("dp", "fsdp"), None),
        P(("dp", "fsdp"), None),
        P(("dp", "fsdp")),
        P(("dp", "fsdp"), None),
        P(),
        P(("dp", "fsdp"), None),
        P(("dp", "fsdp"), None),
        P(("dp", "fsdp"), None),
        P(("dp", "fsdp"), None),
        P(("dp", "fsdp")),
        P(("dp", "fsdp"), None),
        P(("dp", "fsdp")),
        P(("dp", "fsdp")),
        P(("dp", "fsdp")),
        P(("dp", "fsdp")),
        P(("dp", "fsdp")),
        P(("dp", "fsdp"), None),
        P(("dp", "fsdp")),
        P(None, ("dp", "fsdp")),
        P(None, ("dp", "fsdp")),
        P(("dp", "fsdp"), None),
    )
    out_specs = (
        P(),
        P(("dp", "fsdp"), None),
        P(("dp", "fsdp"), None),
        P(("dp", "fsdp"), None),
        P(("dp", "fsdp"), None),
        P(("dp", "fsdp"), None),
        P(("dp", "fsdp")),
        P(("dp", "fsdp"), None),
        P(("dp", "fsdp")),
        P(("dp", "fsdp")),
        P(("dp", "fsdp")),
        P(("dp", "fsdp")),
        P(("dp", "fsdp")),
        P(("dp", "fsdp"), None),
        P(("dp", "fsdp")),
        P(None, ("dp", "fsdp")),
        P(None, ("dp", "fsdp")),
        P(("dp", "fsdp"), None),
    )
    return jax.shard_map(shards, mesh=mesh, in_specs=in_specs, out_specs=out_specs, check_vma=False)
```

```python
import functools
import math

import jax
import jax.numpy as jnp
from jax import lax
from jax.experimental import pallas as pl
from jax.experimental.pallas import tpu as pltpu
from jax.sharding import PartitionSpec as P

D = 1024
HEAD_DIM = 64
GENES = 13500
LATENT = 512


NEG_SCORE = -1000000000.0
NORM_EPS = 1e-05
FREE_FLOOR = 1.0
FREE_TEMP = 0.25


def layer_norm(hidden, gain, shift):
    center = hidden - jnp.mean(hidden, axis=-1, keepdims=True)
    spread = jnp.mean(center * center, axis=-1, keepdims=True)
    return center * lax.rsqrt(spread + NORM_EPS) * gain + shift


def positions(coordinates):
    quarter = D // 4
    frequency = jnp.exp(jnp.arange(quarter, dtype=jnp.float32) * (-math.log(10000.0) / quarter))
    angle_x = coordinates[0][:, None] * frequency[None, :]
    angle_y = coordinates[1][:, None] * frequency[None, :]
    return jnp.concatenate(
        [jnp.sin(angle_x), jnp.cos(angle_x), jnp.sin(angle_y), jnp.cos(angle_y)], axis=1
    )


def matmul(left, right):
    return jnp.dot(left, right, preferred_element_type=jnp.float32)


def across(left, right):
    return lax.dot_general(
        left, right, (((1,), (1,)), ((), ())), preferred_element_type=jnp.float32
    )


def contract_rows(left, right):
    return lax.dot_general(
        left, right, (((0,), (0,)), ((), ())), preferred_element_type=jnp.float32
    )


def split_heads(joint):
    row_count = joint.shape[0]
    queries = joint[:, :D].reshape(row_count, -1, HEAD_DIM)
    keys = joint[:, D : 2 * D].reshape(row_count, -1, HEAD_DIM)
    values = joint[:, 2 * D :].reshape(row_count, -1, HEAD_DIM)
    return (queries, keys, values)


def masked_scores(queries, keys, allowed):
    scores = jnp.einsum(
        "qhd,khd->hqk", queries, keys, preferred_element_type=jnp.float32
    ) * HEAD_DIM ** (-0.5)
    return jnp.where(allowed[None], scores, NEG_SCORE)


def attention_forward(joint, allowed):
    queries, keys, values = split_heads(joint)
    masked = masked_scores(queries, keys, allowed)
    peak = jnp.max(masked, axis=-1, keepdims=True)
    raised = jnp.exp(masked - peak)
    denom = jnp.sum(raised, axis=-1, keepdims=True)
    probs = raised / denom
    logsum = peak + jnp.log(denom)
    context = jnp.einsum(
        "hqk,khd->qhd", probs.astype(jnp.bfloat16), values, preferred_element_type=jnp.float32
    )
    return (context.reshape(joint.shape[0], D).astype(jnp.bfloat16), logsum)


def attention_backward(joint, allowed, logsum, context_grad):
    row_count = joint.shape[0]
    queries, keys, values = split_heads(joint)
    probs = jnp.exp(masked_scores(queries, keys, allowed) - logsum)
    probs_low = probs.astype(jnp.bfloat16)
    incoming = context_grad.reshape(row_count, -1, HEAD_DIM)
    value_grad = jnp.einsum("hqk,qhd->khd", probs_low, incoming, preferred_element_type=jnp.float32)
    prob_grad = jnp.einsum("qhd,khd->hqk", incoming, values, preferred_element_type=jnp.float32)
    score_grad = (probs * (prob_grad - jnp.sum(probs * prob_grad, axis=-1, keepdims=True))).astype(
        jnp.bfloat16
    )
    query_grad = jnp.einsum(
        "hqk,khd->qhd", score_grad, keys, preferred_element_type=jnp.float32
    ) * HEAD_DIM ** (-0.5)
    key_grad = jnp.einsum(
        "hqk,qhd->khd", score_grad, queries, preferred_element_type=jnp.float32
    ) * HEAD_DIM ** (-0.5)
    return jnp.concatenate(
        [
            query_grad.reshape(row_count, D),
            key_grad.reshape(row_count, D),
            value_grad.reshape(row_count, D),
        ],
        axis=1,
    ).astype(jnp.bfloat16)

AXES = ("dp", "fsdp")
GROUP = 4
CHUNK = 3456
SLICE = 384
NARROW = 8


def low(values):
    return values.astype(jnp.bfloat16)


def wide(values):
    return values.astype(jnp.float32)


def device_total():
    return lax.axis_size("dp") * lax.axis_size("fsdp")


def device_index():
    return lax.axis_index("dp") * lax.axis_size("fsdp") + lax.axis_index("fsdp")


def swap(values, mask):
    return lax.ppermute(values, AXES, [(i, i ^ mask) for i in range(device_total())])


def same_quarter():
    return [[d for d in range(lax.axis_size("dp")) if d % 2 == odd] for odd in range(2)]


def pick(blocks, index):
    return lax.dynamic_index_in_dim(blocks, index, 0, keepdims=False)


def group_exchange(blocks, quarter):
    return [pick(blocks, quarter)] + [swap(pick(blocks, quarter ^ m), m) for m in range(1, GROUP)]


def group_gather(values):
    pair = jnp.stack([values, swap(values, 2)])
    other = swap(pair, 1)
    return jnp.stack([pair[0], other[0], pair[1], other[1]])


def group_scatter(parts):
    mine = jnp.stack([parts[0], parts[2]])
    theirs = low(jnp.stack([parts[1], parts[3]]))
    summed = wide(mine) + wide(swap(theirs, 1))
    return summed[0] + wide(swap(low(summed[1]), 2))


def by_quarter(pieces, quarter):
    stacked = jnp.stack(pieces)
    return [pick(stacked, quarter ^ j) for j in range(GROUP)]


def gene_chunks(values):
    padded = jnp.pad(values, ((0, 0), (0, GROUP * CHUNK - GENES)))
    return jnp.stack([padded[:, j * CHUNK : (j + 1) * CHUNK] for j in range(GROUP)])


def sum_all(values):
    mask = 1
    while mask < device_total():
        values = values + swap(values, mask)
        mask *= 2
    return values


MESH = pl.DeviceIdType.MESH


class Where:
    def __init__(self, total):
        dp = lax.axis_index("dp")
        self.total = total
        self.core = lax.axis_index("fsdp")
        self.x = dp % 2
        self.t = dp // 2
        self.quarter = 2 * self.x + self.core
        y, z = self.t % 2, self.t // 2
        self.k = z + y * (total - 1 - 2 * z)
        self.right = (2 * self.owner(-1) + self.x, self.core)
        self.left = (2 * self.owner(1) + self.x, self.core)
        self.peers = [
            None,
            (dp, 1 - self.core),
            (2 * self.t + 1 - self.x, self.core),
            (2 * self.t + 1 - self.x, 1 - self.core),
        ]
        self.quarters = [
            self.quarter,
            2 * self.x + 1 - self.core,
            2 * (1 - self.x) + self.core,
            2 * (1 - self.x) + 1 - self.core,
        ]

    def owner(self, step):
        place = (self.k - step + self.total) % self.total
        y = place // (self.total // 2)
        return 2 * (place + y * (self.total - 1 - 2 * place)) + y

    def same(self, step):
        t = (self.t + step) % self.total
        return t, (2 * t + self.x, self.core)

    def meet(self, everyone=False):
        barrier = pltpu.get_barrier_semaphore()
        others = self.peers[1:]
        if everyone:
            others = others + [self.same(step)[1] for step in range(1, self.total)]
        else:
            others = others + [self.right, self.left]
        for other in others:
            pl.semaphore_signal(barrier, inc=1, device_id=other, device_id_type=MESH)
        pl.semaphore_wait(barrier, len(others))


class Copies:
    def __init__(self, send_sems, recv_sems, local_sems):
        self.send_sems, self.recv_sems, self.local_sems = send_sems, recv_sems, local_sems
        self.remote_count = self.local_count = 0
        self.sent = []

    def send(self, source, target, device):
        at = self.remote_count
        self.remote_count += 1
        copy = pltpu.make_async_remote_copy(
            source,
            target,
            self.send_sems.at[at],
            self.recv_sems.at[at],
            device_id=device,
            device_id_type=MESH,
        )
        copy.start()
        self.sent.append(copy)
        return copy

    def local(self, source, target):
        at = self.local_count
        self.local_count += 1
        copy = pltpu.make_async_copy(source, target, self.local_sems.at[at])
        copy.start()
        return copy

    def free(self, copy):
        copy.wait_send()
        self.sent = [other for other in self.sent if other is not copy]

    def finish(self):
        for copy in self.sent:
            copy.wait_send()


def gather_kernel(total, *refs):
    (cells, embed, decoder, joint, small, output, encoder, up, down) = refs[:9]
    (cells_all, embed_all, decoder_all, joint_all, small_all) = refs[9:14]
    (output_all, encoder_all, up_all, down_all, embedded) = refs[14:19]
    (held_cells, held_embed, partial, other_core, for_x, other_x, raw, turned) = refs[19:27]
    here = Where(total)
    copies = Copies(*refs[27:])
    here.meet()
    t, x, core = here.t, here.x, here.core
    last = total - 1
    towards = {1: here.right, -1: here.left}
    flying = {}

    late = [(up, up_all, 1), (output, output_all, 1), (down, down_all, -1), (encoder, encoder_all, -1)]
    shares = {
        name: [
            copies.send(own.at[here.quarters[m]], full.at[t, here.quarter], here.peers[m])
            for m in (2, 3, 1)
        ]
        for name, own, full in (("embed", embed, embed_all), ("decoder", decoder, decoder_all))
    }
    for n, (own, full, way) in enumerate(late):
        flying["late", n] = copies.send(own, full.at[t, x, core], towards[way])
    across_x = [copies.send(own, full.at[t, x, core], here.peers[2]) for own, full, _ in late]
    reads = [copies.local(cells.at[chunk], raw.at[chunk]) for chunk in range(2)]
    shares["early"] = [
        copies.send(own, full.at[t, x, core], here.peers[2])
        for own, full in ((joint, joint_all), (small, small_all))
    ]
    own_copies = {
        "embed": [copies.local(embed.at[here.quarter], embed_all.at[t, here.quarter])],
        "decoder": [copies.local(decoder.at[here.quarter], decoder_all.at[t, here.quarter])],
        "early": [
            copies.local(own, full.at[t, x, core])
            for own, full in ((joint, joint_all), (small, small_all))
        ],
    }
    own_late = [copies.local(own, full.at[t, x, core]) for own, full, _ in late]

    def late_step(s):
        for n, (_, full, way) in enumerate(late):
            flying["late", n].wait_recv()
            block = full.at[here.owner(way * s), x, core]
            if s < last:
                flying["late", n] = copies.send(block, block, towards[way])
            across_x.append(copies.send(block, block, here.peers[2]))

    def early_block(full, way, s):
        return full.at[here.owner(way * s), 0 if way == 1 else 1, core]

    def table_block(full, way, s):
        return full.at[here.owner(way * s), pl.ds(0 if way == 1 else 2, 2)]

    rings = {
        "embed": [(embed_all, way, table_block) for way in (1, -1)],
        "decoder": [(decoder_all, way, table_block) for way in (1, -1)],
        "early": [(full, way, early_block) for full in (joint_all, small_all) for way in (1, -1)],
    }

    def step(name, s):
        if s == 0:
            for copy in own_copies[name]:
                copy.wait()
            for copy in shares[name]:
                copy.wait_recv()
        for n, (full, way, block_of) in enumerate(rings[name]):
            if s > 0:
                flying[name, n].wait_recv()
            if s < last:
                block = block_of(full, way, s)
                flying[name, n] = copies.send(block, block, towards[way])

    holds = {}

    def hold(block):
        holds[block] = copies.local(embed_all.at[block], held_embed.at[block % 2])

    def multiply(block):
        holds[block].wait()
        features = held_embed.shape[1] * held_embed.shape[2]
        table = held_embed[block % 2].reshape(features, held_embed.shape[3])
        for row in range(2):
            for column in range(2):
                partial[row, column, :, pl.ds(block * features, features)] = low(
                    across(held_cells[2 * row + column], table)
                )
        if block + 2 < total:
            hold(block + 2)

    across_core = []

    def send_cells():
        for chunk in range(GROUP):
            reads[chunk].wait()

            @pl.loop(0, CHUNK // 128)
            def _(i):
                part = pl.ds(pl.multiple_of(i * 128, 128), 128)
                turned[chunk, :, part] = low(wide(raw[chunk % 2, part, :]).T)

            if chunk + 2 < GROUP:
                reads.append(copies.local(cells.at[chunk + 2], raw.at[chunk % 2]))
        own = copies.local(turned.at[here.quarter], cells_all.at[0])
        return own, [
            copies.send(turned.at[here.quarters[m]], cells_all.at[m], here.peers[m])
            for m in (2, 3, 1)
        ]

    def to_core(copies_of, block_of):
        for copy, (_, full, way) in zip(copies_of, late):
            copy.wait_recv()
            block = block_of(full, way)
            across_core.append(copies.send(block, block, here.peers[1]))

    def crossed(s):
        to_core(
            across_x[len(late) * s : len(late) * (s + 1)],
            lambda full, way: full.at[here.owner(way * s), 1 - x, core],
        )

    for s in range(1, last + 1):
        late_step(s)
        if s == 1:
            step("embed", 0)
            own_cells, cell_moves = send_cells()
        step("embed", s)
        if s == last - 1:
            step("early", 0)
            step("decoder", 0)
    hold(0)
    hold(1)
    for copy in own_late:
        copy.wait()
    for _, full, _ in late:
        block = full.at[:, x, core]
        across_core.append(copies.send(block, block, here.peers[1]))
    for copy in cell_moves:
        copy.wait_recv()
    own_cells.wait()
    held = copies.local(cells_all, held_cells)
    step("early", 1)
    step("decoder", 1)
    held.wait()
    for s in range(2, last + 1):
        multiply(s - 2)
        step("early", s)
        step("decoder", s)
        crossed(s - 2)
    for block in range(last - 1, total):
        multiply(block)
    sums = copies.send(partial.at[:, 1], other_core, here.peers[1])
    for full in (joint_all, small_all):
        block = full.at[:, :, core]
        across_core.append(copies.send(block, block, here.peers[1]))
    sums.wait_recv()
    for_x[...] = low(wide(partial[1, 0]) + wide(other_core[1]))
    sums = copies.send(for_x, other_x, here.peers[2])
    for s in range(last - 1, total):
        crossed(s)
    sums.wait_recv()
    embedded[...] = wide(partial[0, 0]) + wide(other_core[0]) + wide(other_x[...])
    for copy in across_core:
        copy.wait_recv()
    copies.finish()


def gather_weights(cells, embed, decoder, joint, small, output, encoder, up, down):
    total = device_total() // GROUP
    own = [joint, small, output, encoder, up, down]
    tables = [embed, decoder]
    operands = [cells] + tables + own
    shapes = (
        [(GROUP, cells.shape[2], cells.shape[1])]
        + [(total,) + v.shape for v in tables]
        + [(total, 2, 2) + v.shape for v in own]
    )
    remote = 15 + 12 * (total - 1) + 8 * total + 8
    genes, cell_rows = cells.shape[1:]
    features = total * GROUP * embed.shape[1]
    by_cell = (GROUP, cell_rows, genes)
    buffers = [
        by_cell,
        (2,) + embed.shape,
        (2, 2, cell_rows, features),
        (2, cell_rows, features),
        (cell_rows, features),
        (cell_rows, features),
        (2, genes, cell_rows),
        by_cell,
    ]
    return pl.pallas_call(
        functools.partial(gather_kernel, total),
        out_shape=[jax.ShapeDtypeStruct(s, jnp.bfloat16) for s in shapes]
        + [jax.ShapeDtypeStruct((cell_rows, features), jnp.float32)],
        in_specs=[pl.BlockSpec(memory_space=pl.ANY)] * len(operands),
        out_specs=[pl.BlockSpec(memory_space=pl.ANY)] * len(operands)
        + [pl.BlockSpec(memory_space=pltpu.VMEM)],
        scratch_shapes=[pltpu.VMEM(shape, jnp.bfloat16) for shape in buffers]
        + [
            pltpu.SemaphoreType.DMA((remote,)),
            pltpu.SemaphoreType.DMA((remote,)),
            pltpu.SemaphoreType.DMA((14 + total,)),
        ],
        compiler_params=pltpu.CompilerParams(
            collective_id=1, has_side_effects=True, vmem_limit_bytes=20 * 2**20
        ),
        name="gather_weights",
    )(*operands)


def add_rows(target, first, second, dtype):
    rows, columns = target.shape
    step = min(rows, 16 if columns > 2048 else 32)

    @pl.loop(0, rows // step)
    def _(i):
        part = pl.ds(pl.multiple_of(i * step, step), step)
        target[part, :] = (wide(first[part, :]) + wide(second[part, :])).astype(dtype)


def product(target, left, right, accumulate):
    total, _, rows, columns = target.shape
    step = 256 // (2 * rows)
    width = 512

    @pl.loop(0, total // step)
    def _(i):
        blocks = pl.ds(i * step, step)
        part = left(i * 2 * step, 2 * step)

        @pl.loop(0, columns // width)
        def _(n):
            across_columns = pl.ds(pl.multiple_of(n * width, width), width)
            value = matmul(part, right[:, across_columns]).reshape(step, 2, rows, width)
            if accumulate:
                value = value + wide(target[blocks, :, :, across_columns])
            target[blocks, :, :, across_columns] = low(value)


MIDDLE = ("joint", "output", "encoder", "up", "down")


def scatter_kernel(total, *refs):
    (recon, start, small, decoder, cells, table, grads) = refs[:7]
    left = dict(zip(MIDDLE, refs[7:12]))
    right = dict(zip(MIDDLE, refs[12:17]))
    (embed_out, decoder_out, cells_out, embed, back) = refs[17:22]
    results = dict(zip(MIDDLE, refs[22:27]))
    (small_out, recon_out) = refs[27:29]
    (chip_small, stage_small, sum_small, hop_small, group_recon, all_recon) = refs[29:35]
    chip = dict(zip(MIDDLE, refs[35:40]))
    (send_up, send_down) = refs[40:42]
    sums = dict(zip(MIDDLE[1:], refs[42:46]))
    (hop_embed, hop_decoder, hop_joint) = refs[46:49]
    hops_of = dict(zip(MIDDLE[1:], refs[49:53]))
    (local_embed, local_decoder) = refs[53:55]
    (other_joint, starts, turned) = refs[55:58]
    (in_cells, in_table, in_grads, out_term, out_back, blocks) = refs[58:64]
    here = Where(total)
    copies = Copies(*refs[64:67])
    stream_sems = refs[67]
    here.meet()
    x, core, last = here.x, here.core, total - 1
    towards = {1: here.right, -1: here.left}
    flying = {}

    def lanes(term, hops, local):
        return [(term, hops, local, way, side) for side, way in ((0, 1), (1, -1))]

    tables = {
        "embed": lanes(embed, hop_embed, local_embed),
        "decoder": lanes(decoder, hop_decoder, local_decoder),
    }

    def table_block(term, way, side, h):
        return term.at[here.owner(way * h), pl.ds(2 * side, 2)]

    def fetch(name, h):
        for n, (term, _, local, way, side) in enumerate(tables[name]):
            flying["local", name, n, h] = copies.local(
                table_block(term, way, side, h + 1), local.at[h % 2, side]
            )

    def table_start(name):
        for n, (term, hops, _, way, side) in enumerate(tables[name]):
            flying[name, n] = copies.send(
                table_block(term, way, side, 1), hops.at[0, side], towards[way]
            )
        fetch(name, 1)
        fetch(name, 2)

    def table_hop(name, h):
        for n, (_, hops, local, way, side) in enumerate(tables[name]):
            flying[name, n].wait_recv()
            flying["local", name, n, h].wait()
            for row in range(2):
                arrived = hops.at[h - 1, side, row]
                add_rows(arrived, arrived, local.at[h % 2, side, row], jnp.bfloat16)
            if h < last:
                flying[name, n] = copies.send(hops.at[h - 1, side], hops.at[h, side], towards[way])
        if h + 2 <= last:
            fetch(name, h + 2)

    table_start("decoder")
    moves = [copies.send(start, starts.at[m], here.peers[m]) for m in (2, 1)]
    starts[0] = start[...]
    group_recon[here.quarter] = recon[...]
    recons = [copies.send(recon, group_recon.at[here.quarter], here.peers[m]) for m in (2, 3, 1)]
    halves = {"small": copies.send(small.at[:, :, 1 - core], chip_small, here.peers[1])}
    own_small = copies.local(small.at[:, :, core], stage_small)

    def half(name, which):
        source = left[name]
        if results[name].shape[0] == 128:

            def wide_blocks(first, size):
                lanes = [
                    pl.ds(pl.multiple_of((2 * (first + n) + which) * 128, 128), 128)
                    for n in range(size)
                ]
                return jnp.concatenate([low(wide(source[:, part]).T) for part in lanes])

            return wide_blocks
        blocks[...] = low(wide(source[...]).T).reshape(blocks.shape)

        def narrow_blocks(first, size):
            return blocks[pl.ds(first, size), which].reshape(-1, blocks.shape[-1])

        return narrow_blocks

    def give(name, buffer):
        product(buffer, half(name, 1 - core), right[name], False)
        halves[name] = copies.send(buffer, chip[name], here.peers[1])

    across = {}

    def cross(name, held, target):
        across[name] = copies.send(held.at[:, 1 - x], target, here.peers[2])

    def take(name):
        halves[name].wait_recv()
        product(chip[name], half(name, core), right[name], True)
        if name in sums:
            cross(name, chip[name], sums[name])

    give("up", send_up)
    give("down", send_down)
    moves[0].wait_recv()
    moves[0] = copies.send(starts.at[2], starts.at[3], here.peers[1])
    table_hop("decoder", 1)
    take("up")
    copies.free(halves["up"])
    give("joint", send_up.at[:, :, :, pl.ds(0, right["joint"].shape[1])])
    table_hop("decoder", 2)
    take("down")
    copies.free(halves["down"])
    slim = results["output"].shape[0]
    give("output", send_down.at[:, :, pl.ds(0, slim)])
    give("encoder", send_down.at[:, :, pl.ds(slim, slim)])
    table_hop("decoder", 3)
    take("joint")
    for side, way in ((0, 1), (1, -1)):
        flying["joint", side] = copies.send(
            chip["joint"].at[here.owner(way), side], hop_joint.at[0, side], towards[way]
        )
    take("output")
    take("encoder")
    own_small.wait()
    halves["small"].wait_recv()

    @pl.loop(0, total)
    def _(t):
        for side in range(2):
            held = chip_small.at[t, side]
            add_rows(held, held, stage_small.at[t, side], jnp.float32)

    cross("small", chip_small, sum_small)
    for copy in recons:
        copy.wait_recv()
    all_recon[here.t] = group_recon[0] + group_recon[1] + group_recon[2] + group_recon[3]
    own_recon = all_recon.at[here.t]
    flying["recon"] = copies.send(own_recon, own_recon, here.right)
    table_hop("decoder", 4)

    def joint_hop(h):
        for side, way in ((0, 1), (1, -1)):
            flying["joint", side].wait_recv()
            arrived = hop_joint.at[h - 1, side]
            local = chip["joint"].at[here.owner(way * (h + 1)), side]
            add_rows(arrived, arrived, local, jnp.bfloat16)
            if h < last:
                flying["joint", side] = copies.send(arrived, hop_joint.at[h, side], towards[way])

    for copy in moves:
        copy.wait_recv()
    moves = []
    rows, rows_of_t = start.shape[0], turned.shape[0] // total
    for m in range(GROUP):
        turned[:, m * rows : (m + 1) * rows] = low(wide(starts[m]).T)

    def moved(i, pairs, first):
        part = pl.ds(pl.multiple_of(i * SLICE, 128), SLICE)
        slot = i % 2
        return [
            pltpu.make_async_copy(*ends(part, slot), stream_sems.at[first + n, slot])
            for n, ends in enumerate(pairs)
        ]

    def loads_of(i):
        return moved(
            i,
            [
                lambda part, slot: (cells.at[:, :, part], in_cells.at[slot]),
                lambda part, slot: (table.at[:, part], in_table.at[slot]),
                lambda part, slot: (grads.at[:, :, part], in_grads.at[slot]),
            ],
            0,
        )

    def stores_of(i):
        return moved(
            i,
            [
                lambda part, slot: (out_term.at[slot], embed.at[:, :, :, part]),
                lambda part, slot: (out_back.at[slot], back.at[:, :, part]),
            ],
            3,
        )

    count = CHUNK // SLICE
    for copy in loads_of(0):
        copy.start()

    def stream(first, end):
        @pl.loop(first, end)
        def _(i):
            slot = i % 2
            @pl.when(i + 1 < count)
            def _():
                for copy in loads_of(i + 1):
                    copy.start()

            for copy in loads_of(i):
                copy.wait()

            @pl.when(i >= 2)
            def _():
                for copy in stores_of(i - 2):
                    copy.wait()

            for t in range(total):
                term = matmul(
                    turned[pl.ds(t * rows_of_t, rows_of_t), :],
                    in_cells[slot].reshape(GROUP * rows, SLICE),
                )
                out_term[slot, t] = low(term).reshape(out_term.shape[2:])
            for m in range(GROUP):
                out_back[slot, m] = low(matmul(starts[m], in_table[slot]) - wide(in_grads[slot, m]))
            for copy in stores_of(i):
                copy.start()

    joint_hop(1)
    stream(0, count // 3)
    table_hop("decoder", 5)
    joint_hop(2)
    stream(count // 3, 2 * count // 3)
    table_hop("decoder", 6)
    joint_hop(3)
    stream(2 * count // 3, count)
    for i in (count - 2, count - 1):
        for copy in stores_of(i):
            copy.wait()
    table_start("embed")
    moves = [copies.send(back.at[m], cells_out.at[here.quarter], here.peers[m]) for m in (2, 3, 1)]
    own = [copies.local(back.at[0], cells_out.at[here.quarter])]
    table_hop("decoder", last)

    def send_back(hops, out):
        done = [hops.at[last - 1, quarter // 2, quarter % 2] for quarter in here.quarters]
        for m in (2, 3, 1):
            moves.append(copies.send(done[m], out.at[here.quarter], here.peers[m]))
        own.append(copies.local(done[0], out.at[here.quarter]))

    send_back(hop_decoder, decoder_out)

    def recon_hop(h):
        flying["recon"].wait_recv()
        if h < last:
            arrived = all_recon.at[here.owner(h)]
            flying["recon"] = copies.send(arrived, arrived, here.right)

    late = [
        (name, sums[name], chip[name], hops_of[name], results[name], way)
        for name, way in (("up", 1), ("down", -1), ("output", 1), ("encoder", -1))
    ] + [("small", sum_small, chip_small, hop_small, small_out, 1)]

    def late_start():
        for name, summed, held, hops, _, way in late:
            across[name].wait_recv()

            @pl.loop(0, total)
            def _(t):
                add_rows(summed.at[t], summed.at[t], held.at[t, x], summed.dtype)

            flying["late", name] = copies.send(summed.at[here.owner(way)], hops.at[0], towards[way])

    def late_hop(h):
        for name, summed, _, hops, result, way in late:
            flying["late", name].wait_recv()
            local = summed.at[here.owner(way * (h + 1))]
            if h < last:
                add_rows(hops.at[h - 1], hops.at[h - 1], local, hops.dtype)
                flying["late", name] = copies.send(hops.at[h - 1], hops.at[h], towards[way])
            else:
                add_rows(result, hops.at[h - 1], local, jnp.float32)

    for h in range(1, last + 1):
        if h + 3 <= last:
            joint_hop(h + 3)
        table_hop("embed", h)
        recon_hop(h)
    send_back(hop_embed, embed_out)
    done_joint = hop_joint.at[last - 1]
    joint_move = copies.send(done_joint.at[1 - x], other_joint, here.peers[2])
    late_start()
    for h in range(1, last + 1):
        late_hop(h)
    summed = all_recon[0]
    for t in range(1, total):
        summed = summed + all_recon[t]
    recon_out[...] = summed
    joint_move.wait_recv()
    add_rows(results["joint"], done_joint.at[x], other_joint, jnp.float32)
    for copy in moves:
        copy.wait_recv()
    for copy in own:
        copy.wait()
    copies.finish()


def scatter_sums(pairs, start, decoder, cells, table, grads, small, recon):
    total = device_total() // GROUP
    last = total - 1
    rows, features = start.shape
    thin = jnp.bfloat16
    share = features // (total * GROUP)
    lefts, rights, shapes = [], [], []
    for before, after in pairs:
        block = before.shape[1] // device_total()
        lefts.append(before)
        rights.append(after)
        shapes.append((block, after.shape[1]))
    operands = [recon, start, small, decoder, cells, table, grads] + lefts + rights
    decoder_share = decoder.shape[1:]
    embed_share = (GROUP, share, CHUNK)
    out_shape = [
        jax.ShapeDtypeStruct(v, thin)
        for v in (embed_share, decoder_share, cells.shape, (total,) + embed_share, cells.shape)
    ]
    block = small.shape[3:]
    out_shape += [jax.ShapeDtypeStruct(v, jnp.float32) for v in shapes + [block, recon.shape]]
    exact = [(total, 2) + block, (total, 2) + block, (total,) + block, (last,) + block]
    exact += [(GROUP,) + recon.shape, (total,) + recon.shape]
    chips = [(total, 2) + v for v in shapes]
    buffers = chips + [chips[3], chips[4]] + [(total,) + v for v in shapes[1:]]
    buffers += [(last, 2, 2) + v[1:] for v in (embed_share, decoder_share)]
    buffers += [(last, 2) + shapes[0]] + [(last,) + v for v in shapes[1:]]
    buffers += [(2, 2, 2) + v[1:] for v in (embed_share, decoder_share)]
    buffers += [shapes[0], (GROUP,) + start.shape, (features, GROUP * rows)]
    buffers += [(2, GROUP, rows, SLICE), (2, features, SLICE), (2, GROUP, rows, SLICE)]
    buffers += [(2, total, GROUP, share, SLICE), (2, GROUP, rows, SLICE)]
    buffers += [(2 * total, 2, shapes[0][0], rows)]
    remote, here = 12 + 6 * last + 4 * last + 15 + 2 * last, 4 * last + 9
    anywhere, vmem = pl.BlockSpec(memory_space=pl.ANY), pl.BlockSpec(memory_space=pltpu.VMEM)
    outs = pl.pallas_call(
        functools.partial(scatter_kernel, total),
        out_shape=out_shape,
        in_specs=[vmem] * 2 + [anywhere] * 5 + [vmem] * 10,
        out_specs=[anywhere] * 5 + [vmem] * 7,
        scratch_shapes=[pltpu.VMEM(shape, jnp.float32) for shape in exact]
        + [pltpu.VMEM(shape, thin) for shape in buffers]
        + [
            pltpu.SemaphoreType.DMA((remote,)),
            pltpu.SemaphoreType.DMA((remote,)),
            pltpu.SemaphoreType.DMA((here,)),
            pltpu.SemaphoreType.DMA((5, 2)),
        ],
        compiler_params=pltpu.CompilerParams(
            collective_id=2, has_side_effects=True, vmem_limit_bytes=60 * 2**20
        ),
        name="scatter_sums",
    )(*operands)
    return outs[:3] + outs[5:]


def scatter_plain(pairs, start, decoder, cells, table, grads, small, recon):
    quarter = device_index() % GROUP
    total = device_total() // GROUP
    starts = group_gather(start).reshape(-1, start.shape[1])
    wide_cells = cells.reshape(-1, CHUNK)
    embed = low(contract_rows(starts, wide_cells)).reshape(total, GROUP, -1, CHUNK)
    back = low(matmul(starts, table) - wide(grads.reshape(-1, CHUNK))).reshape(cells.shape)

    def sent(blocks):
        pieces = [pick(blocks, 0)] + [swap(blocks[m], m) for m in range(1, GROUP)]
        return jnp.stack(by_quarter(pieces, quarter))

    def table_sum(term):
        block = lax.psum_scatter(
            term, "dp", axis_index_groups=same_quarter(), scatter_dimension=0, tiled=False
        )
        return sent(jnp.stack(by_quarter(list(block), quarter)))

    def middle(term):
        rows = term.reshape((device_total(), -1) + term.shape[-1:])
        return wide(lax.psum_scatter(rows, AXES, scatter_dimension=0, tiled=False))

    terms = [low(contract_rows(before, after)) for before, after in pairs]
    small = small.reshape((device_total(),) + small.shape[3:])
    return (
        [table_sum(embed), table_sum(decoder), sent(back)]
        + [middle(term) for term in terms]
        + [lax.psum_scatter(small, AXES, scatter_dimension=0, tiled=False), sum_all(recon)]
    )


def latent_kernel(total, *refs):
    (message, spread, ratio, decoder, cells) = refs[:5]
    (recon_grad, decoder_term, latent_grad, spread_sum, recon_sum) = refs[5:10]
    (latents, held_decoder, held_cells, held_grad, held_term, turned, partial) = refs[10:17]
    (leaving, arriving, group_spread, all_spread) = refs[17:21]
    here = Where(total)
    copies = Copies(*refs[21:])
    here.meet(everyone=True)
    arrivals = {m: copies.send(message, latents.at[m], here.peers[m]) for m in (1, 2, 3)}
    spreads = [copies.send(spread, group_spread.at[here.quarter], here.peers[m]) for m in (2, 3, 1)]
    loads = [
        copies.local(message, latents.at[0]),
        copies.local(decoder, held_decoder),
        copies.local(cells, held_cells),
    ]
    group_spread[here.quarter] = spread[...]
    for copy in spreads:
        copy.wait_recv()
    all_spread[here.t] = (
        group_spread[0] + group_spread[1] + group_spread[2] + group_spread[3]
    )
    spreads = []
    for away in range(1, total):
        own = all_spread.at[here.t]
        spreads.append(copies.send(own, own, here.same(away)[1]))
    for copy in loads:
        copy.wait()
    rows = message.shape[0]
    size = held_decoder.shape[0]
    partial[...] = jnp.zeros_like(partial)
    recon_sum[...] = jnp.zeros_like(recon_sum)

    both = 2 * rows

    def reconstruct(pair):
        at = pl.ds(2 * pair, 2)
        for m in (2 * pair, 2 * pair + 1):
            turned[:, m * rows : (m + 1) * rows] = low(wide(latents[m, :, :size]).T)
        values = latents[at, :, :size].reshape(both, size)
        live = wide(latents[at, :, size : size + 128]).reshape(both, 128)
        live = jnp.concatenate([live] * (SLICE // 128), axis=1)

        @pl.loop(0, CHUNK // SLICE)
        def _(i):
            part = pl.ds(pl.multiple_of(i * SLICE, 128), SLICE)
            table = held_decoder[:, part]
            miss = matmul(values, table) - wide(held_cells[at, :, part]).reshape(both, SLICE)
            weighted = live * miss
            recon_sum[...] += jnp.sum((weighted * miss).reshape(both // 8, 8, SLICE), axis=0)
            grad = low(ratio[0, 0] * weighted)
            held_grad[at, :, part] = grad.reshape(2, rows, SLICE)
            partial[at] += across(grad, table).reshape(2, rows, size)

    arrivals[1].wait_recv()
    reconstruct(0)
    leaving[1] = low(partial[1])
    returns = [copies.send(leaving.at[1], arriving.at[0], here.peers[1])]
    for m in (2, 3):
        arrivals[m].wait_recv()
    reconstruct(1)
    for m in (2, 3):
        leaving[m] = low(partial[m])
        returns.append(copies.send(leaving.at[m], arriving.at[m - 1], here.peers[m]))

    @pl.loop(0, CHUNK // SLICE)
    def _(i):
        part = pl.ds(pl.multiple_of(i * SLICE, 128), SLICE)
        grads = held_grad[:, :, part].reshape(GROUP * rows, SLICE)
        held_term[:, part] = low(matmul(turned[...], grads))

    stores = [copies.local(held_grad, recon_grad), copies.local(held_term, decoder_term)]
    for copy in spreads:
        copy.wait_recv()
    summed = all_spread[0]
    for t in range(1, total):
        summed = summed + all_spread[t]
    spread_sum[...] = summed
    for copy in returns:
        copy.wait_recv()
    latent_grad[...] = (
        (partial[0] + wide(arriving[0])) + (wide(arriving[1]) + wide(arriving[2]))
    )
    for copy in stores:
        copy.wait()
    copies.finish()


def latent_step(message, spread, ratio, decoder, cells):
    total = device_total() // GROUP
    rows, size = message.shape[0], decoder.shape[0]
    thin = jnp.bfloat16
    vmem = pl.BlockSpec(memory_space=pltpu.VMEM)
    anywhere = pl.BlockSpec(memory_space=pl.ANY)
    remote = 9 + total - 1
    return pl.pallas_call(
        functools.partial(latent_kernel, total),
        out_shape=[
            jax.ShapeDtypeStruct(cells.shape, thin),
            jax.ShapeDtypeStruct(decoder.shape, thin),
            jax.ShapeDtypeStruct((rows, size), jnp.float32),
            jax.ShapeDtypeStruct(spread.shape, jnp.float32),
            jax.ShapeDtypeStruct((8, SLICE), jnp.float32),
        ],
        in_specs=[vmem, vmem, pl.BlockSpec(memory_space=pltpu.SMEM), anywhere, anywhere],
        out_specs=[anywhere, anywhere, vmem, vmem, vmem],
        scratch_shapes=[
            pltpu.VMEM((GROUP,) + message.shape, thin),
            pltpu.VMEM(decoder.shape, thin),
            pltpu.VMEM(cells.shape, thin),
            pltpu.VMEM(cells.shape, thin),
            pltpu.VMEM(decoder.shape, thin),
            pltpu.VMEM((size, GROUP * rows), thin),
            pltpu.VMEM((GROUP, rows, size), jnp.float32),
            pltpu.VMEM((GROUP, rows, size), thin),
            pltpu.VMEM((GROUP - 1, rows, size), thin),
            pltpu.VMEM((GROUP,) + spread.shape, jnp.float32),
            pltpu.VMEM((total,) + spread.shape, jnp.float32),
            pltpu.SemaphoreType.DMA((remote,)),
            pltpu.SemaphoreType.DMA((remote,)),
            pltpu.SemaphoreType.DMA((5,)),
        ],
        compiler_params=pltpu.CompilerParams(
            collective_id=3, has_side_effects=True, vmem_limit_bytes=40 * 2**20
        ),
        name="latent_step",
    )(message, spread, ratio, decoder, cells)


def latent_plain(message, spread, ratio, decoder, cells):
    size = decoder.shape[0]
    gathered = group_gather(message).reshape(-1, message.shape[1])
    latents, live = gathered[:, :size], wide(gathered[:, size : size + 1])
    miss = matmul(latents, decoder) - wide(cells.reshape(-1, CHUNK))
    grad = low(ratio[0, 0] * live * miss)
    recon_sum = jnp.sum((live * miss * miss).reshape(-1, 8, CHUNK), axis=0)
    latent_grad = group_scatter(low(across(grad, decoder)).reshape(GROUP, -1, size))
    term = low(contract_rows(latents, grad))
    return grad.reshape(cells.shape), term, latent_grad, sum_all(spread), recon_sum


def gather_plain(cells, embed, decoder, *own):
    quarter = device_index() % GROUP
    total = device_total() // GROUP
    groups = same_quarter()

    def table(values):
        block = jnp.stack(by_quarter(group_exchange(values, quarter), quarter))
        return lax.all_gather(block, "dp", axis_index_groups=groups, axis=0, tiled=False)

    cells = cells.transpose(0, 2, 1)
    cells_all = jnp.stack(group_exchange(cells, quarter))
    embed_all = table(embed)
    rows, genes = cells.shape[1:]
    embedded = low(across(cells_all.reshape(-1, genes), embed_all.reshape(-1, genes)))
    embedded = group_scatter(embedded.reshape(GROUP, rows, -1))
    middle = [lax.all_gather(v, AXES, axis=0, tiled=False) for v in own]
    return [cells_all, embed_all, table(decoder)] + middle + [embedded]


def shards(
    cells,
    coordinates,
    slide_ids,
    live_mask,
    components,
    noise,
    ramp_weight,
    embed_weight,
    query_key_value,
    output_weight,
    up_weight,
    up_bias,
    down_weight,
    down_bias,
    first_gain,
    first_shift,
    second_gain,
    second_shift,
    encoder_weight,
    encoder_bias,
    prior_mean,
    prior_logvar,
    decoder_weight,
):
    row_count = cells.shape[0]
    devices = device_total()
    total = devices // GROUP
    me = device_index()
    quarter = me % GROUP
    rows = embed_weight.shape[0]
    thin = decoder_weight.shape[0]
    cell_total = row_count * devices
    live = live_mask[0].astype(jnp.float32)
    slides = slide_ids[0]
    places = jnp.arange(row_count)
    allowed = (slides[:, None] == slides[None, :]) & (
        (live[None, :] > 0.5) | (places[:, None] == places[None, :])
    )
    onehot = (
        components[:, None] == jnp.arange(prior_mean.shape[0], dtype=jnp.int32)[None, :]
    ).astype(jnp.float32)

    kinds = prior_mean.shape[0]
    vectors = [down_bias, first_gain, first_shift, second_gain, second_shift, encoder_bias]
    lone = jnp.full((1,), jnp.sum(live), jnp.bfloat16)
    row = jnp.arange(16)[:, None]
    packs = jnp.where(row == 7, lone[None, :], jnp.zeros((16, rows), jnp.bfloat16))
    for n, vector in enumerate(vectors):
        packs = jnp.where(row == n + 1, vector[None, :], packs)
    packs = jnp.pad(packs, ((0, 0), (0, 128 - rows)))
    bias = jnp.pad(up_bias, (0, 128 - up_bias.shape[0]))
    packs = jnp.where(row == 0, bias[None, :], packs)
    priors = jnp.concatenate([prior_mean, prior_logvar])
    small = jnp.concatenate([jnp.pad(priors, ((0, 0), (0, 128 - priors.shape[1]))), packs])
    gather = gather_weights if total <= NARROW else gather_plain
    cells_group, embed_cols, decoder_cols, *middle, embedded = gather(
        jnp.pad(cells.T, ((0, GROUP * CHUNK - GENES), (0, 0))).reshape(GROUP, CHUNK, row_count),
        gene_chunks(embed_weight),
        gene_chunks(decoder_weight),
        query_key_value,
        small,
        output_weight,
        encoder_weight,
        up_weight,
        down_weight,
    )
    embed_cols = embed_cols.reshape(-1, CHUNK)
    decoder_cols = decoder_cols.reshape(-1, CHUNK)
    middle = [full.reshape(-1, full.shape[-1]) for full in middle]
    joint_full, small_full, output_full, encoder_full, up_full, down_full = middle
    small_full = wide(small_full.reshape(devices, 48, 128))
    up_bias_full = small_full[:, 2 * kinds, : 4 * rows].reshape(1, -1)
    vectors = small_full[:, 2 * kinds + 1 : 2 * kinds + 7, :rows].transpose(1, 0, 2).reshape(6, D)
    down_bias_full, gain_first, shift_first, gain_second, shift_second, encoder_bias_full = vectors
    prior_full = small_full[:, : 2 * kinds, : prior_mean.shape[1]]
    prior_full = prior_full.transpose(1, 0, 2).reshape(2 * kinds, LATENT)
    prior_mean_full, prior_logvar_full = prior_full[:kinds], prior_full[kinds:]
    count = jnp.sum(small_full[:, 2 * kinds + 7, 0])

    start_state = embedded + positions(coordinates)
    normed_first = layer_norm(start_state, gain_first, shift_first).astype(jnp.bfloat16)
    joint = matmul(normed_first, joint_full).astype(jnp.bfloat16)
    context, logsum = attention_forward(joint, allowed)
    middle_state = start_state + matmul(context, output_full)
    normed_second = layer_norm(middle_state, gain_second, shift_second).astype(jnp.bfloat16)
    pre = matmul(normed_second, up_full) + up_bias_full
    active = jax.nn.gelu(pre, approximate=True).astype(jnp.bfloat16)
    end_state = middle_state + (matmul(active, down_full) + down_bias_full)
    end_low = end_state.astype(jnp.bfloat16)
    encoded = matmul(end_low, encoder_full) + encoder_bias_full
    latent_mean = encoded[:, :LATENT]
    latent_logvar = encoded[:, LATENT:]
    latent = (latent_mean + jnp.exp(0.5 * latent_logvar) * noise).astype(jnp.bfloat16)
    center = jnp.dot(onehot, prior_mean_full, precision=lax.Precision.HIGHEST)
    scale = jnp.dot(onehot, prior_logvar_full, precision=lax.Precision.HIGHEST)
    gap = latent_mean - center
    inverse = jnp.exp(-scale)
    grown = jnp.exp(latent_logvar)
    diverge = 0.5 * (scale - latent_logvar + (grown + gap * gap) * inverse - 1.0)
    ratio = cell_total / count
    spread = jnp.broadcast_to(jnp.sum(live[:, None] * diverge, axis=0, keepdims=True), (8, LATENT))
    message = jnp.concatenate(
        [latent, jnp.broadcast_to(low(live)[:, None], (row_count, 128))], axis=1
    )
    latent_pass = latent_step if total <= NARROW else latent_plain
    recon_grad, decoder_term, latent_grad, spread_sum, recon_sum = latent_pass(
        message, spread, ratio.reshape(1, 1), decoder_cols, cells_group
    )
    kl_mean = spread_sum[0] / count
    shifted = (kl_mean - FREE_FLOOR) / FREE_TEMP
    free = FREE_FLOOR + FREE_TEMP * jax.nn.softplus(shifted)
    latent_grad = wide(low(latent_grad))

    kl_scale = ratio * ramp_weight * jax.nn.sigmoid(shifted)[None, :] * live[:, None]
    pulled = kl_scale * gap * inverse
    mean_grad = latent_grad + pulled
    logvar_grad = latent_grad * 0.5 * jnp.exp(0.5 * latent_logvar) * noise + kl_scale * 0.5 * (
        grown * inverse - 1.0
    )
    encoded_grad = jnp.concatenate([mean_grad, logvar_grad], axis=1).astype(jnp.bfloat16)
    prior_mean_grad = jnp.dot(onehot.T, -pulled, precision=lax.Precision.HIGHEST)
    prior_logvar_grad = jnp.dot(
        onehot.T,
        kl_scale * 0.5 * (1.0 - (grown + gap * gap) * inverse),
        precision=lax.Precision.HIGHEST,
    )
    end_grad = across(encoded_grad, encoder_full)
    branch_grad = end_grad.astype(jnp.bfloat16)
    encoder_bias_grad = jnp.sum(encoded_grad.astype(jnp.float32), axis=0)
    down_bias_grad = jnp.sum(branch_grad.astype(jnp.float32), axis=0)
    active_grad = across(branch_grad, down_full)
    gelu_value, gelu_back = jax.vjp(lambda value: jax.nn.gelu(value, approximate=True), pre)
    pre_grad = gelu_back(active_grad)[0].astype(jnp.bfloat16)
    up_bias_grad = jnp.sum(pre_grad.astype(jnp.float32), axis=0)
    second_out_grad = across(pre_grad, up_full)
    norm_value, second_back = jax.vjp(layer_norm, middle_state, gain_second, shift_second)
    state_part, second_gain_grad, second_shift_grad = second_back(second_out_grad)
    middle_grad = end_grad + state_part
    attend_grad = middle_grad.astype(jnp.bfloat16)
    context_grad = across(attend_grad, output_full).astype(jnp.bfloat16)
    joint_grad = attention_backward(joint, allowed, logsum, context_grad)
    first_out_grad = across(joint_grad, joint_full)
    first_value, first_back = jax.vjp(layer_norm, start_state, gain_first, shift_first)
    start_part, first_gain_grad, first_shift_grad = first_back(first_out_grad)
    start_grad = middle_grad + start_part
    start_low = start_grad.astype(jnp.bfloat16)
    vectors = [
        up_bias_grad,
        down_bias_grad,
        first_gain_grad,
        first_shift_grad,
        second_gain_grad,
        second_shift_grad,
        encoder_bias_grad,
    ]
    priors = jnp.concatenate([prior_mean_grad, prior_logvar_grad])
    priors = priors.reshape(2 * kinds, devices, -1).transpose(1, 0, 2).reshape(devices, -1)
    prior_size = priors.shape[1]
    packed = jnp.concatenate([v.reshape(devices, -1) for v in vectors] + [priors], axis=1)
    packed = jnp.pad(packed, ((0, 0), (0, 1024 - packed.shape[1])))
    packed = packed.reshape(total, 2, 2, 8, 128)

    scatter = scatter_sums if total <= NARROW else scatter_plain
    embed_grad, decoder_grad, cells_grad, *middle_grads, small_sum, recon_total = scatter(
        [
            (normed_first, joint_grad),
            (context, attend_grad),
            (end_low, encoded_grad),
            (normed_second, pre_grad),
            (active, branch_grad),
        ],
        start_low,
        decoder_term.reshape(total, GROUP, thin, CHUNK),
        cells_group,
        embed_cols,
        recon_grad,
        packed,
        recon_sum,
    )

    def all_genes(chunks):
        return chunks.transpose(1, 0, 2).reshape(chunks.shape[1], -1)[:, :GENES]

    cells_grad = all_genes(cells_grad)
    embed_grad = wide(all_genes(embed_grad))
    decoder_grad = wide(all_genes(decoder_grad))
    (
        joint_weight_grad,
        output_weight_grad,
        encoder_weight_grad,
        up_weight_grad,
        down_weight_grad,
    ) = middle_grads

    ends = [0]
    for vector in vectors:
        ends.append(ends[-1] + vector.shape[0] // devices)
    packed = small_sum.reshape(-1)
    vector_grads = [packed[ends[i] : ends[i + 1]] for i in range(len(vectors))]
    prior_out = packed[ends[-1] : ends[-1] + prior_size].reshape(2, kinds, -1)
    recon_total = 0.5 * jnp.sum(recon_total)
    loss = (recon_total / count + ramp_weight * jnp.sum(free)) / GENES
    return (
        loss,
        cells_grad,
        embed_grad,
        joint_weight_grad,
        output_weight_grad,
        up_weight_grad,
        vector_grads[0],
        down_weight_grad,
        vector_grads[1],
        vector_grads[2],
        vector_grads[3],
        vector_grads[4],
        vector_grads[5],
        encoder_weight_grad,
        vector_grads[6],
        prior_out[0],
        prior_out[1],
        decoder_grad,
    )


def solution(mesh):
    in_specs = (
        P(("dp", "fsdp"), None),
        P(None, ("dp", "fsdp")),
        P(("dp", "fsdp"), None),
        P(("dp", "fsdp"), None),
        P(("dp", "fsdp")),
        P(("dp", "fsdp"), None),
        P(),
        P(("dp", "fsdp"), None),
        P(("dp", "fsdp"), None),
        P(("dp", "fsdp"), None),
        P(("dp", "fsdp"), None),
        P(("dp", "fsdp")),
        P(("dp", "fsdp"), None),
        P(("dp", "fsdp")),
        P(("dp", "fsdp")),
        P(("dp", "fsdp")),
        P(("dp", "fsdp")),
        P(("dp", "fsdp")),
        P(("dp", "fsdp"), None),
        P(("dp", "fsdp")),
        P(None, ("dp", "fsdp")),
        P(None, ("dp", "fsdp")),
        P(("dp", "fsdp"), None),
    )
    out_specs = (
        P(),
        P(("dp", "fsdp"), None),
        P(("dp", "fsdp"), None),
        P(("dp", "fsdp"), None),
        P(("dp", "fsdp"), None),
        P(("dp", "fsdp"), None),
        P(("dp", "fsdp")),
        P(("dp", "fsdp"), None),
        P(("dp", "fsdp")),
        P(("dp", "fsdp")),
        P(("dp", "fsdp")),
        P(("dp", "fsdp")),
        P(("dp", "fsdp")),
        P(("dp", "fsdp"), None),
        P(("dp", "fsdp")),
        P(None, ("dp", "fsdp")),
        P(None, ("dp", "fsdp")),
        P(("dp", "fsdp"), None),
    )
    return jax.shard_map(shards, mesh=mesh, in_specs=in_specs, out_specs=out_specs, check_vma=False)
```

```python
import functools
import math

import jax
import jax.numpy as jnp
from jax import lax
from jax.experimental import pallas as pl
from jax.experimental.pallas import tpu as pltpu
from jax.sharding import PartitionSpec as P

D = 1024
HEAD_DIM = 64
GENES = 13500
LATENT = 512


NEG_SCORE = -1000000000.0
NORM_EPS = 1e-05
FREE_FLOOR = 1.0
FREE_TEMP = 0.25


def layer_norm(hidden, gain, shift):
    center = hidden - jnp.mean(hidden, axis=-1, keepdims=True)
    spread = jnp.mean(center * center, axis=-1, keepdims=True)
    return center * lax.rsqrt(spread + NORM_EPS) * gain + shift


def positions(coordinates):
    quarter = D // 4
    frequency = jnp.exp(jnp.arange(quarter, dtype=jnp.float32) * (-math.log(10000.0) / quarter))
    angle_x = coordinates[0][:, None] * frequency[None, :]
    angle_y = coordinates[1][:, None] * frequency[None, :]
    return jnp.concatenate(
        [jnp.sin(angle_x), jnp.cos(angle_x), jnp.sin(angle_y), jnp.cos(angle_y)], axis=1
    )


def matmul(left, right):
    return jnp.dot(left, right, preferred_element_type=jnp.float32)


def across(left, right):
    return lax.dot_general(
        left, right, (((1,), (1,)), ((), ())), preferred_element_type=jnp.float32
    )


def contract_rows(left, right):
    return lax.dot_general(
        left, right, (((0,), (0,)), ((), ())), preferred_element_type=jnp.float32
    )


def split_heads(joint):
    row_count = joint.shape[0]
    queries = joint[:, :D].reshape(row_count, -1, HEAD_DIM)
    keys = joint[:, D : 2 * D].reshape(row_count, -1, HEAD_DIM)
    values = joint[:, 2 * D :].reshape(row_count, -1, HEAD_DIM)
    return (queries, keys, values)


def masked_scores(queries, keys, allowed):
    scores = jnp.einsum(
        "qhd,khd->hqk", queries, keys, preferred_element_type=jnp.float32
    ) * HEAD_DIM ** (-0.5)
    return jnp.where(allowed[None], scores, NEG_SCORE)


def attention_forward(joint, allowed):
    queries, keys, values = split_heads(joint)
    masked = masked_scores(queries, keys, allowed)
    peak = jnp.max(masked, axis=-1, keepdims=True)
    raised = jnp.exp(masked - peak)
    denom = jnp.sum(raised, axis=-1, keepdims=True)
    probs = raised / denom
    logsum = peak + jnp.log(denom)
    context = jnp.einsum(
        "hqk,khd->qhd", probs.astype(jnp.bfloat16), values, preferred_element_type=jnp.float32
    )
    return (context.reshape(joint.shape[0], D).astype(jnp.bfloat16), logsum)


def attention_backward(joint, allowed, logsum, context_grad):
    row_count = joint.shape[0]
    queries, keys, values = split_heads(joint)
    probs = jnp.exp(masked_scores(queries, keys, allowed) - logsum)
    probs_low = probs.astype(jnp.bfloat16)
    incoming = context_grad.reshape(row_count, -1, HEAD_DIM)
    value_grad = jnp.einsum("hqk,qhd->khd", probs_low, incoming, preferred_element_type=jnp.float32)
    prob_grad = jnp.einsum("qhd,khd->hqk", incoming, values, preferred_element_type=jnp.float32)
    score_grad = (probs * (prob_grad - jnp.sum(probs * prob_grad, axis=-1, keepdims=True))).astype(
        jnp.bfloat16
    )
    query_grad = jnp.einsum(
        "hqk,khd->qhd", score_grad, keys, preferred_element_type=jnp.float32
    ) * HEAD_DIM ** (-0.5)
    key_grad = jnp.einsum(
        "hqk,qhd->khd", score_grad, queries, preferred_element_type=jnp.float32
    ) * HEAD_DIM ** (-0.5)
    return jnp.concatenate(
        [
            query_grad.reshape(row_count, D),
            key_grad.reshape(row_count, D),
            value_grad.reshape(row_count, D),
        ],
        axis=1,
    ).astype(jnp.bfloat16)

AXES = ("dp", "fsdp")
GROUP = 4
CHUNK = 3456
SLICE = 384
NARROW = 8


def low(values):
    return values.astype(jnp.bfloat16)


def wide(values):
    return values.astype(jnp.float32)


def device_total():
    return lax.axis_size("dp") * lax.axis_size("fsdp")


def device_index():
    return lax.axis_index("dp") * lax.axis_size("fsdp") + lax.axis_index("fsdp")


def swap(values, mask):
    return lax.ppermute(values, AXES, [(i, i ^ mask) for i in range(device_total())])


def same_quarter():
    return [[d for d in range(lax.axis_size("dp")) if d % 2 == odd] for odd in range(2)]


def pick(blocks, index):
    return lax.dynamic_index_in_dim(blocks, index, 0, keepdims=False)


def group_exchange(blocks, quarter):
    return [pick(blocks, quarter)] + [swap(pick(blocks, quarter ^ m), m) for m in range(1, GROUP)]


def group_gather(values):
    pair = jnp.stack([values, swap(values, 2)])
    other = swap(pair, 1)
    return jnp.stack([pair[0], other[0], pair[1], other[1]])


def group_scatter(parts):
    mine = jnp.stack([parts[0], parts[2]])
    theirs = low(jnp.stack([parts[1], parts[3]]))
    summed = wide(mine) + wide(swap(theirs, 1))
    return summed[0] + wide(swap(low(summed[1]), 2))


def by_quarter(pieces, quarter):
    stacked = jnp.stack(pieces)
    return [pick(stacked, quarter ^ j) for j in range(GROUP)]


def gene_chunks(values):
    padded = jnp.pad(values, ((0, 0), (0, GROUP * CHUNK - GENES)))
    return jnp.stack([padded[:, j * CHUNK : (j + 1) * CHUNK] for j in range(GROUP)])


def sum_all(values):
    mask = 1
    while mask < device_total():
        values = values + swap(values, mask)
        mask *= 2
    return values


MESH = pl.DeviceIdType.MESH


class Where:
    def __init__(self, total):
        dp = lax.axis_index("dp")
        self.total = total
        self.core = lax.axis_index("fsdp")
        self.x = dp % 2
        self.t = dp // 2
        self.quarter = 2 * self.x + self.core
        y, z = self.t % 2, self.t // 2
        self.k = z + y * (total - 1 - 2 * z)
        self.right = (2 * self.owner(-1) + self.x, self.core)
        self.left = (2 * self.owner(1) + self.x, self.core)
        self.peers = [
            None,
            (dp, 1 - self.core),
            (2 * self.t + 1 - self.x, self.core),
            (2 * self.t + 1 - self.x, 1 - self.core),
        ]
        self.quarters = [
            self.quarter,
            2 * self.x + 1 - self.core,
            2 * (1 - self.x) + self.core,
            2 * (1 - self.x) + 1 - self.core,
        ]

    def owner(self, step):
        place = (self.k - step + self.total) % self.total
        y = place // (self.total // 2)
        return 2 * (place + y * (self.total - 1 - 2 * place)) + y

    def same(self, step):
        t = (self.t + step) % self.total
        return t, (2 * t + self.x, self.core)

    def meet(self, everyone=False):
        barrier = pltpu.get_barrier_semaphore()
        others = self.peers[1:]
        if everyone:
            others = others + [self.same(step)[1] for step in range(1, self.total)]
        else:
            others = others + [self.right, self.left]
        for other in others:
            pl.semaphore_signal(barrier, inc=1, device_id=other, device_id_type=MESH)
        pl.semaphore_wait(barrier, len(others))


class Copies:
    def __init__(self, send_sems, recv_sems, local_sems):
        self.send_sems, self.recv_sems, self.local_sems = send_sems, recv_sems, local_sems
        self.remote_count = self.local_count = 0
        self.sent = []

    def send(self, source, target, device):
        at = self.remote_count
        self.remote_count += 1
        copy = pltpu.make_async_remote_copy(
            source,
            target,
            self.send_sems.at[at],
            self.recv_sems.at[at],
            device_id=device,
            device_id_type=MESH,
        )
        copy.start()
        self.sent.append(copy)
        return copy

    def local(self, source, target):
        at = self.local_count
        self.local_count += 1
        copy = pltpu.make_async_copy(source, target, self.local_sems.at[at])
        copy.start()
        return copy

    def free(self, copy):
        copy.wait_send()
        self.sent = [other for other in self.sent if other is not copy]

    def finish(self):
        for copy in self.sent:
            copy.wait_send()


def gather_kernel(total, *refs):
    (cells, embed, decoder, joint, small, output, encoder, up, down) = refs[:9]
    (cells_all, embed_all, decoder_all, joint_all, small_all) = refs[9:14]
    (output_all, encoder_all, up_all, down_all, embedded) = refs[14:19]
    (held_cells, held_embed, partial, other_core, for_x, other_x, raw, turned) = refs[19:27]
    here = Where(total)
    copies = Copies(*refs[27:])
    here.meet()
    t, x, core = here.t, here.x, here.core
    last = total - 1
    towards = {1: here.right, -1: here.left}
    flying = {}

    late = [(up, up_all, 1), (output, output_all, 1), (down, down_all, -1), (encoder, encoder_all, -1)]
    shares = {
        name: [
            copies.send(own.at[here.quarters[m]], full.at[t, here.quarter], here.peers[m])
            for m in (2, 3, 1)
        ]
        for name, own, full in (("embed", embed, embed_all), ("decoder", decoder, decoder_all))
    }
    for n, (own, full, way) in enumerate(late):
        flying["late", n] = copies.send(own, full.at[t, x, core], towards[way])
    across_x = [copies.send(own, full.at[t, x, core], here.peers[2]) for own, full, _ in late]
    reads = [copies.local(cells.at[chunk], raw.at[chunk]) for chunk in range(2)]
    shares["early"] = [
        copies.send(own, full.at[t, x, core], here.peers[2])
        for own, full in ((joint, joint_all), (small, small_all))
    ]
    own_copies = {
        "embed": [copies.local(embed.at[here.quarter], embed_all.at[t, here.quarter])],
        "decoder": [copies.local(decoder.at[here.quarter], decoder_all.at[t, here.quarter])],
        "early": [
            copies.local(own, full.at[t, x, core])
            for own, full in ((joint, joint_all), (small, small_all))
        ],
    }
    own_late = [copies.local(own, full.at[t, x, core]) for own, full, _ in late]

    def late_step(s):
        for n, (_, full, way) in enumerate(late):
            flying["late", n].wait_recv()
            block = full.at[here.owner(way * s), x, core]
            if s < last:
                flying["late", n] = copies.send(block, block, towards[way])
            across_x.append(copies.send(block, block, here.peers[2]))

    def early_block(full, way, s):
        return full.at[here.owner(way * s), 0 if way == 1 else 1, core]

    def table_block(full, way, s):
        return full.at[here.owner(way * s), pl.ds(0 if way == 1 else 2, 2)]

    rings = {
        "embed": [(embed_all, way, table_block) for way in (1, -1)],
        "decoder": [(decoder_all, way, table_block) for way in (1, -1)],
        "early": [(full, way, early_block) for full in (joint_all, small_all) for way in (1, -1)],
    }

    def step(name, s):
        if s == 0:
            for copy in own_copies[name]:
                copy.wait()
            for copy in shares[name]:
                copy.wait_recv()
        for n, (full, way, block_of) in enumerate(rings[name]):
            if s > 0:
                flying[name, n].wait_recv()
            if s < last:
                block = block_of(full, way, s)
                flying[name, n] = copies.send(block, block, towards[way])

    holds = {}

    def hold(block):
        holds[block] = copies.local(embed_all.at[block], held_embed.at[block % 2])

    def multiply(block):
        holds[block].wait()
        features = held_embed.shape[1] * held_embed.shape[2]
        table = held_embed[block % 2].reshape(features, held_embed.shape[3])
        for row in range(2):
            for column in range(2):
                partial[row, column, :, pl.ds(block * features, features)] = low(
                    across(held_cells[2 * row + column], table)
                )
        if block + 2 < total:
            hold(block + 2)

    across_core = []

    def send_cells():
        for chunk in range(GROUP):
            reads[chunk].wait()

            @pl.loop(0, CHUNK // 128)
            def _(i):
                part = pl.ds(pl.multiple_of(i * 128, 128), 128)
                turned[chunk, :, part] = low(wide(raw[chunk % 2, part, :]).T)

            if chunk + 2 < GROUP:
                reads.append(copies.local(cells.at[chunk + 2], raw.at[chunk % 2]))
        own = copies.local(turned.at[here.quarter], cells_all.at[0])
        return own, [
            copies.send(turned.at[here.quarters[m]], cells_all.at[m], here.peers[m])
            for m in (2, 3, 1)
        ]

    def to_core(copies_of, block_of):
        for copy, (_, full, way) in zip(copies_of, late):
            copy.wait_recv()
            block = block_of(full, way)
            across_core.append(copies.send(block, block, here.peers[1]))

    def crossed(s):
        to_core(
            across_x[len(late) * s : len(late) * (s + 1)],
            lambda full, way: full.at[here.owner(way * s), 1 - x, core],
        )

    for s in range(1, last + 1):
        late_step(s)
        if s == 1:
            step("embed", 0)
            own_cells, cell_moves = send_cells()
        step("embed", s)
        if s == last - 1:
            step("early", 0)
            step("decoder", 0)
    hold(0)
    hold(1)
    for copy in own_late:
        copy.wait()
    for _, full, _ in late:
        block = full.at[:, x, core]
        across_core.append(copies.send(block, block, here.peers[1]))
    for copy in cell_moves:
        copy.wait_recv()
    own_cells.wait()
    held = copies.local(cells_all, held_cells)
    step("early", 1)
    step("decoder", 1)
    held.wait()
    for s in range(2, last + 1):
        multiply(s - 2)
        step("early", s)
        step("decoder", s)
        crossed(s - 2)
    for block in range(last - 1, total):
        multiply(block)
    sums = copies.send(partial.at[:, 1], other_core, here.peers[1])
    for full in (joint_all, small_all):
        block = full.at[:, :, core]
        across_core.append(copies.send(block, block, here.peers[1]))
    sums.wait_recv()
    for_x[...] = low(wide(partial[1, 0]) + wide(other_core[1]))
    sums = copies.send(for_x, other_x, here.peers[2])
    for s in range(last - 1, total):
        crossed(s)
    sums.wait_recv()
    embedded[...] = wide(partial[0, 0]) + wide(other_core[0]) + wide(other_x[...])
    for copy in across_core:
        copy.wait_recv()
    copies.finish()


def gather_weights(cells, embed, decoder, joint, small, output, encoder, up, down):
    total = device_total() // GROUP
    own = [joint, small, output, encoder, up, down]
    tables = [embed, decoder]
    operands = [cells] + tables + own
    shapes = (
        [(GROUP, cells.shape[2], cells.shape[1])]
        + [(total,) + v.shape for v in tables]
        + [(total, 2, 2) + v.shape for v in own]
    )
    remote = 15 + 12 * (total - 1) + 8 * total + 8
    genes, cell_rows = cells.shape[1:]
    features = total * GROUP * embed.shape[1]
    by_cell = (GROUP, cell_rows, genes)
    buffers = [
        by_cell,
        (2,) + embed.shape,
        (2, 2, cell_rows, features),
        (2, cell_rows, features),
        (cell_rows, features),
        (cell_rows, features),
        (2, genes, cell_rows),
        by_cell,
    ]
    return pl.pallas_call(
        functools.partial(gather_kernel, total),
        out_shape=[jax.ShapeDtypeStruct(s, jnp.bfloat16) for s in shapes]
        + [jax.ShapeDtypeStruct((cell_rows, features), jnp.float32)],
        in_specs=[pl.BlockSpec(memory_space=pl.ANY)] * len(operands),
        out_specs=[pl.BlockSpec(memory_space=pl.ANY)] * len(operands)
        + [pl.BlockSpec(memory_space=pltpu.VMEM)],
        scratch_shapes=[pltpu.VMEM(shape, jnp.bfloat16) for shape in buffers]
        + [
            pltpu.SemaphoreType.DMA((remote,)),
            pltpu.SemaphoreType.DMA((remote,)),
            pltpu.SemaphoreType.DMA((14 + total,)),
        ],
        compiler_params=pltpu.CompilerParams(
            collective_id=1, has_side_effects=True, vmem_limit_bytes=20 * 2**20
        ),
        name="gather_weights",
    )(*operands)


def add_rows(target, first, second, dtype):
    rows, columns = target.shape
    step = min(rows, 16 if columns > 2048 else 32)

    @pl.loop(0, rows // step)
    def _(i):
        part = pl.ds(pl.multiple_of(i * step, step), step)
        target[part, :] = (wide(first[part, :]) + wide(second[part, :])).astype(dtype)


def product(target, left, right, accumulate):
    total, _, rows, columns = target.shape
    step = 256 // (2 * rows)
    width = 512

    @pl.loop(0, total // step)
    def _(i):
        blocks = pl.ds(i * step, step)
        part = left(i * 2 * step, 2 * step)

        @pl.loop(0, columns // width)
        def _(n):
            across_columns = pl.ds(pl.multiple_of(n * width, width), width)
            value = matmul(part, right[:, across_columns]).reshape(step, 2, rows, width)
            if accumulate:
                value = value + wide(target[blocks, :, :, across_columns])
            target[blocks, :, :, across_columns] = low(value)


MIDDLE = ("joint", "output", "encoder", "up", "down")


def scatter_kernel(total, *refs):
    (recon, start, small, decoder, cells, table, grads) = refs[:7]
    left = dict(zip(MIDDLE, refs[7:12]))
    right = dict(zip(MIDDLE, refs[12:17]))
    (embed_out, decoder_out, cells_out, embed, back) = refs[17:22]
    results = dict(zip(MIDDLE, refs[22:27]))
    (small_out, recon_out) = refs[27:29]
    (chip_small, stage_small, sum_small, hop_small, group_recon, all_recon) = refs[29:35]
    chip = dict(zip(MIDDLE, refs[35:40]))
    (send_up, send_down) = refs[40:42]
    sums = dict(zip(MIDDLE[1:], refs[42:46]))
    (hop_embed, hop_decoder, hop_joint) = refs[46:49]
    hops_of = dict(zip(MIDDLE[1:], refs[49:53]))
    (local_embed, local_decoder) = refs[53:55]
    (other_joint, starts, turned) = refs[55:58]
    (in_cells, in_table, in_grads, out_term, out_back, blocks) = refs[58:64]
    here = Where(total)
    copies = Copies(*refs[64:67])
    stream_sems = refs[67]
    here.meet()
    x, core, last = here.x, here.core, total - 1
    towards = {1: here.right, -1: here.left}
    flying = {}

    def lanes(term, hops, local):
        return [(term, hops, local, way, side) for side, way in ((0, 1), (1, -1))]

    tables = {
        "embed": lanes(embed, hop_embed, local_embed),
        "decoder": lanes(decoder, hop_decoder, local_decoder),
    }

    def table_block(term, way, side, h):
        return term.at[here.owner(way * h), pl.ds(2 * side, 2)]

    def fetch(name, h):
        for n, (term, _, local, way, side) in enumerate(tables[name]):
            flying["local", name, n, h] = copies.local(
                table_block(term, way, side, h + 1), local.at[h % 2, side]
            )

    def table_start(name):
        for n, (term, hops, _, way, side) in enumerate(tables[name]):
            flying[name, n] = copies.send(
                table_block(term, way, side, 1), hops.at[0, side], towards[way]
            )
        fetch(name, 1)
        fetch(name, 2)

    def table_hop(name, h):
        for n, (_, hops, local, way, side) in enumerate(tables[name]):
            flying[name, n].wait_recv()
            flying["local", name, n, h].wait()
            for row in range(2):
                arrived = hops.at[h - 1, side, row]
                add_rows(arrived, arrived, local.at[h % 2, side, row], jnp.bfloat16)
            if h < last:
                flying[name, n] = copies.send(hops.at[h - 1, side], hops.at[h, side], towards[way])
        if h + 2 <= last:
            fetch(name, h + 2)

    table_start("decoder")
    moves = [copies.send(start, starts.at[m], here.peers[m]) for m in (2, 1)]
    starts[0] = start[...]
    group_recon[here.quarter] = recon[...]
    recons = [copies.send(recon, group_recon.at[here.quarter], here.peers[m]) for m in (2, 3, 1)]
    halves = {"small": copies.send(small.at[:, :, 1 - core], chip_small, here.peers[1])}
    own_small = copies.local(small.at[:, :, core], stage_small)

    def half(name, which):
        source = left[name]
        if results[name].shape[0] == 128:

            def wide_blocks(first, size):
                lanes = [
                    pl.ds(pl.multiple_of((2 * (first + n) + which) * 128, 128), 128)
                    for n in range(size)
                ]
                return jnp.concatenate([low(wide(source[:, part]).T) for part in lanes])

            return wide_blocks
        blocks[...] = low(wide(source[...]).T).reshape(blocks.shape)

        def narrow_blocks(first, size):
            return blocks[pl.ds(first, size), which].reshape(-1, blocks.shape[-1])

        return narrow_blocks

    def give(name, buffer):
        product(buffer, half(name, 1 - core), right[name], False)
        halves[name] = copies.send(buffer, chip[name], here.peers[1])

    across = {}

    def cross(name, held, target):
        across[name] = copies.send(held.at[:, 1 - x], target, here.peers[2])

    def take(name):
        halves[name].wait_recv()
        product(chip[name], half(name, core), right[name], True)
        if name in sums:
            cross(name, chip[name], sums[name])

    give("up", send_up)
    give("down", send_down)
    moves[0].wait_recv()
    moves[0] = copies.send(starts.at[2], starts.at[3], here.peers[1])
    table_hop("decoder", 1)
    take("up")
    copies.free(halves["up"])
    give("joint", send_up.at[:, :, :, pl.ds(0, right["joint"].shape[1])])
    table_hop("decoder", 2)
    take("down")
    copies.free(halves["down"])
    slim = results["output"].shape[0]
    give("output", send_down.at[:, :, pl.ds(0, slim)])
    give("encoder", send_down.at[:, :, pl.ds(slim, slim)])
    table_hop("decoder", 3)
    take("joint")
    for side, way in ((0, 1), (1, -1)):
        flying["joint", side] = copies.send(
            chip["joint"].at[here.owner(way), side], hop_joint.at[0, side], towards[way]
        )
    take("output")
    take("encoder")
    own_small.wait()
    halves["small"].wait_recv()

    @pl.loop(0, total)
    def _(t):
        for side in range(2):
            held = chip_small.at[t, side]
            add_rows(held, held, stage_small.at[t, side], jnp.float32)

    cross("small", chip_small, sum_small)
    for copy in recons:
        copy.wait_recv()
    all_recon[here.t] = group_recon[0] + group_recon[1] + group_recon[2] + group_recon[3]
    own_recon = all_recon.at[here.t]
    flying["recon"] = copies.send(own_recon, own_recon, here.right)
    table_hop("decoder", 4)

    def joint_hop(h):
        for side, way in ((0, 1), (1, -1)):
            flying["joint", side].wait_recv()
            arrived = hop_joint.at[h - 1, side]
            local = chip["joint"].at[here.owner(way * (h + 1)), side]
            add_rows(arrived, arrived, local, jnp.bfloat16)
            if h < last:
                flying["joint", side] = copies.send(arrived, hop_joint.at[h, side], towards[way])

    for copy in moves:
        copy.wait_recv()
    moves = []
    rows, rows_of_t = start.shape[0], turned.shape[0] // total
    for m in range(GROUP):
        turned[:, m * rows : (m + 1) * rows] = low(wide(starts[m]).T)

    def moved(i, pairs, first):
        part = pl.ds(pl.multiple_of(i * SLICE, 128), SLICE)
        slot = i % 2
        return [
            pltpu.make_async_copy(*ends(part, slot), stream_sems.at[first + n, slot])
            for n, ends in enumerate(pairs)
        ]

    def loads_of(i):
        return moved(
            i,
            [
                lambda part, slot: (cells.at[:, :, part], in_cells.at[slot]),
                lambda part, slot: (table.at[:, part], in_table.at[slot]),
                lambda part, slot: (grads.at[:, :, part], in_grads.at[slot]),
            ],
            0,
        )

    def stores_of(i):
        return moved(
            i,
            [
                lambda part, slot: (out_term.at[slot], embed.at[:, :, :, part]),
                lambda part, slot: (out_back.at[slot], back.at[:, part, :]),
            ],
            3,
        )

    count = CHUNK // SLICE
    for copy in loads_of(0):
        copy.start()

    def stream(first, end):
        @pl.loop(first, end)
        def _(i):
            slot = i % 2
            @pl.when(i + 1 < count)
            def _():
                for copy in loads_of(i + 1):
                    copy.start()

            for copy in loads_of(i):
                copy.wait()

            @pl.when(i >= 2)
            def _():
                for copy in stores_of(i - 2):
                    copy.wait()

            for t in range(total):
                term = matmul(
                    turned[pl.ds(t * rows_of_t, rows_of_t), :],
                    in_cells[slot].reshape(GROUP * rows, SLICE),
                )
                out_term[slot, t] = low(term).reshape(out_term.shape[2:])
            for m in range(GROUP):
                value = matmul(starts[m], in_table[slot]) - wide(in_grads[slot, m])
                out_back[slot, m] = low(value.T)
            for copy in stores_of(i):
                copy.start()

    joint_hop(1)
    stream(0, count // 3)
    table_hop("decoder", 5)
    joint_hop(2)
    stream(count // 3, 2 * count // 3)
    table_hop("decoder", 6)
    joint_hop(3)
    stream(2 * count // 3, count)
    for i in (count - 2, count - 1):
        for copy in stores_of(i):
            copy.wait()
    table_start("embed")
    moves = [copies.send(back.at[m], cells_out.at[here.quarter], here.peers[m]) for m in (2, 3, 1)]
    own = [copies.local(back.at[0], cells_out.at[here.quarter])]
    table_hop("decoder", last)

    def send_back(hops, out):
        done = [hops.at[last - 1, quarter // 2, quarter % 2] for quarter in here.quarters]
        for m in (2, 3, 1):
            moves.append(copies.send(done[m], out.at[here.quarter], here.peers[m]))
        own.append(copies.local(done[0], out.at[here.quarter]))

    send_back(hop_decoder, decoder_out)

    def recon_hop(h):
        flying["recon"].wait_recv()
        if h < last:
            arrived = all_recon.at[here.owner(h)]
            flying["recon"] = copies.send(arrived, arrived, here.right)

    late = [
        (name, sums[name], chip[name], hops_of[name], results[name], way)
        for name, way in (("up", 1), ("down", -1), ("output", 1), ("encoder", -1))
    ] + [("small", sum_small, chip_small, hop_small, small_out, 1)]

    def late_start():
        for name, summed, held, hops, _, way in late:
            across[name].wait_recv()

            @pl.loop(0, total)
            def _(t):
                add_rows(summed.at[t], summed.at[t], held.at[t, x], summed.dtype)

            flying["late", name] = copies.send(summed.at[here.owner(way)], hops.at[0], towards[way])

    def late_hop(h):
        for name, summed, _, hops, result, way in late:
            flying["late", name].wait_recv()
            local = summed.at[here.owner(way * (h + 1))]
            if h < last:
                add_rows(hops.at[h - 1], hops.at[h - 1], local, hops.dtype)
                flying["late", name] = copies.send(hops.at[h - 1], hops.at[h], towards[way])
            else:
                add_rows(result, hops.at[h - 1], local, jnp.float32)

    for h in range(1, last + 1):
        if h + 3 <= last:
            joint_hop(h + 3)
        table_hop("embed", h)
        recon_hop(h)
    send_back(hop_embed, embed_out)
    done_joint = hop_joint.at[last - 1]
    joint_move = copies.send(done_joint.at[1 - x], other_joint, here.peers[2])
    late_start()
    for h in range(1, last + 1):
        late_hop(h)
    summed = all_recon[0]
    for t in range(1, total):
        summed = summed + all_recon[t]
    recon_out[...] = summed
    joint_move.wait_recv()
    add_rows(results["joint"], done_joint.at[x], other_joint, jnp.float32)
    for copy in moves:
        copy.wait_recv()
    for copy in own:
        copy.wait()
    copies.finish()


def scatter_sums(pairs, start, decoder, cells, table, grads, small, recon):
    total = device_total() // GROUP
    last = total - 1
    rows, features = start.shape
    thin = jnp.bfloat16
    share = features // (total * GROUP)
    lefts, rights, shapes = [], [], []
    for before, after in pairs:
        block = before.shape[1] // device_total()
        lefts.append(before)
        rights.append(after)
        shapes.append((block, after.shape[1]))
    operands = [recon, start, small, decoder, cells, table, grads] + lefts + rights
    decoder_share = decoder.shape[1:]
    embed_share, by_gene = (GROUP, share, CHUNK), (GROUP, CHUNK, rows)
    out_shape = [
        jax.ShapeDtypeStruct(v, thin)
        for v in (embed_share, decoder_share, by_gene, (total,) + embed_share, by_gene)
    ]
    block = small.shape[3:]
    out_shape += [jax.ShapeDtypeStruct(v, jnp.float32) for v in shapes + [block, recon.shape]]
    exact = [(total, 2) + block, (total, 2) + block, (total,) + block, (last,) + block]
    exact += [(GROUP,) + recon.shape, (total,) + recon.shape]
    chips = [(total, 2) + v for v in shapes]
    buffers = chips + [chips[3], chips[4]] + [(total,) + v for v in shapes[1:]]
    buffers += [(last, 2, 2) + v[1:] for v in (embed_share, decoder_share)]
    buffers += [(last, 2) + shapes[0]] + [(last,) + v for v in shapes[1:]]
    buffers += [(2, 2, 2) + v[1:] for v in (embed_share, decoder_share)]
    buffers += [shapes[0], (GROUP,) + start.shape, (features, GROUP * rows)]
    buffers += [(2, GROUP, rows, SLICE), (2, features, SLICE), (2, GROUP, rows, SLICE)]
    buffers += [(2, total, GROUP, share, SLICE), (2, GROUP, SLICE, rows)]
    buffers += [(2 * total, 2, shapes[0][0], rows)]
    remote, here = 12 + 6 * last + 4 * last + 15 + 2 * last, 4 * last + 9
    anywhere, vmem = pl.BlockSpec(memory_space=pl.ANY), pl.BlockSpec(memory_space=pltpu.VMEM)
    outs = pl.pallas_call(
        functools.partial(scatter_kernel, total),
        out_shape=out_shape,
        in_specs=[vmem] * 2 + [anywhere] * 5 + [vmem] * 10,
        out_specs=[anywhere] * 5 + [vmem] * 7,
        scratch_shapes=[pltpu.VMEM(shape, jnp.float32) for shape in exact]
        + [pltpu.VMEM(shape, thin) for shape in buffers]
        + [
            pltpu.SemaphoreType.DMA((remote,)),
            pltpu.SemaphoreType.DMA((remote,)),
            pltpu.SemaphoreType.DMA((here,)),
            pltpu.SemaphoreType.DMA((5, 2)),
        ],
        compiler_params=pltpu.CompilerParams(
            collective_id=2, has_side_effects=True, vmem_limit_bytes=60 * 2**20
        ),
        name="scatter_sums",
    )(*operands)
    return outs[:3] + outs[5:]


def scatter_plain(pairs, start, decoder, cells, table, grads, small, recon):
    quarter = device_index() % GROUP
    total = device_total() // GROUP
    starts = group_gather(start).reshape(-1, start.shape[1])
    wide_cells = cells.reshape(-1, CHUNK)
    embed = low(contract_rows(starts, wide_cells)).reshape(total, GROUP, -1, CHUNK)
    back = low(matmul(starts, table) - wide(grads.reshape(-1, CHUNK))).reshape(cells.shape)

    def sent(blocks):
        pieces = [pick(blocks, 0)] + [swap(blocks[m], m) for m in range(1, GROUP)]
        return jnp.stack(by_quarter(pieces, quarter))

    def table_sum(term):
        block = lax.psum_scatter(
            term, "dp", axis_index_groups=same_quarter(), scatter_dimension=0, tiled=False
        )
        return sent(jnp.stack(by_quarter(list(block), quarter)))

    def middle(term):
        rows = term.reshape((device_total(), -1) + term.shape[-1:])
        return wide(lax.psum_scatter(rows, AXES, scatter_dimension=0, tiled=False))

    terms = [low(contract_rows(before, after)) for before, after in pairs]
    small = small.reshape((device_total(),) + small.shape[3:])
    return (
        [table_sum(embed), table_sum(decoder), sent(back).transpose(0, 2, 1)]
        + [middle(term) for term in terms]
        + [lax.psum_scatter(small, AXES, scatter_dimension=0, tiled=False), sum_all(recon)]
    )


def latent_kernel(total, *refs):
    (message, spread, ratio, decoder, cells) = refs[:5]
    (recon_grad, decoder_term, latent_grad, spread_sum, recon_sum) = refs[5:10]
    (latents, held_decoder, held_cells, held_grad, held_term, turned, partial) = refs[10:17]
    (leaving, arriving, group_spread, all_spread) = refs[17:21]
    here = Where(total)
    copies = Copies(*refs[21:])
    here.meet(everyone=True)
    arrivals = {m: copies.send(message, latents.at[m], here.peers[m]) for m in (1, 2, 3)}
    spreads = [copies.send(spread, group_spread.at[here.quarter], here.peers[m]) for m in (2, 3, 1)]
    loads = [
        copies.local(message, latents.at[0]),
        copies.local(decoder, held_decoder),
        copies.local(cells, held_cells),
    ]
    group_spread[here.quarter] = spread[...]
    for copy in spreads:
        copy.wait_recv()
    all_spread[here.t] = (
        group_spread[0] + group_spread[1] + group_spread[2] + group_spread[3]
    )
    spreads = []
    for away in range(1, total):
        own = all_spread.at[here.t]
        spreads.append(copies.send(own, own, here.same(away)[1]))
    for copy in loads:
        copy.wait()
    rows = message.shape[0]
    size = held_decoder.shape[0]
    partial[...] = jnp.zeros_like(partial)
    recon_sum[...] = jnp.zeros_like(recon_sum)

    both = 2 * rows

    def reconstruct(pair):
        at = pl.ds(2 * pair, 2)
        for m in (2 * pair, 2 * pair + 1):
            turned[:, m * rows : (m + 1) * rows] = low(wide(latents[m, :, :size]).T)
        values = latents[at, :, :size].reshape(both, size)
        live = wide(latents[at, :, size : size + 128]).reshape(both, 128)
        live = jnp.concatenate([live] * (SLICE // 128), axis=1)

        @pl.loop(0, CHUNK // SLICE)
        def _(i):
            part = pl.ds(pl.multiple_of(i * SLICE, 128), SLICE)
            table = held_decoder[:, part]
            miss = matmul(values, table) - wide(held_cells[at, :, part]).reshape(both, SLICE)
            weighted = live * miss
            recon_sum[...] += jnp.sum((weighted * miss).reshape(both // 8, 8, SLICE), axis=0)
            grad = low(ratio[0, 0] * weighted)
            held_grad[at, :, part] = grad.reshape(2, rows, SLICE)
            partial[at] += across(grad, table).reshape(2, rows, size)

    arrivals[1].wait_recv()
    reconstruct(0)
    leaving[1] = low(partial[1])
    returns = [copies.send(leaving.at[1], arriving.at[0], here.peers[1])]
    for m in (2, 3):
        arrivals[m].wait_recv()
    reconstruct(1)
    for m in (2, 3):
        leaving[m] = low(partial[m])
        returns.append(copies.send(leaving.at[m], arriving.at[m - 1], here.peers[m]))

    @pl.loop(0, CHUNK // SLICE)
    def _(i):
        part = pl.ds(pl.multiple_of(i * SLICE, 128), SLICE)
        grads = held_grad[:, :, part].reshape(GROUP * rows, SLICE)
        held_term[:, part] = low(matmul(turned[...], grads))

    stores = [copies.local(held_grad, recon_grad), copies.local(held_term, decoder_term)]
    for copy in spreads:
        copy.wait_recv()
    summed = all_spread[0]
    for t in range(1, total):
        summed = summed + all_spread[t]
    spread_sum[...] = summed
    for copy in returns:
        copy.wait_recv()
    latent_grad[...] = (
        (partial[0] + wide(arriving[0])) + (wide(arriving[1]) + wide(arriving[2]))
    )
    for copy in stores:
        copy.wait()
    copies.finish()


def latent_step(message, spread, ratio, decoder, cells):
    total = device_total() // GROUP
    rows, size = message.shape[0], decoder.shape[0]
    thin = jnp.bfloat16
    vmem = pl.BlockSpec(memory_space=pltpu.VMEM)
    anywhere = pl.BlockSpec(memory_space=pl.ANY)
    remote = 9 + total - 1
    return pl.pallas_call(
        functools.partial(latent_kernel, total),
        out_shape=[
            jax.ShapeDtypeStruct(cells.shape, thin),
            jax.ShapeDtypeStruct(decoder.shape, thin),
            jax.ShapeDtypeStruct((rows, size), jnp.float32),
            jax.ShapeDtypeStruct(spread.shape, jnp.float32),
            jax.ShapeDtypeStruct((8, SLICE), jnp.float32),
        ],
        in_specs=[vmem, vmem, pl.BlockSpec(memory_space=pltpu.SMEM), anywhere, anywhere],
        out_specs=[anywhere, anywhere, vmem, vmem, vmem],
        scratch_shapes=[
            pltpu.VMEM((GROUP,) + message.shape, thin),
            pltpu.VMEM(decoder.shape, thin),
            pltpu.VMEM(cells.shape, thin),
            pltpu.VMEM(cells.shape, thin),
            pltpu.VMEM(decoder.shape, thin),
            pltpu.VMEM((size, GROUP * rows), thin),
            pltpu.VMEM((GROUP, rows, size), jnp.float32),
            pltpu.VMEM((GROUP, rows, size), thin),
            pltpu.VMEM((GROUP - 1, rows, size), thin),
            pltpu.VMEM((GROUP,) + spread.shape, jnp.float32),
            pltpu.VMEM((total,) + spread.shape, jnp.float32),
            pltpu.SemaphoreType.DMA((remote,)),
            pltpu.SemaphoreType.DMA((remote,)),
            pltpu.SemaphoreType.DMA((5,)),
        ],
        compiler_params=pltpu.CompilerParams(
            collective_id=3, has_side_effects=True, vmem_limit_bytes=40 * 2**20
        ),
        name="latent_step",
    )(message, spread, ratio, decoder, cells)


def latent_plain(message, spread, ratio, decoder, cells):
    size = decoder.shape[0]
    gathered = group_gather(message).reshape(-1, message.shape[1])
    latents, live = gathered[:, :size], wide(gathered[:, size : size + 1])
    miss = matmul(latents, decoder) - wide(cells.reshape(-1, CHUNK))
    grad = low(ratio[0, 0] * live * miss)
    recon_sum = jnp.sum((live * miss * miss).reshape(-1, 8, CHUNK), axis=0)
    latent_grad = group_scatter(low(across(grad, decoder)).reshape(GROUP, -1, size))
    term = low(contract_rows(latents, grad))
    return grad.reshape(cells.shape), term, latent_grad, sum_all(spread), recon_sum


def gather_plain(cells, embed, decoder, *own):
    quarter = device_index() % GROUP
    total = device_total() // GROUP
    groups = same_quarter()

    def table(values):
        block = jnp.stack(by_quarter(group_exchange(values, quarter), quarter))
        return lax.all_gather(block, "dp", axis_index_groups=groups, axis=0, tiled=False)

    cells = cells.transpose(0, 2, 1)
    cells_all = jnp.stack(group_exchange(cells, quarter))
    embed_all = table(embed)
    rows, genes = cells.shape[1:]
    embedded = low(across(cells_all.reshape(-1, genes), embed_all.reshape(-1, genes)))
    embedded = group_scatter(embedded.reshape(GROUP, rows, -1))
    middle = [lax.all_gather(v, AXES, axis=0, tiled=False) for v in own]
    return [cells_all, embed_all, table(decoder)] + middle + [embedded]


def shards(
    cells,
    coordinates,
    slide_ids,
    live_mask,
    components,
    noise,
    ramp_weight,
    embed_weight,
    query_key_value,
    output_weight,
    up_weight,
    up_bias,
    down_weight,
    down_bias,
    first_gain,
    first_shift,
    second_gain,
    second_shift,
    encoder_weight,
    encoder_bias,
    prior_mean,
    prior_logvar,
    decoder_weight,
):
    row_count = cells.shape[0]
    devices = device_total()
    total = devices // GROUP
    me = device_index()
    quarter = me % GROUP
    rows = embed_weight.shape[0]
    thin = decoder_weight.shape[0]
    cell_total = row_count * devices
    live = live_mask[0].astype(jnp.float32)
    slides = slide_ids[0]
    places = jnp.arange(row_count)
    allowed = (slides[:, None] == slides[None, :]) & (
        (live[None, :] > 0.5) | (places[:, None] == places[None, :])
    )
    onehot = (
        components[:, None] == jnp.arange(prior_mean.shape[0], dtype=jnp.int32)[None, :]
    ).astype(jnp.float32)

    kinds = prior_mean.shape[0]
    vectors = [down_bias, first_gain, first_shift, second_gain, second_shift, encoder_bias]
    lone = jnp.full((1,), jnp.sum(live), jnp.bfloat16)
    row = jnp.arange(16)[:, None]
    packs = jnp.where(row == 7, lone[None, :], jnp.zeros((16, rows), jnp.bfloat16))
    for n, vector in enumerate(vectors):
        packs = jnp.where(row == n + 1, vector[None, :], packs)
    packs = jnp.pad(packs, ((0, 0), (0, 128 - rows)))
    bias = jnp.pad(up_bias, (0, 128 - up_bias.shape[0]))
    packs = jnp.where(row == 0, bias[None, :], packs)
    priors = jnp.concatenate([prior_mean, prior_logvar])
    small = jnp.concatenate([jnp.pad(priors, ((0, 0), (0, 128 - priors.shape[1]))), packs])
    gather = gather_weights if total <= NARROW else gather_plain
    cells_group, embed_cols, decoder_cols, *middle, embedded = gather(
        jnp.pad(cells.T, ((0, GROUP * CHUNK - GENES), (0, 0))).reshape(GROUP, CHUNK, row_count),
        gene_chunks(embed_weight),
        gene_chunks(decoder_weight),
        query_key_value,
        small,
        output_weight,
        encoder_weight,
        up_weight,
        down_weight,
    )
    embed_cols = embed_cols.reshape(-1, CHUNK)
    decoder_cols = decoder_cols.reshape(-1, CHUNK)
    middle = [full.reshape(-1, full.shape[-1]) for full in middle]
    joint_full, small_full, output_full, encoder_full, up_full, down_full = middle
    small_full = wide(small_full.reshape(devices, 48, 128))
    up_bias_full = small_full[:, 2 * kinds, : 4 * rows].reshape(1, -1)
    vectors = small_full[:, 2 * kinds + 1 : 2 * kinds + 7, :rows].transpose(1, 0, 2).reshape(6, D)
    down_bias_full, gain_first, shift_first, gain_second, shift_second, encoder_bias_full = vectors
    prior_full = small_full[:, : 2 * kinds, : prior_mean.shape[1]]
    prior_full = prior_full.transpose(1, 0, 2).reshape(2 * kinds, LATENT)
    prior_mean_full, prior_logvar_full = prior_full[:kinds], prior_full[kinds:]
    count = jnp.sum(small_full[:, 2 * kinds + 7, 0])

    start_state = embedded + positions(coordinates)
    normed_first = layer_norm(start_state, gain_first, shift_first).astype(jnp.bfloat16)
    joint = matmul(normed_first, joint_full).astype(jnp.bfloat16)
    context, logsum = attention_forward(joint, allowed)
    middle_state = start_state + matmul(context, output_full)
    normed_second = layer_norm(middle_state, gain_second, shift_second).astype(jnp.bfloat16)
    pre = matmul(normed_second, up_full) + up_bias_full
    active = jax.nn.gelu(pre, approximate=True).astype(jnp.bfloat16)
    end_state = middle_state + (matmul(active, down_full) + down_bias_full)
    end_low = end_state.astype(jnp.bfloat16)
    encoded = matmul(end_low, encoder_full) + encoder_bias_full
    latent_mean = encoded[:, :LATENT]
    latent_logvar = encoded[:, LATENT:]
    latent = (latent_mean + jnp.exp(0.5 * latent_logvar) * noise).astype(jnp.bfloat16)
    center = jnp.dot(onehot, prior_mean_full, precision=lax.Precision.HIGHEST)
    scale = jnp.dot(onehot, prior_logvar_full, precision=lax.Precision.HIGHEST)
    gap = latent_mean - center
    inverse = jnp.exp(-scale)
    grown = jnp.exp(latent_logvar)
    diverge = 0.5 * (scale - latent_logvar + (grown + gap * gap) * inverse - 1.0)
    ratio = cell_total / count
    spread = jnp.broadcast_to(jnp.sum(live[:, None] * diverge, axis=0, keepdims=True), (8, LATENT))
    message = jnp.concatenate(
        [latent, jnp.broadcast_to(low(live)[:, None], (row_count, 128))], axis=1
    )
    latent_pass = latent_step if total <= NARROW else latent_plain
    recon_grad, decoder_term, latent_grad, spread_sum, recon_sum = latent_pass(
        message, spread, ratio.reshape(1, 1), decoder_cols, cells_group
    )
    kl_mean = spread_sum[0] / count
    shifted = (kl_mean - FREE_FLOOR) / FREE_TEMP
    free = FREE_FLOOR + FREE_TEMP * jax.nn.softplus(shifted)
    latent_grad = wide(low(latent_grad))

    kl_scale = ratio * ramp_weight * jax.nn.sigmoid(shifted)[None, :] * live[:, None]
    pulled = kl_scale * gap * inverse
    mean_grad = latent_grad + pulled
    logvar_grad = latent_grad * 0.5 * jnp.exp(0.5 * latent_logvar) * noise + kl_scale * 0.5 * (
        grown * inverse - 1.0
    )
    encoded_grad = jnp.concatenate([mean_grad, logvar_grad], axis=1).astype(jnp.bfloat16)
    prior_mean_grad = jnp.dot(onehot.T, -pulled, precision=lax.Precision.HIGHEST)
    prior_logvar_grad = jnp.dot(
        onehot.T,
        kl_scale * 0.5 * (1.0 - (grown + gap * gap) * inverse),
        precision=lax.Precision.HIGHEST,
    )
    end_grad = across(encoded_grad, encoder_full)
    branch_grad = end_grad.astype(jnp.bfloat16)
    encoder_bias_grad = jnp.sum(encoded_grad.astype(jnp.float32), axis=0)
    down_bias_grad = jnp.sum(branch_grad.astype(jnp.float32), axis=0)
    active_grad = across(branch_grad, down_full)
    gelu_value, gelu_back = jax.vjp(lambda value: jax.nn.gelu(value, approximate=True), pre)
    pre_grad = gelu_back(active_grad)[0].astype(jnp.bfloat16)
    up_bias_grad = jnp.sum(pre_grad.astype(jnp.float32), axis=0)
    second_out_grad = across(pre_grad, up_full)
    norm_value, second_back = jax.vjp(layer_norm, middle_state, gain_second, shift_second)
    state_part, second_gain_grad, second_shift_grad = second_back(second_out_grad)
    middle_grad = end_grad + state_part
    attend_grad = middle_grad.astype(jnp.bfloat16)
    context_grad = across(attend_grad, output_full).astype(jnp.bfloat16)
    joint_grad = attention_backward(joint, allowed, logsum, context_grad)
    first_out_grad = across(joint_grad, joint_full)
    first_value, first_back = jax.vjp(layer_norm, start_state, gain_first, shift_first)
    start_part, first_gain_grad, first_shift_grad = first_back(first_out_grad)
    start_grad = middle_grad + start_part
    start_low = start_grad.astype(jnp.bfloat16)
    vectors = [
        up_bias_grad,
        down_bias_grad,
        first_gain_grad,
        first_shift_grad,
        second_gain_grad,
        second_shift_grad,
        encoder_bias_grad,
    ]
    priors = jnp.concatenate([prior_mean_grad, prior_logvar_grad])
    priors = priors.reshape(2 * kinds, devices, -1).transpose(1, 0, 2).reshape(devices, -1)
    prior_size = priors.shape[1]
    packed = jnp.concatenate([v.reshape(devices, -1) for v in vectors] + [priors], axis=1)
    packed = jnp.pad(packed, ((0, 0), (0, 1024 - packed.shape[1])))
    packed = packed.reshape(total, 2, 2, 8, 128)

    scatter = scatter_sums if total <= NARROW else scatter_plain
    embed_grad, decoder_grad, cells_grad, *middle_grads, small_sum, recon_total = scatter(
        [
            (normed_first, joint_grad),
            (context, attend_grad),
            (end_low, encoded_grad),
            (normed_second, pre_grad),
            (active, branch_grad),
        ],
        start_low,
        decoder_term.reshape(total, GROUP, thin, CHUNK),
        cells_group,
        embed_cols,
        recon_grad,
        packed,
        recon_sum,
    )

    def all_genes(chunks):
        return chunks.transpose(1, 0, 2).reshape(chunks.shape[1], -1)[:, :GENES]

    cells_grad = cells_grad.reshape(GROUP * CHUNK, row_count)[:GENES].T
    embed_grad = wide(all_genes(embed_grad))
    decoder_grad = wide(all_genes(decoder_grad))
    (
        joint_weight_grad,
        output_weight_grad,
        encoder_weight_grad,
        up_weight_grad,
        down_weight_grad,
    ) = middle_grads

    ends = [0]
    for vector in vectors:
        ends.append(ends[-1] + vector.shape[0] // devices)
    packed = small_sum.reshape(-1)
    vector_grads = [packed[ends[i] : ends[i + 1]] for i in range(len(vectors))]
    prior_out = packed[ends[-1] : ends[-1] + prior_size].reshape(2, kinds, -1)
    recon_total = 0.5 * jnp.sum(recon_total)
    loss = (recon_total / count + ramp_weight * jnp.sum(free)) / GENES
    return (
        loss,
        cells_grad,
        embed_grad,
        joint_weight_grad,
        output_weight_grad,
        up_weight_grad,
        vector_grads[0],
        down_weight_grad,
        vector_grads[1],
        vector_grads[2],
        vector_grads[3],
        vector_grads[4],
        vector_grads[5],
        encoder_weight_grad,
        vector_grads[6],
        prior_out[0],
        prior_out[1],
        decoder_grad,
    )


def solution(mesh):
    in_specs = (
        P(("dp", "fsdp"), None),
        P(None, ("dp", "fsdp")),
        P(("dp", "fsdp"), None),
        P(("dp", "fsdp"), None),
        P(("dp", "fsdp")),
        P(("dp", "fsdp"), None),
        P(),
        P(("dp", "fsdp"), None),
        P(("dp", "fsdp"), None),
        P(("dp", "fsdp"), None),
        P(("dp", "fsdp"), None),
        P(("dp", "fsdp")),
        P(("dp", "fsdp"), None),
        P(("dp", "fsdp")),
        P(("dp", "fsdp")),
        P(("dp", "fsdp")),
        P(("dp", "fsdp")),
        P(("dp", "fsdp")),
        P(("dp", "fsdp"), None),
        P(("dp", "fsdp")),
        P(None, ("dp", "fsdp")),
        P(None, ("dp", "fsdp")),
        P(("dp", "fsdp"), None),
    )
    out_specs = (
        P(),
        P(("dp", "fsdp"), None),
        P(("dp", "fsdp"), None),
        P(("dp", "fsdp"), None),
        P(("dp", "fsdp"), None),
        P(("dp", "fsdp"), None),
        P(("dp", "fsdp")),
        P(("dp", "fsdp"), None),
        P(("dp", "fsdp")),
        P(("dp", "fsdp")),
        P(("dp", "fsdp")),
        P(("dp", "fsdp")),
        P(("dp", "fsdp")),
        P(("dp", "fsdp"), None),
        P(("dp", "fsdp")),
        P(None, ("dp", "fsdp")),
        P(None, ("dp", "fsdp")),
        P(("dp", "fsdp"), None),
    )
    return jax.shard_map(shards, mesh=mesh, in_specs=in_specs, out_specs=out_specs, check_vma=False)
```
